128 devices in a mesh: row: 8 (over x_lo, y), col: 16 (over z, x_hi, core).
Axes of the slice: x: 4 (x_hi: 2, x_lo: 2; x = x_hi * 2 + x_lo), y: 4, z: 4, core: 2. Of those that a mesh axis runs over, the one named last changes fastest.
Arguments:
- tracer_adj_next: float32 [8, 1024, 8192], P(None, 'row', 'col'), may hold values from -6 to 6
- tracer: float32 [8, 1024, 8192], P(None, 'row', 'col'), may hold values from -6 to 6
- u_east: float32 [1024, 8192], P('row', 'col'), may hold values from -6 to 6
- v_north: float32 [1024, 8192], P('row', 'col'), may hold values from -6 to 6
- surf_adj_next: float32 [1024, 8192], P('row', 'col'), may hold values from -6 to 6
- diag: float32 [1024, 8192], P('row', 'col'), may hold values from 0.1 to 1
- land: int32 [1024, 8192], P('row', 'col'), may hold values 0 or 1
- bottom: int32 [1024, 8192], P('row', 'col'), may hold values from 1 to 8
Outputs:
- tracer_adj: float32 [8, 1024, 8192], P(None, 'row', 'col')
- surf_adj: float32 [1024, 8192], P('row', 'col')
The draws below stay inside these ranges and needn't reach their ends.
All inputs are finite; a program needn't handle non-finite values. No bound on the sum of `land` on one device may be relied on, other than what follows from the above.
Results may differ from the reference program's by a relative error of at most 0.0001.
Values sent between devices are 32-bit elements; how exact they have to be, the bound alone decides.
No kernel may reach another device: no remote copies, remote signals or barrier semaphores. Data moves between devices by JAX's collectives and lax.ppermute only.
A program may use at most 64 MiB of HBM per device.

```python
import math
import jax
import jax.numpy as jnp

LEV = 8
ITERS = 3
NX = 1024
NY = 8192


def plant(result, own_key, least, top_value):
    longest = result.shape.index(max(result.shape))
    spots = []
    for shift in (0, 1):
        where = [jax.random.randint(jax.random.fold_in(own_key, axis), (), 0, length) for axis, length in enumerate(result.shape)]
        where[longest] = (where[longest] + shift) % result.shape[longest]
        spots.append(tuple(where))
    return result.at[spots[0]].set(least).at[spots[1]].set(top_value)


def steps_of(stream_key, shape, shards, least, top_value):
    def one(axis_at, blocks):
        draws = jax.random.uniform(jax.random.fold_in(jax.random.fold_in(stream_key, 6), axis_at), (blocks,), jnp.float32, least / len(shards), top_value / len(shards))
        return jnp.repeat(jnp.exp(draws), shape[axis_at] // blocks).reshape((-1,) + (1,) * (len(shape) - axis_at - 1))

    level = one(*shards[0])
    for cut in shards[1:]:
        level = level * one(*cut)
    return level


def noise(rng, shape, scale, most, cuts=(), kind=jnp.bfloat16):
    array = scale * jax.random.normal(rng, shape, jnp.float32)
    if cuts:
        array = array * steps_of(rng, shape, cuts, -0.22, 0.18)
    return jnp.clip(array, -most, most).astype(kind)


def setup_inputs(seed: int = 0) -> dict:
    key_list = jax.random.split(jax.random.key(seed), 9)
    return {
        "tracer_adj_next": noise(key_list[0], (LEV, NX, NY), 1.0, 6.0, ((1, 8), (2, 16)), jnp.float32),
        "tracer": noise(key_list[1], (LEV, NX, NY), 1.0, 6.0, ((1, 8), (2, 16)), jnp.float32),
        "u_east": noise(key_list[2], (NX, NY), 1.0, 6.0, ((0, 8), (1, 16)), jnp.float32),
        "v_north": noise(key_list[3], (NX, NY), 1.0, 6.0, ((0, 8), (1, 16)), jnp.float32),
        "surf_adj_next": noise(key_list[4], (NX, NY), 1.0, 6.0, ((0, 8), (1, 16)), jnp.float32),
        "diag": jnp.clip(jnp.exp(math.log(1.0) - 2.3025851 * jax.random.uniform(key_list[5], (NX, NY), jnp.float32) ** steps_of(key_list[5], (NX, NY), ((0, 8), (1, 16)), -0.2, 0.2)), 0.1, 1.0),
        "land": plant((jax.random.randint(key_list[6], (NX, NY), 0, 8) < 7).astype(jnp.int32), jax.random.fold_in(key_list[6], 1), 0, 1),
        "bottom": plant(jax.random.randint(key_list[7], (NX, NY), 1, LEV + 1), jax.random.fold_in(key_list[7], 1), 1, LEV).astype(jnp.int32),
    }


def next_col(a):
    widths = [(0, 0)] * (a.ndim - 1) + [(0, 1)]
    return jnp.pad(a[..., 1:], widths)


def prev_col(a):
    widths = [(0, 0)] * (a.ndim - 1) + [(1, 0)]
    return jnp.pad(a[..., :-1], widths)


def next_row(a):
    widths = [(0, 0)] * (a.ndim - 2) + [(0, 1), (0, 0)]
    return jnp.pad(a[..., 1:, :], widths)


def prev_row(a):
    widths = [(0, 0)] * (a.ndim - 2) + [(1, 0), (0, 0)]
    return jnp.pad(a[..., :-1, :], widths)


def operate(field, cu, cv, diag):
    center = diag + cu + prev_col(cu) + cv + prev_row(cv)
    return center * field - cu * next_col(field) - prev_col(cu) * prev_col(field) - cv * next_row(field) - prev_row(cv) * prev_row(field)


def reference(tracer_adj_next, tracer, u_east, v_north, surf_adj_next, diag, land, bottom):
    levels = jnp.arange(LEV, dtype=jnp.int32)[:, None, None]
    wet = jnp.where((land[None] == 1) & (levels < bottom[None]), 1.0, 0.0).astype(jnp.float32)
    open_u = wet * next_col(wet)
    open_v = wet * next_row(wet)
    g = tracer_adj_next
    flux_u = 0.25 * (next_col(g) - g)
    flux_v = 0.25 * (next_row(g) - g)
    push_u = open_u * u_east[None] * flux_u * 0.5
    push_v = open_v * v_north[None] * flux_v * 0.5
    tracer_adj = g + push_u + prev_col(push_u) + push_v + prev_row(push_v)
    ubar = jnp.sum(open_u * flux_u * (tracer + next_col(tracer)) * 0.5, axis=0)
    vbar = jnp.sum(open_v * flux_v * (tracer + next_row(tracer)) * 0.5, axis=0)
    rhs = surf_adj_next + 0.5 * ((ubar - prev_col(ubar)) + (vbar - prev_row(vbar)))
    ocean = jnp.where(land == 1, 1.0, 0.0).astype(jnp.float32)
    depth = bottom.astype(jnp.float32) / LEV
    cu = ocean * next_col(ocean) * jnp.minimum(depth, next_col(depth))
    cv = ocean * next_row(ocean) * jnp.minimum(depth, next_row(depth))
    solution = jnp.zeros_like(rhs)
    residual, direction = rhs, rhs
    rr = jnp.sum(residual * residual)
    for step in range(ITERS):
        image = operate(direction, cu, cv, diag)
        alpha = rr / jnp.sum(direction * image)
        solution = solution + alpha * direction
        residual = residual - alpha * image
        fresh = jnp.sum(residual * residual)
        direction = residual + (fresh / rr) * direction
        rr = fresh
    return tracer_adj, solution
```

```python
import jax
import jax.numpy as jnp
from jax import lax
from jax.experimental import pallas as pl
from jax.experimental.pallas import tpu as pltpu
from jax.sharding import PartitionSpec as P

LEV = 8
DEEP = 4
SHIFT = 1.0
F32 = jnp.float32
VMEM = pl.BlockSpec(memory_space=pltpu.VMEM)
PARAMS = pltpu.CompilerParams(vmem_limit_bytes=48 * 1024 * 1024)


def code_of(land, bottom):
    return jnp.where(land == 1, bottom, 0).astype(F32)


def swap_pairs(axis, first):
    count = lax.axis_size(axis)
    pairs = []
    for low in range(first, count - 1, 2):
        pairs += [(low, low + 1), (low + 1, low)]
    return pairs


def swap(buffers, axis):
    return [lax.ppermute(b, axis, swap_pairs(axis, first)) for first, b in enumerate(buffers)]


def is_even(axis):
    return lax.rem(lax.axis_index(axis), 2) == 0


def iota(shape, dim):
    return lax.broadcasted_iota(jnp.int32, shape, dim)


def planes_of(g, c, land, bottom, surf, diag, speed):
    return (
        [g[k] for k in range(LEV)]
        + [c[k] for k in range(LEV)]
        + [code_of(land[...], bottom[...]), surf[...], diag[...], speed[...]]
    )


def pack_rows(g0, g1, c0, c1, l0, l1, b0, b1, s0, s1, d0, d1, v0, v1, a_ref, b_ref):
    first = planes_of(g0, c0, l0, b0, s0, d0, v0)
    last = planes_of(g1, c1, l1, b1, s1, d1, v1)
    upper = iota(first[0].shape, 0) < 4
    even = is_even("row")
    for t in range(len(first) // 2):
        high = jnp.where(upper, pltpu.roll(last[2 * t], 4, 0), last[2 * t + 1])
        low = jnp.where(upper, first[2 * t], pltpu.roll(first[2 * t + 1], 4, 0))
        a_ref[8 * t : 8 * t + 8, :] = jnp.where(even, high, low)
        b_ref[8 * t : 8 * t + 8, :] = jnp.where(even, low, high)


def row_halo(near, far, lanes):
    even = is_even("row")

    def plane(p):
        t = p // 2
        one, two = near[8 * t : 8 * t + 8, lanes], far[8 * t : 8 * t + 8, lanes]
        north, south = jnp.where(even, one, two), jnp.where(even, two, one)
        upper = iota(north.shape, 0) < 4
        if p % 2 == 0:
            return jnp.where(upper, north, pltpu.roll(south, 4, 0))
        return jnp.where(upper, pltpu.roll(north, 4, 0), south)

    return plane


def lane_pack(planes, of_last):
    lane = iota(planes[0].shape, 1)
    out = jnp.zeros_like(planes[0])
    for p, x in enumerate(planes):
        turn = (DEEP * p + (DEEP if of_last else 0)) % 128
        moved = pltpu.roll(x, turn, 1) if turn else x
        out = jnp.where(lane // DEEP == p, moved, out)
    return out


def pack_cols(g0, g1, c0, c1, l0, l1, b0, b1, s0, s1, d0, d1, u0, u1, a_ref, b_ref):
    low = lane_pack(planes_of(g0, c0, l0, b0, s0, d0, u0), False)
    high = lane_pack(planes_of(g1, c1, l1, b1, s1, d1, u1), True)
    even = is_even("col")
    a_ref[...] = jnp.where(even, high, low)
    b_ref[...] = jnp.where(even, low, high)


def join_cols(a_in, b_in, near, far, a_ref, b_ref):
    rows, width = a_in.shape[0], near.shape[1]
    first = row_halo(near, far, slice(0, 128))
    last = row_halo(near, far, slice(width - 128, width))
    low = lane_pack([first(p) for p in range(2 * LEV + 3)], False)
    high = lane_pack([last(p) for p in range(2 * LEV + 3)], True)
    even = is_even("col")
    a_ref[:rows, :] = a_in[...]
    b_ref[:rows, :] = b_in[...]
    a_ref[rows:, :] = jnp.where(even, high, low)
    b_ref[rows:, :] = jnp.where(even, low, high)


def col_halo(near, far):
    even = is_even("col")
    one, two = near[...], far[...]
    east, west = jnp.where(even, one, two), jnp.where(even, two, one)
    left = iota(east.shape, 1) < 64

    def plane(p):
        e = pltpu.roll(east, (128 - DEEP * p) % 128, 1) if p else east
        w = pltpu.roll(west, 128 - DEEP - DEEP * p, 1)
        return jnp.where(left, e, w)

    return plane


def next_col(a):
    return pltpu.roll(a, a.shape[1] - 1, 1)


def prev_col(a):
    return pltpu.roll(a, 1, 1)


def next_row(a):
    return pltpu.roll(a, a.shape[0] - 1, 0)


def prev_row(a):
    return pltpu.roll(a, 1, 0)


def extended(own, rows, cols):
    return jnp.concatenate([jnp.concatenate([own, rows], axis=0), cols], axis=1)


def faces(code):
    return jnp.minimum(code, next_col(code)), jnp.minimum(code, next_row(code))


def krylov(g, c, land, bottom, surf, diag, rn, rf, cn, cf, r_ref, p1_ref, p2_ref, mom_ref):
    rows, cols = surf.shape
    rh, ch = row_halo(rn, rf, slice(0, cols)), col_halo(cn, cf)

    def wide(own, p):
        return extended(own, rh(p), ch(p))

    cu, cv = faces(wide(code_of(land[...], bottom[...]), 2 * LEV))
    ub = jnp.zeros_like(cu)
    vb = jnp.zeros_like(cv)
    for k in range(LEV):
        gk, ck = wide(g[k], k), wide(c[k], LEV + k)
        ub = ub + jnp.where(cu > k + 0.5, next_col(gk) - gk, 0.0) * (next_col(ck) + ck)
        vb = vb + jnp.where(cv > k + 0.5, next_row(gk) - gk, 0.0) * (next_row(ck) + ck)
    r = wide(surf[...], 2 * LEV + 1) + 0.0625 * ((ub - prev_col(ub)) + (vb - prev_row(vb)))
    cu, cv = cu * 0.125, cv * 0.125
    dg = wide(diag[...], 2 * LEV + 2)

    def shifted(v):
        fu, fv = cu * (v - next_col(v)), cv * (v - next_row(v))
        return (dg - SHIFT) * v + ((fu - prev_col(fu)) + (fv - prev_row(fv)))

    p1 = shifted(r)
    p2 = shifted(p1)
    eu, ev = p2 - next_col(p2), p2 - next_row(p2)
    energy = dg * p2 * p2 + (cu * eu * eu + cv * ev * ev)
    r, p1, p2, energy = [a[:rows, :cols] for a in (r, p1, p2, energy)]
    r_ref[...] = r
    p1_ref[...] = p1
    p2_ref[...] = p2
    lane = iota((8, 128), 1)
    packed = jnp.zeros((8, 128), F32)
    for m, prod in enumerate((r * r, r * p1, p1 * p1, p1 * p2, p2 * p2, energy)):
        tiles = [
            prod[8 * i : 8 * i + 8, 128 * j : 128 * j + 128]
            for i in range(rows // 8)
            for j in range(cols // 128)
        ]
        while len(tiles) > 1:
            tiles = [sum(tiles[i : i + 2][1:], tiles[i]) for i in range(0, len(tiles), 2)]
        part = tiles[0]
        for by in (4, 2, 1):
            part = part + pltpu.roll(part, by, 0)
        for by in (64, 32, 16):
            part = part + pltpu.roll(part, by, 1)
        packed = jnp.where(lane // 16 == m, part, packed)
    for i in range(mom_ref.shape[0] // 8):
        mom_ref[8 * i : 8 * i + 8, :] = packed


def tracer_kernel(g, land, bottom, u, v, rn, rf, cn, cf, out_ref):
    rows, cols = u.shape
    rh, ch = row_halo(rn, rf, slice(0, cols)), col_halo(cn, cf)

    def wide(own, p):
        return extended(own, rh(p), ch(p))

    cu, cv = faces(wide(code_of(land[...], bottom[...]), 2 * LEV))
    uw = 0.125 * wide(u[...], 2 * LEV + 3)
    vw = 0.125 * wide(v[...], 2 * LEV + 3)
    for k in range(LEV):
        gk = wide(g[k], k)
        pu = jnp.where(cu > k + 0.5, next_col(gk) - gk, 0.0) * uw
        pv = jnp.where(cv > k + 0.5, next_row(gk) - gk, 0.0) * vw
        total = gk + pu + prev_col(pu) + pv + prev_row(pv)
        out_ref[k] = total[:rows, :cols]


def two_sum(a, b):
    s = a + b
    t = s - a
    return s, (a - (s - t)) + (b - t)


def quick(a, b):
    s = a + b
    return s, b - (s - a)


def split(a):
    t = a * 4097.0
    high = t - (t - a)
    return high, a - high


def add(x, y):
    s, e = two_sum(x[0], y[0])
    return quick(s, e + (x[1] + y[1]))


def neg(x):
    return -x[0], -x[1]


def mul(x, y):
    p = x[0] * y[0]
    (ah, al), (bh, bl) = split(x[0]), split(y[0])
    e = ((ah * bh - p) + ah * bl + al * bh) + al * bl
    return quick(p, e + (x[0] * y[1] + x[1] * y[0]))


def div(x, y):
    q = x[0] / y[0]
    rest = add(x, neg(mul((q, jnp.zeros_like(q)), y)))
    return quick(q, rest[0] / y[0])


def combine(mom, r, p1, p2, x_ref):
    zero = jnp.zeros((8, 128), F32)
    tiles = [(mom[8 * i : 8 * i + 8, :], zero) for i in range(mom.shape[0] // 8)]
    while len(tiles) > 1:
        tiles = [add(tiles[i], tiles[i + 1]) for i in range(0, len(tiles), 2)]
    total = tiles[0]
    for by in (4, 2, 1):
        total = add(total, tuple(pltpu.roll(a, by, 0) for a in total))
    lane = iota((8, 128), 1)
    sums = []
    for m in range(6):
        mine = tuple(jnp.where(lane // 16 == m, a, 0.0) for a in total)
        for by in (64, 32, 16, 8, 4, 2, 1):
            mine = add(mine, tuple(pltpu.roll(a, by, 1) for a in mine))
        sums.append(mine)
    m00, m01, m11, m12, m22, e22 = sums
    a00, a01, a02 = add(m01, m00), add(m11, m01), add(m12, m11)
    a11, a12, a22 = a02, add(m22, m12), e22
    l10 = div(a01, a00)
    l20 = div(a02, a00)
    w11 = add(a11, neg(mul(l10, a01)))
    w12 = add(a12, neg(mul(l10, a02)))
    ok1 = w11[0] > 1e-9 * a11[0]
    l21 = tuple(jnp.where(ok1, a, 0.0) for a in div(w12, w11))
    w22 = add(add(a22, neg(mul(l20, a02))), neg(mul(l21, w12)))
    ok2 = w22[0] > 1e-9 * a22[0]
    b0 = m00
    b1 = add(m01, neg(mul(l10, b0)))
    z1 = tuple(jnp.where(ok1, a, 0.0) for a in div(b1, w11))
    b2 = add(add(m11, neg(mul(l20, b0))), neg(mul(l21, b1)))
    z2 = tuple(jnp.where(ok2, a, 0.0) for a in div(b2, w22))
    y2 = z2
    y1 = add(z1, neg(mul(l21, y2)))
    y0 = add(div(b0, a00), neg(add(mul(l10, y1), mul(l20, y2))))
    rows, cols = r.shape
    shape = (rows // 8, 8, cols // 128, 128)
    for i in range(rows // 8):
        for j in range(cols // 128):
            at = (slice(8 * i, 8 * i + 8), slice(128 * j, 128 * j + 128))
            x_ref[at] = y0[0] * r[at] + (y1[0] * p1[at] + y2[0] * p2[at])


def shards(tracer_adj_next, tracer, u_east, v_north, surf_adj_next, diag, land, bottom):
    levels, rows, cols = tracer.shape
    planes = 2 * levels + 4
    size = lax.axis_size("row") * lax.axis_size("col")
    twice = lambda *arrays: [a for a in arrays for _ in range(2)]

    def ends(shape3, shape2, dim):
        count = (rows // 8, cols // 128)[dim]
        specs = []
        for s in (shape3, shape3, shape2, shape2, shape2, shape2, shape2):
            for end in (0, count - 1):
                place = tuple(end if d == len(s) - 2 + dim else 0 for d in range(len(s)))
                specs.append(pl.BlockSpec(s, lambda i, place=place: place))
        return specs

    g, c = tracer_adj_next, tracer
    row_bufs = pl.pallas_call(
        pack_rows,
        grid=(1,),
        in_specs=ends((levels, 8, cols), (8, cols), 0),
        out_specs=[pl.BlockSpec((4 * planes, cols), lambda i: (0, 0))] * 2,
        out_shape=[jax.ShapeDtypeStruct((4 * planes, cols), F32)] * 2,
        compiler_params=PARAMS,
        name="pack_rows",
    )(*twice(g, c, land, bottom, surf_adj_next, diag, v_north))
    row_got = swap(row_bufs, "row")
    col_part = pl.pallas_call(
        pack_cols,
        grid=(1,),
        in_specs=ends((levels, rows, 128), (rows, 128), 1),
        out_specs=[pl.BlockSpec((rows, 128), lambda i: (0, 0))] * 2,
        out_shape=[jax.ShapeDtypeStruct((rows, 128), F32)] * 2,
        compiler_params=PARAMS,
        name="pack_cols",
    )(*twice(g, c, land, bottom, surf_adj_next, diag, u_east))
    col_bufs = pl.pallas_call(
        join_cols,
        in_specs=[VMEM] * 4,
        out_specs=[VMEM] * 2,
        out_shape=[jax.ShapeDtypeStruct((rows + 8, 128), F32)] * 2,
        compiler_params=PARAMS,
        name="join_cols",
    )(*col_part, *row_got)
    col_got = swap(col_bufs, "col")
    r, p1, p2, mom = pl.pallas_call(
        krylov,
        in_specs=[VMEM] * 10,
        out_specs=[VMEM] * 4,
        out_shape=[jax.ShapeDtypeStruct((rows, cols), F32)] * 3
        + [jax.ShapeDtypeStruct((size, 128), F32)],
        compiler_params=PARAMS,
        name="krylov",
    )(g, c, land, bottom, surf_adj_next, diag, *row_got, *col_got)
    mom = lax.all_to_all(mom, ("row", "col"), 0, 0, tiled=True)
    tracer_adj = pl.pallas_call(
        tracer_kernel,
        in_specs=[VMEM] * 9,
        out_specs=VMEM,
        out_shape=jax.ShapeDtypeStruct(g.shape, F32),
        compiler_params=PARAMS,
        cost_estimate=pl.CostEstimate(flops=20 * g.size, bytes_accessed=12 * g.size, transcendentals=0),
        name="tracer",
    )(g, land, bottom, u_east, v_north, *row_got, *col_got)
    surf_adj = pl.pallas_call(
        combine,
        in_specs=[VMEM] * 4,
        out_specs=VMEM,
        out_shape=jax.ShapeDtypeStruct((rows, cols), F32),
        compiler_params=PARAMS,
        name="combine",
    )(mom, r, p1, p2)
    return tracer_adj, surf_adj


def solution(mesh):
    three, two = P(None, "row", "col"), P("row", "col")
    return jax.shard_map(
        shards,
        mesh=mesh,
        in_specs=(three, three, two, two, two, two, two, two),
        out_specs=(three, two),
        check_vma=False,
    )
```

```python
import jax
import jax.numpy as jnp
from jax import lax
from jax.experimental import pallas as pl
from jax.experimental.pallas import tpu as pltpu
from jax.sharding import PartitionSpec as P

LEV = 8
DEEP = 4
SHIFT = 1.0
F32 = jnp.float32
VMEM = pl.BlockSpec(memory_space=pltpu.VMEM)
HBM = pl.BlockSpec(memory_space=pltpu.HBM)
PARAMS = pltpu.CompilerParams(vmem_limit_bytes=32 * 1024 * 1024)


CODE, SURF, DIAG, SPEED = 16, 17, 18, 19


def code_of(land, bottom):
    return jnp.where(land == 1, bottom, 0).astype(F32)


def swap_pairs(axis, first):
    count = lax.axis_size(axis)
    pairs = []
    for low in range(first, count - 1, 2):
        pairs += [(low, low + 1), (low + 1, low)]
    return pairs


def swap(buffers, axis):
    return [lax.ppermute(b, axis, swap_pairs(axis, first)) for first, b in enumerate(buffers)]


def is_even(axis):
    return lax.rem(lax.axis_index(axis), 2) == 0


def iota(shape, dim):
    return lax.broadcasted_iota(jnp.int32, shape, dim)


def turn(x, by, dim):
    by = by % x.shape[dim]
    return pltpu.roll(x, by, dim) if by else x


def next_col(a):
    return turn(a, -1, 1)


def prev_col(a):
    return turn(a, 1, 1)


def next_row(a):
    return turn(a, -1, 0)


def prev_row(a):
    return turn(a, 1, 0)


def pick(even, one, two):
    return jnp.where(even, one, two), jnp.where(even, two, one)


def start_all(copies):
    for copy in copies:
        copy.start()


def wait_all(copies):
    for copy in copies:
        copy.wait()


def pack_rows(g, c, land, bottom, surf, diag, v, a_ref, b_ref, g0, g1, c0, c1, l0, l1, b0, b1, s0, s1, d0, d1, v0, v1, sems):
    rows = surf.shape[0]
    copies = []
    for src, low, high in ((g, g0, g1), (c, c0, c1), (land, l0, l1), (bottom, b0, b1), (surf, s0, s1), (diag, d0, d1), (v, v0, v1)):
        for dst, at in ((low, slice(0, 8)), (high, slice(rows - 8, rows))):
            part = src.at[:, at, :] if len(src.shape) == 3 else src.at[at, :]
            copies.append(pltpu.make_async_copy(part, dst, sems.at[len(copies)]))
    start_all(copies)
    wait_all(copies)

    def planes(g, c, land, bottom, surf, diag, v):
        pairs = [x for k in range(LEV) for x in (g[k], c[k])]
        return pairs + [code_of(land[...], bottom[...]), surf[...], diag[...], v[...]]

    first = planes(g0, c0, l0, b0, s0, d0, v0)
    last = planes(g1, c1, l1, b1, s1, d1, v1)
    upper = iota(first[0].shape, 0) < DEEP
    even = is_even("row")
    for t in range(len(first) // 2):
        high = jnp.where(upper, turn(last[2 * t], DEEP, 0), last[2 * t + 1])
        low = jnp.where(upper, first[2 * t], turn(first[2 * t + 1], DEEP, 0))
        a_ref[8 * t : 8 * t + 8, :], b_ref[8 * t : 8 * t + 8, :] = pick(even, high, low)


def lane_pack(g, c, code, rest, of_last):
    group = iota(code.shape, 1) // DEEP
    base = DEEP if of_last else 0
    out = jnp.where(group == 16, turn(code, 64 + base, 1), 0.0)
    for by in (8, 16, 32):
        out = out + turn(out, by, 1)
    for k in range(LEV):
        out = jnp.where(group == 2 * k, turn(g[k], 8 * k + base, 1), out)
        out = jnp.where(group == 2 * k + 1, turn(c[k], 8 * k + 4 + base, 1), out)
    for n, x in enumerate(rest):
        out = jnp.where(group == 17 + 2 * n, turn(x, 68 + 8 * n + base, 1), out)
    return out


def local(g, c, land, bottom, surf, diag, u, s_ref, code_ref, diag_ref, a_ref, b_ref, gv, cv, lv, bv, sv, uv, sems, band_sems):
    rows, cols = surf.shape
    bands = band_sems.shape[0]
    tall = rows // bands
    flat = [
        pltpu.make_async_copy(src, dst, sems.at[n])
        for n, (src, dst) in enumerate(((land, lv), (bottom, bv), (surf, sv), (diag, diag_ref), (u, uv)))
    ]
    deep = []
    for b in range(bands):
        at = slice(b * tall, (b + 1) * tall)
        for n, (src, dst) in enumerate(((g, gv), (c, cv))):
            deep.append(pltpu.make_async_copy(src.at[:, at, :], dst.at[:, at, :], band_sems.at[b, n]))
    start_all(flat[:2] + deep[:2] + flat[2:] + deep[2:])
    wait_all(flat)
    code_ref[...] = code_of(lv[...], bv[...])
    even = is_even("col")
    lane, sub = iota((8, cols), 1), iota((8, cols), 0)
    vb_before = jnp.zeros((8, cols), F32)
    for i in range(rows // 8):
        at = slice(8 * i, 8 * i + 8)
        after = slice(8 * i + 8, 8 * i + 16)
        is_last = i == rows // 8 - 1
        if i == 0:
            wait_all(deep[:2])
        if (8 * i + 8) % tall == 0 and not is_last:
            b = (8 * i + 8) // tall
            wait_all(deep[2 * b : 2 * b + 2])

        def down(here, there):
            return turn(jnp.where(sub == 0, there, here), -1, 0)

        code = code_ref[at, :]
        cu = jnp.where(lane < cols - 1, jnp.minimum(code, next_col(code)), 0.0)
        if is_last:
            co = jnp.where(sub < 7, jnp.minimum(code, next_row(code)), 0.0)
        else:
            co = jnp.minimum(code, down(code, code_ref[after, :]))
        ub = jnp.zeros((8, cols), F32)
        vb = jnp.zeros((8, cols), F32)
        gs, cs = [], []
        for k in range(LEV):
            gk, ck = gv[k, at, :], cv[k, at, :]
            gs.append(gk)
            cs.append(ck)
            gn = next_row(gk) if is_last else down(gk, gv[k, after, :])
            cn = next_row(ck) if is_last else down(ck, cv[k, after, :])
            ub = ub + jnp.where(cu > k + 0.5, next_col(gk) - gk, 0.0) * (next_col(ck) + ck)
            vb = vb + jnp.where(co > k + 0.5, gn - gk, 0.0) * (cn + ck)
        vb_prev = turn(jnp.where(sub == 7, vb_before, vb), 1, 0)
        vb_before = vb
        s_ref[at, :] = sv[at, :] + 0.0625 * ((ub - prev_col(ub)) + (vb - vb_prev))
        rest = (sv[at, :], diag_ref[at, :], uv[at, :])
        packs = []
        for of_last, lanes in ((True, slice(cols - 128, cols)), (False, slice(0, 128))):
            cut = lambda xs: [x[:, lanes] for x in xs]
            packs.append(lane_pack(cut(gs), cut(cs), code[:, lanes], cut(rest), of_last))
        a_ref[at, :], b_ref[at, :] = pick(even, *packs)


def row_halo(near, far, lanes):
    even = is_even("row")

    def plane(p):
        at = slice(8 * (p // 2), 8 * (p // 2) + 8)
        north, south = pick(even, near[at, lanes], far[at, lanes])
        upper = iota(north.shape, 0) < DEEP
        if p % 2 == 0:
            return jnp.where(upper, north, turn(south, DEEP, 0))
        return jnp.where(upper, turn(north, DEEP, 0), south)

    return plane


def join_cols(a_in, b_in, near, far, a_ref, b_ref):
    rows, width = a_in.shape[0], near.shape[1]
    packs = []
    for of_last, lanes in ((True, slice(width - 128, width)), (False, slice(0, 128))):
        halo = row_halo(near, far, lanes)
        packs.append(
            lane_pack(
                [halo(2 * k) for k in range(LEV)],
                [halo(2 * k + 1) for k in range(LEV)],
                halo(CODE),
                [halo(SURF), halo(DIAG)],
                of_last,
            )
        )
    a_ref[:rows, :] = a_in[...]
    b_ref[:rows, :] = b_in[...]
    a_ref[rows:, :], b_ref[rows:, :] = pick(is_even("col"), *packs)


def halo_rows(s, code, diag, sent_a, sent_b, near, far, s_ref, code_ref, diag_ref):
    rows, cols = s.shape
    even = is_even("row")
    lane, sub = iota((8, cols), 1), iota((8, cols), 0)
    upper = sub < DEEP

    def strips(t):
        at = slice(8 * t, 8 * t + 8)
        high, low = pick(even, sent_a[at, :], sent_b[at, :])
        north, south = pick(even, near[at, :], far[at, :])
        one = [jnp.where(upper, x, turn(y, DEEP, 0)) for x, y in ((high, north), (south, low))]
        two = [jnp.where(upper, turn(x, DEEP, 0), y) for x, y in ((high, north), (south, low))]
        return one, two

    codes, surfs = strips(LEV)
    cus = [jnp.where(lane < cols - 1, jnp.minimum(x, next_col(x)), 0.0) for x in codes]
    cos = [jnp.where(sub < 7, jnp.minimum(x, next_row(x)), 0.0) for x in codes]
    ubs = [jnp.zeros((8, cols), F32)] * 2
    vbs = [jnp.zeros((8, cols), F32)] * 2
    for k in range(LEV):
        gs, cs = strips(k)
        for n in range(2):
            gk, ck = gs[n], cs[n]
            ubs[n] = ubs[n] + jnp.where(cus[n] > k + 0.5, next_col(gk) - gk, 0.0) * (next_col(ck) + ck)
            vbs[n] = vbs[n] + jnp.where(cos[n] > k + 0.5, next_row(gk) - gk, 0.0) * (next_row(ck) + ck)
    north, south = [
        surfs[n] + 0.0625 * ((ubs[n] - prev_col(ubs[n])) + (vbs[n] - prev_row(vbs[n]))) for n in range(2)
    ]
    s_ref[:rows, :] = s[...]
    code_ref[:rows, :] = code[...]
    diag_ref[:rows, :] = diag[...]
    s_ref[rows - 8 : rows, :] = s[rows - 8 :, :] + jnp.where(sub == 7, turn(0.0625 * vbs[0], 4, 0), 0.0)
    s_ref[:8, :] = s[:8, :] - jnp.where(sub == 0, turn(0.0625 * vbs[1], -3, 0), 0.0)
    s_ref[rows:, :] = turn(jnp.where(upper, south, north), DEEP, 0)
    halo = row_halo(near, far, slice(0, cols))
    code_ref[rows:, :] = halo(CODE)
    diag_ref[rows:, :] = halo(DIAG)


def col_halo(near, far):
    east, west = pick(is_even("col"), near[...], far[...])
    left = iota(east.shape, 1) < 64

    def plane(at):
        return jnp.where(left, turn(east, -at, 1), turn(west, 124 - at, 1))

    return plane


def krylov(s, code, diag, sent_a, sent_b, near, far, r_ref, p1_ref, p2_ref, mom_ref, r_v, p1_v, p2_v, sems):
    rows, cols = r_v.shape
    even = is_even("col")
    high, low = pick(even, sent_a[...], sent_b[...])
    east, west = pick(even, near[...], far[...])
    lane = iota(high.shape, 1)
    own, left = lane % 8 < DEEP, lane < 64

    def strip(one, two):
        return jnp.where(left, one, turn(two, 64, 1))

    gs = strip(*[jnp.where(own, x, turn(y, 4, 1)) for x, y in ((high, east), (west, low))])
    cs = strip(*[jnp.where(own, turn(x, -4, 1), y) for x, y in ((high, east), (west, low))])
    ks = strip(*[jnp.where(own, turn(x, -64, 1), turn(y, -60, 1)) for x, y in ((high, east), (west, low))])
    level = ((lane % 64) // 8).astype(F32) + 0.5
    open_u = (jnp.minimum(ks, next_col(ks)) > level) & (lane % 8 < 7)
    open_v = jnp.minimum(ks, next_row(ks)) > level
    ub = jnp.where(open_u, next_col(gs) - gs, 0.0) * (next_col(cs) + cs)
    vb = jnp.where(open_v, next_row(gs) - gs, 0.0) * (next_row(cs) + cs)
    for by in (8, 16, 32):
        ub = ub + turn(ub, -by, 1)
        vb = vb + turn(vb, -by, 1)
    ub, vb = 0.0625 * ub, 0.0625 * vb
    terms = (ub - prev_col(ub)) + (vb - prev_row(vb))
    halo = col_halo(near, far)
    r_side = jnp.where(left, turn(terms, -4, 1), turn(terms, 60, 1)) + halo(68)
    r = jnp.concatenate(
        [
            s[:, :128] - jnp.where(lane == 0, turn(ub, -67, 1), 0.0),
            s[:, 128 : cols - 128],
            s[:, cols - 128 :] + jnp.where(lane == 127, turn(ub, 124, 1), 0.0),
            r_side,
        ],
        axis=1,
    )
    code = 0.125 * jnp.concatenate([code[...], halo(64)], axis=1)
    dg = jnp.concatenate([diag[...], halo(76)], axis=1)
    cu, cv = jnp.minimum(code, next_col(code)), jnp.minimum(code, next_row(code))

    def shifted(v):
        fu, fv = cu * (v - next_col(v)), cv * (v - next_row(v))
        return (dg - SHIFT) * v + ((fu - prev_col(fu)) + (fv - prev_row(fv)))

    copies = []

    def send(x, own, out):
        own[...] = x[:rows, :cols]
        copies.append(pltpu.make_async_copy(own, out, sems.at[len(copies)]))
        copies[-1].start()

    send(r, r_v, r_ref)
    p1 = shifted(r)
    send(p1, p1_v, p1_ref)
    p2 = shifted(p1)
    send(p2, p2_v, p2_ref)
    eu, ev = p2 - next_col(p2), p2 - next_row(p2)
    energy = dg * p2 * p2 + (cu * eu * eu + cv * ev * ev)
    r, p1, p2, energy = [a[:rows, :cols] for a in (r, p1, p2, energy)]
    lane = iota((8, 128), 1)
    packed = jnp.zeros((8, 128), F32)
    for m, prod in enumerate((r * r, r * p1, p1 * p1, p1 * p2, p2 * p2, energy)):
        tiles = [
            prod[8 * i : 8 * i + 8, 128 * j : 128 * j + 128]
            for i in range(rows // 8)
            for j in range(cols // 128)
        ]
        while len(tiles) > 1:
            tiles = [sum(tiles[i : i + 2][1:], tiles[i]) for i in range(0, len(tiles), 2)]
        part = tiles[0]
        for by in (4, 2, 1):
            part = part + pltpu.roll(part, by, 0)
        for by in (64, 32, 16):
            part = part + pltpu.roll(part, by, 1)
        packed = jnp.where(lane // 16 == m, part, packed)
    for i in range(mom_ref.shape[0] // 8):
        mom_ref[8 * i : 8 * i + 8, :] = packed
    wait_all(copies)


def tracer_kernel(g, land, bottom, u, v, rn, rf, cn, cf, out_ref):
    rows, cols = u.shape
    rh, ch = row_halo(rn, rf, slice(0, cols)), col_halo(cn, cf)

    def wide(own, p, lane):
        return jnp.concatenate([jnp.concatenate([own, rh(p)], axis=0), ch(lane)], axis=1)

    code = wide(code_of(land[...], bottom[...]), CODE, 64)
    cu, cv = jnp.minimum(code, next_col(code)), jnp.minimum(code, next_row(code))
    uw = 0.125 * wide(u[...], SPEED, 84)
    vw = 0.125 * wide(v[...], SPEED, 84)
    for k in range(LEV):
        gk = wide(g[k], 2 * k, 8 * k)
        pu = jnp.where(cu > k + 0.5, next_col(gk) - gk, 0.0) * uw
        pv = jnp.where(cv > k + 0.5, next_row(gk) - gk, 0.0) * vw
        total = gk + pu + prev_col(pu) + pv + prev_row(pv)
        out_ref[k] = total[:rows, :cols]


def two_sum(a, b):
    s = a + b
    t = s - a
    return s, (a - (s - t)) + (b - t)


def quick(a, b):
    s = a + b
    return s, b - (s - a)


def split(a):
    t = a * 4097.0
    high = t - (t - a)
    return high, a - high


def add(x, y):
    s, e = two_sum(x[0], y[0])
    return quick(s, e + (x[1] + y[1]))


def neg(x):
    return -x[0], -x[1]


def mul(x, y):
    p = x[0] * y[0]
    (ah, al), (bh, bl) = split(x[0]), split(y[0])
    e = ((ah * bh - p) + ah * bl + al * bh) + al * bl
    return quick(p, e + (x[0] * y[1] + x[1] * y[0]))


def div(x, y):
    q = x[0] / y[0]
    rest = add(x, neg(mul((q, jnp.zeros_like(q)), y)))
    return quick(q, rest[0] / y[0])


def combine(mom_in, r_in, p1_in, p2_in, x_ref, mom, r, p1, p2, sems):
    copies = [
        pltpu.make_async_copy(src, dst, sems.at[n])
        for n, (src, dst) in enumerate(((mom_in, mom), (r_in, r), (p1_in, p1), (p2_in, p2)))
    ]
    start_all(copies)
    copies[0].wait()
    zero = jnp.zeros((8, 128), F32)
    tiles = [(mom[8 * i : 8 * i + 8, :], zero) for i in range(mom.shape[0] // 8)]
    while len(tiles) > 1:
        tiles = [add(tiles[i], tiles[i + 1]) for i in range(0, len(tiles), 2)]
    total = tiles[0]
    for by in (4, 2, 1):
        total = add(total, tuple(pltpu.roll(a, by, 0) for a in total))
    lane = iota((8, 128), 1)
    sums = []
    for m in range(6):
        mine = tuple(jnp.where(lane // 16 == m, a, 0.0) for a in total)
        for by in (64, 32, 16, 8, 4, 2, 1):
            mine = add(mine, tuple(pltpu.roll(a, by, 1) for a in mine))
        sums.append(mine)
    m00, m01, m11, m12, m22, e22 = sums
    a00, a01, a02 = add(m01, m00), add(m11, m01), add(m12, m11)
    a11, a12, a22 = a02, add(m22, m12), e22
    l10 = div(a01, a00)
    l20 = div(a02, a00)
    w11 = add(a11, neg(mul(l10, a01)))
    w12 = add(a12, neg(mul(l10, a02)))
    ok1 = w11[0] > 1e-9 * a11[0]
    l21 = tuple(jnp.where(ok1, a, 0.0) for a in div(w12, w11))
    w22 = add(add(a22, neg(mul(l20, a02))), neg(mul(l21, w12)))
    ok2 = w22[0] > 1e-9 * a22[0]
    b0 = m00
    b1 = add(m01, neg(mul(l10, b0)))
    z1 = tuple(jnp.where(ok1, a, 0.0) for a in div(b1, w11))
    b2 = add(add(m11, neg(mul(l20, b0))), neg(mul(l21, b1)))
    z2 = tuple(jnp.where(ok2, a, 0.0) for a in div(b2, w22))
    y2 = z2
    y1 = add(z1, neg(mul(l21, y2)))
    y0 = add(div(b0, a00), neg(add(mul(l10, y1), mul(l20, y2))))
    wait_all(copies[1:])
    rows, cols = r.shape
    for i in range(rows // 8):
        for j in range(cols // 128):
            at = (slice(8 * i, 8 * i + 8), slice(128 * j, 128 * j + 128))
            x_ref[at] = y0[0] * r[at] + (y1[0] * p1[at] + y2[0] * p2[at])


def call(kernel, ins, outs, scratch=(), name=None, cost=None):
    return pl.pallas_call(
        kernel,
        in_specs=list(ins),
        out_specs=[spec for spec, _ in outs],
        out_shape=[jax.ShapeDtypeStruct(shape, F32) for _, shape in outs],
        scratch_shapes=list(scratch),
        compiler_params=PARAMS,
        cost_estimate=cost,
        name=name,
    )


def shards(tracer_adj_next, tracer, u_east, v_north, surf_adj_next, diag, land, bottom):
    levels, rows, cols = tracer.shape
    planes = 2 * levels + 4
    size = lax.axis_size("row") * lax.axis_size("col")
    g, c = tracer_adj_next, tracer
    dma = pltpu.SemaphoreType.DMA
    two, wide, side = (rows, cols), (rows + 8, cols), (rows + 8, 128)
    whole = lambda kind=F32: pltpu.VMEM(two, kind)
    edges = [pltpu.VMEM((levels, 8, cols), F32)] * 4 + [pltpu.VMEM((8, cols), jnp.int32)] * 4 + [pltpu.VMEM((8, cols), F32)] * 6
    row_sent = call(
        pack_rows, [HBM] * 7, [(VMEM, (4 * planes, cols))] * 2, edges + [dma((14,))], name="pack_rows"
    )(g, c, land, bottom, surf_adj_next, diag, v_north)
    row_got = swap(row_sent, "row")
    deep = pltpu.VMEM(g.shape, F32)
    s, code, dg, a, b = call(
        local,
        [HBM] * 7,
        [(VMEM, two)] * 3 + [(VMEM, (rows, 128))] * 2,
        [deep, deep, whole(jnp.int32), whole(jnp.int32), whole(), whole(), dma((5,)), dma((4, 2))],
        name="local",
        cost=pl.CostEstimate(flops=24 * g.size, bytes_accessed=8 * g.size, transcendentals=0),
    )(g, c, land, bottom, surf_adj_next, diag, u_east)
    col_sent = call(join_cols, [VMEM] * 4, [(VMEM, side)] * 2, name="join_cols")(a, b, *row_got)
    col_got = swap(col_sent, "col")
    s, code, dg = call(halo_rows, [VMEM] * 7, [(VMEM, wide)] * 3, name="halo_rows")(
        s, code, dg, *row_sent, *row_got
    )
    r, p1, p2, mom = call(
        krylov,
        [VMEM] * 7,
        [(HBM, two)] * 3 + [(VMEM, (size, 128))],
        [whole(), whole(), whole(), dma((3,))],
        name="krylov",
    )(s, code, dg, *col_sent, *col_got)
    mom = lax.all_to_all(mom, ("row", "col"), 0, 0, tiled=True)
    (tracer_adj,) = call(
        tracer_kernel,
        [VMEM] * 9,
        [(VMEM, g.shape)],
        name="tracer",
        cost=pl.CostEstimate(flops=20 * g.size, bytes_accessed=12 * g.size, transcendentals=0),
    )(g, land, bottom, u_east, v_north, *row_got, *col_got)
    (surf_adj,) = call(
        combine,
        [HBM] * 4,
        [(VMEM, two)],
        [pltpu.VMEM((size, 128), F32), whole(), whole(), whole(), dma((4,))],
        name="combine",
    )(mom, r, p1, p2)
    return tracer_adj, surf_adj


def solution(mesh):
    three, two = P(None, "row", "col"), P("row", "col")
    return jax.shard_map(
        shards,
        mesh=mesh,
        in_specs=(three, three, two, two, two, two, two, two),
        out_specs=(three, two),
        check_vma=False,
    )
```

```python
import jax
import jax.numpy as jnp
from jax import lax
from jax.experimental import pallas as pl
from jax.experimental.pallas import tpu as pltpu
from jax.sharding import PartitionSpec as P

LEV = 8
DEEP = 4
SHIFT = 1.0
F32 = jnp.float32
VMEM = pl.BlockSpec(memory_space=pltpu.VMEM)
HBM = pl.BlockSpec(memory_space=pltpu.HBM)
PARAMS = pltpu.CompilerParams(vmem_limit_bytes=32 * 1024 * 1024)


CODE, SURF, DIAG, SPEED = 16, 17, 18, 19


def code_of(land, bottom):
    return jnp.where(land == 1, bottom, 0).astype(F32)


def swap_pairs(axis, first):
    count = lax.axis_size(axis)
    pairs = []
    for low in range(first, count - 1, 2):
        pairs += [(low, low + 1), (low + 1, low)]
    return pairs


def swap(buffers, axis):
    return [lax.ppermute(b, axis, swap_pairs(axis, first)) for first, b in enumerate(buffers)]


def is_even(axis):
    return lax.rem(lax.axis_index(axis), 2) == 0


def iota(shape, dim):
    return lax.broadcasted_iota(jnp.int32, shape, dim)


def turn(x, by, dim):
    by = by % x.shape[dim]
    return pltpu.roll(x, by, dim) if by else x


def next_col(a):
    return turn(a, -1, 1)


def prev_col(a):
    return turn(a, 1, 1)


def next_row(a):
    return turn(a, -1, 0)


def prev_row(a):
    return turn(a, 1, 0)


def pick(even, one, two):
    return jnp.where(even, one, two), jnp.where(even, two, one)


def start_all(copies):
    for copy in copies:
        copy.start()


def wait_all(copies):
    for copy in copies:
        copy.wait()


def pack_rows(g, c, land, bottom, surf, diag, v, a_ref, b_ref, g0, g1, c0, c1, l0, l1, b0, b1, s0, s1, d0, d1, v0, v1, sems):
    rows = surf.shape[0]
    copies = []
    for src, low, high in ((g, g0, g1), (c, c0, c1), (land, l0, l1), (bottom, b0, b1), (surf, s0, s1), (diag, d0, d1), (v, v0, v1)):
        for dst, at in ((low, slice(0, 8)), (high, slice(rows - 8, rows))):
            part = src.at[:, at, :] if len(src.shape) == 3 else src.at[at, :]
            copies.append(pltpu.make_async_copy(part, dst, sems.at[len(copies)]))
    start_all(copies)
    wait_all(copies)

    def planes(g, c, land, bottom, surf, diag, v):
        pairs = [x for k in range(LEV) for x in (g[k], c[k])]
        return pairs + [code_of(land[...], bottom[...]), surf[...], diag[...], v[...]]

    first = planes(g0, c0, l0, b0, s0, d0, v0)
    last = planes(g1, c1, l1, b1, s1, d1, v1)
    upper = iota(first[0].shape, 0) < DEEP
    even = is_even("row")
    for t in range(len(first) // 2):
        high = jnp.where(upper, turn(last[2 * t], DEEP, 0), last[2 * t + 1])
        low = jnp.where(upper, first[2 * t], turn(first[2 * t + 1], DEEP, 0))
        a_ref[8 * t : 8 * t + 8, :], b_ref[8 * t : 8 * t + 8, :] = pick(even, high, low)


def lane_pack(g, c, code, rest, of_last):
    group = iota(code.shape, 1) // DEEP
    base = DEEP if of_last else 0
    out = jnp.where(group == 16, turn(code, 64 + base, 1), 0.0)
    for by in (8, 16, 32):
        out = out + turn(out, by, 1)
    for k in range(LEV):
        out = jnp.where(group == 2 * k, turn(g[k], 8 * k + base, 1), out)
        out = jnp.where(group == 2 * k + 1, turn(c[k], 8 * k + 4 + base, 1), out)
    for n, x in enumerate(rest):
        out = jnp.where(group == 17 + 2 * n, turn(x, 68 + 8 * n + base, 1), out)
    return out


def local(g, c, land, bottom, surf, diag, u, s_ref, code_ref, diag_ref, a_ref, b_ref, gv, cv, lv, bv, sv, uv, sems, deep_sems):
    rows, cols = surf.shape
    flat = [
        pltpu.make_async_copy(src, dst, sems.at[n])
        for n, (src, dst) in enumerate(((land, lv), (bottom, bv), (surf, sv), (diag, diag_ref), (u, uv)))
    ]
    deep = [
        pltpu.make_async_copy(src.at[k], dst.at[k], deep_sems.at[k, n])
        for k in range(LEV)
        for n, (src, dst) in enumerate(((g, gv), (c, cv)))
    ]
    start_all(flat[:2] + deep + flat[2:])
    wait_all(flat[:2])
    code = code_of(lv[...], bv[...])
    code_ref[...] = code
    cu = jnp.where(iota(code.shape, 1) < cols - 1, jnp.minimum(code, next_col(code)), 0.0)
    co = jnp.where(iota(code.shape, 0) < rows - 1, jnp.minimum(code, next_row(code)), 0.0)
    ub, vb = jnp.zeros_like(cu), jnp.zeros_like(co)
    for k in range(LEV):
        wait_all(deep[2 * k : 2 * k + 2])
        gk, ck = gv[k], cv[k]
        ub = ub + jnp.where(cu > k + 0.5, next_col(gk) - gk, 0.0) * (next_col(ck) + ck)
        vb = vb + jnp.where(co > k + 0.5, next_row(gk) - gk, 0.0) * (next_row(ck) + ck)
    wait_all(flat[2:])
    s_ref[...] = sv[...] + 0.0625 * ((ub - prev_col(ub)) + (vb - prev_row(vb)))
    packs = [
        lane_pack(
            [gv[k, :, lanes] for k in range(LEV)],
            [cv[k, :, lanes] for k in range(LEV)],
            code_ref[:, lanes],
            [x[:, lanes] for x in (sv, diag_ref, uv)],
            of_last,
        )
        for of_last, lanes in ((True, slice(cols - 128, cols)), (False, slice(0, 128)))
    ]
    a_ref[...], b_ref[...] = pick(is_even("col"), *packs)


def row_halo(near, far, lanes):
    even = is_even("row")

    def plane(p):
        at = slice(8 * (p // 2), 8 * (p // 2) + 8)
        north, south = pick(even, near[at, lanes], far[at, lanes])
        upper = iota(north.shape, 0) < DEEP
        if p % 2 == 0:
            return jnp.where(upper, north, turn(south, DEEP, 0))
        return jnp.where(upper, turn(north, DEEP, 0), south)

    return plane


def join_cols(a_in, b_in, near, far, a_ref, b_ref):
    rows, width = a_in.shape[0], near.shape[1]
    packs = []
    for of_last, lanes in ((True, slice(width - 128, width)), (False, slice(0, 128))):
        halo = row_halo(near, far, lanes)
        packs.append(
            lane_pack(
                [halo(2 * k) for k in range(LEV)],
                [halo(2 * k + 1) for k in range(LEV)],
                halo(CODE),
                [halo(SURF), halo(DIAG)],
                of_last,
            )
        )
    a_ref[:rows, :] = a_in[...]
    b_ref[:rows, :] = b_in[...]
    a_ref[rows:, :], b_ref[rows:, :] = pick(is_even("col"), *packs)


def halo_rows(s, code, diag, sent_a, sent_b, near, far, s_ref, code_ref, diag_ref):
    rows, cols = s.shape
    even = is_even("row")
    lane, sub = iota((8, cols), 1), iota((8, cols), 0)
    upper = sub < DEEP

    def strips(t):
        at = slice(8 * t, 8 * t + 8)
        high, low = pick(even, sent_a[at, :], sent_b[at, :])
        north, south = pick(even, near[at, :], far[at, :])
        one = [jnp.where(upper, x, turn(y, DEEP, 0)) for x, y in ((high, north), (south, low))]
        two = [jnp.where(upper, turn(x, DEEP, 0), y) for x, y in ((high, north), (south, low))]
        return one, two

    codes, surfs = strips(LEV)
    cus = [jnp.where(lane < cols - 1, jnp.minimum(x, next_col(x)), 0.0) for x in codes]
    cos = [jnp.where(sub < 7, jnp.minimum(x, next_row(x)), 0.0) for x in codes]
    ubs = [jnp.zeros((8, cols), F32)] * 2
    vbs = [jnp.zeros((8, cols), F32)] * 2
    for k in range(LEV):
        gs, cs = strips(k)
        for n in range(2):
            gk, ck = gs[n], cs[n]
            ubs[n] = ubs[n] + jnp.where(cus[n] > k + 0.5, next_col(gk) - gk, 0.0) * (next_col(ck) + ck)
            vbs[n] = vbs[n] + jnp.where(cos[n] > k + 0.5, next_row(gk) - gk, 0.0) * (next_row(ck) + ck)
    north, south = [
        surfs[n] + 0.0625 * ((ubs[n] - prev_col(ubs[n])) + (vbs[n] - prev_row(vbs[n]))) for n in range(2)
    ]
    s_ref[:rows, :] = s[...]
    code_ref[:rows, :] = code[...]
    diag_ref[:rows, :] = diag[...]
    s_ref[rows - 8 : rows, :] = s[rows - 8 :, :] + jnp.where(sub == 7, turn(0.0625 * vbs[0], 4, 0), 0.0)
    s_ref[:8, :] = s[:8, :] - jnp.where(sub == 0, turn(0.0625 * vbs[1], -3, 0), 0.0)
    s_ref[rows:, :] = turn(jnp.where(upper, south, north), DEEP, 0)
    halo = row_halo(near, far, slice(0, cols))
    code_ref[rows:, :] = halo(CODE)
    diag_ref[rows:, :] = halo(DIAG)


def col_halo(near, far):
    east, west = pick(is_even("col"), near[...], far[...])
    left = iota(east.shape, 1) < 64

    def plane(at):
        return jnp.where(left, turn(east, -at, 1), turn(west, 124 - at, 1))

    return plane


def krylov(s, code, diag, sent_a, sent_b, near, far, r_ref, p1_ref, p2_ref, mom_ref):
    rows, cols = r_ref.shape
    even = is_even("col")
    high, low = pick(even, sent_a[...], sent_b[...])
    east, west = pick(even, near[...], far[...])
    lane = iota(high.shape, 1)
    own, left = lane % 8 < DEEP, lane < 64

    def strip(one, two):
        return jnp.where(left, one, turn(two, 64, 1))

    gs = strip(*[jnp.where(own, x, turn(y, 4, 1)) for x, y in ((high, east), (west, low))])
    cs = strip(*[jnp.where(own, turn(x, -4, 1), y) for x, y in ((high, east), (west, low))])
    ks = strip(*[jnp.where(own, turn(x, -64, 1), turn(y, -60, 1)) for x, y in ((high, east), (west, low))])
    level = ((lane % 64) // 8).astype(F32) + 0.5
    open_u = (jnp.minimum(ks, next_col(ks)) > level) & (lane % 8 < 7)
    open_v = jnp.minimum(ks, next_row(ks)) > level
    ub = jnp.where(open_u, next_col(gs) - gs, 0.0) * (next_col(cs) + cs)
    vb = jnp.where(open_v, next_row(gs) - gs, 0.0) * (next_row(cs) + cs)
    for by in (8, 16, 32):
        ub = ub + turn(ub, -by, 1)
        vb = vb + turn(vb, -by, 1)
    ub, vb = 0.0625 * ub, 0.0625 * vb
    terms = (ub - prev_col(ub)) + (vb - prev_row(vb))
    halo = col_halo(near, far)
    r_side = jnp.where(left, turn(terms, -4, 1), turn(terms, 60, 1)) + halo(68)
    r = jnp.concatenate(
        [
            s[:, :128] - jnp.where(lane == 0, turn(ub, -67, 1), 0.0),
            s[:, 128 : cols - 128],
            s[:, cols - 128 :] + jnp.where(lane == 127, turn(ub, 124, 1), 0.0),
            r_side,
        ],
        axis=1,
    )
    code = 0.125 * jnp.concatenate([code[...], halo(64)], axis=1)
    dg = jnp.concatenate([diag[...], halo(76)], axis=1)
    cu, cv = jnp.minimum(code, next_col(code)), jnp.minimum(code, next_row(code))

    def shifted(v):
        fu, fv = cu * (v - next_col(v)), cv * (v - next_row(v))
        return (dg - SHIFT) * v + ((fu - prev_col(fu)) + (fv - prev_row(fv)))

    p1 = shifted(r)
    p2 = shifted(p1)
    eu, ev = p2 - next_col(p2), p2 - next_row(p2)
    energy = dg * p2 * p2 + (cu * eu * eu + cv * ev * ev)
    r, p1, p2, energy = [a[:rows, :cols] for a in (r, p1, p2, energy)]
    r_ref[...] = r
    p1_ref[...] = p1
    p2_ref[...] = p2
    lane = iota((8, 128), 1)
    packed = jnp.zeros((8, 128), F32)
    for m, prod in enumerate((r * r, r * p1, p1 * p1, p1 * p2, p2 * p2, energy)):
        tiles = [
            prod[8 * i : 8 * i + 8, 128 * j : 128 * j + 128]
            for i in range(rows // 8)
            for j in range(cols // 128)
        ]
        while len(tiles) > 1:
            tiles = [sum(tiles[i : i + 2][1:], tiles[i]) for i in range(0, len(tiles), 2)]
        part = tiles[0]
        for by in (4, 2, 1):
            part = part + pltpu.roll(part, by, 0)
        for by in (64, 32, 16):
            part = part + pltpu.roll(part, by, 1)
        packed = jnp.where(lane // 16 == m, part, packed)
    for i in range(mom_ref.shape[0] // 8):
        mom_ref[8 * i : 8 * i + 8, :] = packed


def tracer_kernel(g_in, land_in, bottom_in, u_in, v_in, rn, rf, cn, cf, out_ref, g, land, bottom, u, v, out, sems, g_sems, out_sems):
    flat = [
        pltpu.make_async_copy(src, dst, sems.at[n])
        for n, (src, dst) in enumerate(((land_in, land), (bottom_in, bottom), (u_in, u), (v_in, v)))
    ]
    deep = [pltpu.make_async_copy(g_in.at[k], g.at[k], g_sems.at[k]) for k in range(LEV)]
    done = [pltpu.make_async_copy(out.at[k], out_ref.at[k], out_sems.at[k]) for k in range(LEV)]
    start_all(flat + deep)
    wait_all(flat)
    rows, cols = u.shape
    rh, ch = row_halo(rn, rf, slice(0, cols)), col_halo(cn, cf)

    def wide(own, p, lane):
        return jnp.concatenate([jnp.concatenate([own, rh(p)], axis=0), ch(lane)], axis=1)

    code = wide(code_of(land[...], bottom[...]), CODE, 64)
    cu, cv = jnp.minimum(code, next_col(code)), jnp.minimum(code, next_row(code))
    uw = 0.125 * wide(u[...], SPEED, 84)
    vw = 0.125 * wide(v[...], SPEED, 84)
    for k in range(LEV):
        deep[k].wait()
        gk = wide(g[k], 2 * k, 8 * k)
        pu = jnp.where(cu > k + 0.5, next_col(gk) - gk, 0.0) * uw
        pv = jnp.where(cv > k + 0.5, next_row(gk) - gk, 0.0) * vw
        total = gk + pu + prev_col(pu) + pv + prev_row(pv)
        out[k] = total[:rows, :cols]
        done[k].start()
    wait_all(done)


def two_sum(a, b):
    s = a + b
    t = s - a
    return s, (a - (s - t)) + (b - t)


def quick(a, b):
    s = a + b
    return s, b - (s - a)


def split(a):
    t = a * 4097.0
    high = t - (t - a)
    return high, a - high


def add(x, y):
    s, e = two_sum(x[0], y[0])
    return quick(s, e + (x[1] + y[1]))


def neg(x):
    return -x[0], -x[1]


def mul(x, y):
    p = x[0] * y[0]
    (ah, al), (bh, bl) = split(x[0]), split(y[0])
    e = ((ah * bh - p) + ah * bl + al * bh) + al * bl
    return quick(p, e + (x[0] * y[1] + x[1] * y[0]))


def div(x, y):
    q = x[0] / y[0]
    rest = add(x, neg(mul((q, jnp.zeros_like(q)), y)))
    return quick(q, rest[0] / y[0])


def combine(mom_in, r, p1, p2, x_ref, mom, x, sems):
    load = pltpu.make_async_copy(mom_in, mom, sems.at[0])
    load.start()
    load.wait()
    zero = jnp.zeros((8, 128), F32)
    tiles = [(mom[8 * i : 8 * i + 8, :], zero) for i in range(mom.shape[0] // 8)]
    while len(tiles) > 1:
        tiles = [add(tiles[i], tiles[i + 1]) for i in range(0, len(tiles), 2)]
    total = tiles[0]
    for by in (4, 2, 1):
        total = add(total, tuple(pltpu.roll(a, by, 0) for a in total))
    lane = iota((8, 128), 1)
    sums = []
    for m in range(6):
        mine = tuple(jnp.where(lane // 16 == m, a, 0.0) for a in total)
        for by in (64, 32, 16, 8, 4, 2, 1):
            mine = add(mine, tuple(pltpu.roll(a, by, 1) for a in mine))
        sums.append(mine)
    m00, m01, m11, m12, m22, e22 = sums
    a00, a01, a02 = add(m01, m00), add(m11, m01), add(m12, m11)
    a11, a12, a22 = a02, add(m22, m12), e22
    l10 = div(a01, a00)
    l20 = div(a02, a00)
    w11 = add(a11, neg(mul(l10, a01)))
    w12 = add(a12, neg(mul(l10, a02)))
    ok1 = w11[0] > 1e-9 * a11[0]
    l21 = tuple(jnp.where(ok1, a, 0.0) for a in div(w12, w11))
    w22 = add(add(a22, neg(mul(l20, a02))), neg(mul(l21, w12)))
    ok2 = w22[0] > 1e-9 * a22[0]
    b0 = m00
    b1 = add(m01, neg(mul(l10, b0)))
    z1 = tuple(jnp.where(ok1, a, 0.0) for a in div(b1, w11))
    b2 = add(add(m11, neg(mul(l20, b0))), neg(mul(l21, b1)))
    z2 = tuple(jnp.where(ok2, a, 0.0) for a in div(b2, w22))
    y2 = z2
    y1 = add(z1, neg(mul(l21, y2)))
    y0 = add(div(b0, a00), neg(add(mul(l10, y1), mul(l20, y2))))
    rows, cols = r.shape
    bands = sems.shape[0] - 1
    tall = rows // bands
    done = []
    for b in range(bands):
        band = slice(b * tall, (b + 1) * tall)
        for i in range(b * tall // 8, (b + 1) * tall // 8):
            for j in range(cols // 128):
                at = (slice(8 * i, 8 * i + 8), slice(128 * j, 128 * j + 128))
                x[at] = y0[0] * r[at] + (y1[0] * p1[at] + y2[0] * p2[at])
        done.append(pltpu.make_async_copy(x.at[band, :], x_ref.at[band, :], sems.at[1 + b]))
        done[-1].start()
    wait_all(done)


def call(kernel, ins, outs, scratch=(), name=None, cost=None):
    run = pl.pallas_call(
        kernel,
        in_specs=list(ins),
        out_specs=[spec for spec, _ in outs],
        out_shape=[spec.memory_space(shape, F32) for spec, shape in outs],
        scratch_shapes=list(scratch),
        compiler_params=PARAMS,
        cost_estimate=cost,
        name=name,
    )
    return lambda *args: run(*[pltpu.with_memory_space_constraint(x, spec.memory_space) for x, spec in zip(args, ins)])


def shards(tracer_adj_next, tracer, u_east, v_north, surf_adj_next, diag, land, bottom):
    levels, rows, cols = tracer.shape
    planes = 2 * levels + 4
    size = lax.axis_size("row") * lax.axis_size("col")
    g, c = tracer_adj_next, tracer
    dma = pltpu.SemaphoreType.DMA
    two, wide, side = (rows, cols), (rows + 8, cols), (rows + 8, 128)
    whole = lambda kind=F32: pltpu.VMEM(two, kind)
    edges = [pltpu.VMEM((levels, 8, cols), F32)] * 4 + [pltpu.VMEM((8, cols), jnp.int32)] * 4 + [pltpu.VMEM((8, cols), F32)] * 6
    row_sent = call(
        pack_rows, [HBM] * 7, [(VMEM, (4 * planes, cols))] * 2, edges + [dma((14,))], name="pack_rows"
    )(g, c, land, bottom, surf_adj_next, diag, v_north)
    row_got = swap(row_sent, "row")
    deep = pltpu.VMEM(g.shape, F32)
    s, code, dg, a, b = call(
        local,
        [HBM] * 7,
        [(VMEM, two)] * 3 + [(VMEM, (rows, 128))] * 2,
        [deep, deep, whole(jnp.int32), whole(jnp.int32), whole(), whole(), dma((5,)), dma((levels, 2))],
        name="local",
        cost=pl.CostEstimate(flops=24 * g.size, bytes_accessed=8 * g.size, transcendentals=0),
    )(g, c, land, bottom, surf_adj_next, diag, u_east)
    col_sent = call(join_cols, [VMEM] * 4, [(VMEM, side)] * 2, name="join_cols")(a, b, *row_got)
    col_got = swap(col_sent, "col")
    s, code, dg = call(halo_rows, [VMEM] * 7, [(VMEM, wide)] * 3, name="halo_rows")(
        s, code, dg, *row_sent, *row_got
    )
    r, p1, p2, mom = call(
        krylov,
        [VMEM] * 7,
        [(VMEM, two)] * 3 + [(VMEM, (size, 128))],
        name="krylov",
    )(s, code, dg, *col_sent, *col_got)
    mom = lax.all_to_all(mom, ("row", "col"), 0, 0, tiled=True)
    (tracer_adj,) = call(
        tracer_kernel,
        [HBM] * 5 + [VMEM] * 4,
        [(HBM, g.shape)],
        [deep, whole(jnp.int32), whole(jnp.int32), whole(), whole(), deep, dma((4,)), dma((levels,)), dma((levels,))],
        name="tracer",
        cost=pl.CostEstimate(flops=20 * g.size, bytes_accessed=12 * g.size, transcendentals=0),
    )(g, land, bottom, u_east, v_north, *row_got, *col_got)
    (surf_adj,) = call(
        combine,
        [HBM] + [VMEM] * 3,
        [(HBM, two)],
        [pltpu.VMEM((size, 128), F32), whole(), dma((5,))],
        name="combine",
    )(mom, r, p1, p2)
    return tracer_adj, surf_adj


def solution(mesh):
    three, two = P(None, "row", "col"), P("row", "col")
    return jax.shard_map(
        shards,
        mesh=mesh,
        in_specs=(three, three, two, two, two, two, two, two),
        out_specs=(three, two),
        check_vma=False,
    )
```

```python
import jax
import jax.numpy as jnp
from jax import lax
from jax.experimental import pallas as pl
from jax.experimental.pallas import tpu as pltpu
from jax.sharding import PartitionSpec as P

LEV = 8
DEEP = 4
SHIFT = 1.0
F32 = jnp.float32
VMEM = pl.BlockSpec(memory_space=pltpu.VMEM)
HBM = pl.BlockSpec(memory_space=pltpu.HBM)
PARAMS = pltpu.CompilerParams(vmem_limit_bytes=32 * 1024 * 1024)


G, C, RHS, CODE, DIAG = 0, 1, 4, 5, 6


def code_of(land, bottom):
    return jnp.where(land == 1, bottom, 0).astype(F32)


def swap_pairs(axis, first):
    count = lax.axis_size(axis)
    pairs = []
    for low in range(first, count - 1, 2):
        pairs += [(low, low + 1), (low + 1, low)]
    return pairs


def swap(buffers, axis):
    return [lax.ppermute(b, axis, swap_pairs(axis, first)) for first, b in enumerate(buffers)]


def is_even(axis):
    return lax.rem(lax.axis_index(axis), 2) == 0


def iota(shape, dim):
    return lax.broadcasted_iota(jnp.int32, shape, dim)


def turn(x, by, dim):
    by = by % x.shape[dim]
    return pltpu.roll(x, by, dim) if by else x


def next_col(a):
    return turn(a, -1, 1)


def prev_col(a):
    return turn(a, 1, 1)


def next_row(a):
    return turn(a, -1, 0)


def prev_row(a):
    return turn(a, 1, 0)


def pick(even, one, two):
    return jnp.where(even, one, two), jnp.where(even, two, one)


def start_all(copies):
    for copy in copies:
        copy.start()


def wait_all(copies):
    for copy in copies:
        copy.wait()


def pack_rows(g, c, land, bottom, surf, diag, v, a_ref, b_ref, g0, g1, c0, c1, l0, l1, b0, b1, s0, s1, d0, d1, v0, v1, sems):
    rows = surf.shape[0]
    copies = []
    for src, low, high in ((g, g0, g1), (c, c0, c1), (land, l0, l1), (bottom, b0, b1), (surf, s0, s1), (diag, d0, d1), (v, v0, v1)):
        for dst, at in ((low, slice(0, 8)), (high, slice(rows - 8, rows))):
            part = src.at[:, at, :] if len(src.shape) == 3 else src.at[at, :]
            copies.append(pltpu.make_async_copy(part, dst, sems.at[len(copies)]))
    start_all(copies)
    wait_all(copies)

    cols = surf.shape[1]
    lane, sub = iota((8, cols), 1), iota((8, cols), 0)
    upper = sub < DEEP

    def tiles(g, c, land, bottom, surf, diag, v, of_last):
        code = code_of(land[...], bottom[...])
        g, c = [g[k] for k in range(LEV)], [c[k] for k in range(LEV)]
        cu = jnp.where(lane < cols - 1, jnp.minimum(code, next_col(code)), 0.0)
        cv = jnp.where(sub < 7, jnp.minimum(code, next_row(code)), 0.0)
        ub, vb = faces(g, c, cu, cv)
        rhs = surf[...] + 0.0625 * ((ub - prev_col(ub)) + (vb - prev_row(vb)))
        edge = 7 if of_last else 0

        def outermost(x):
            out = turn(x[0], -edge, 0)
            for k in range(1, LEV):
                out = jnp.where(sub == k, turn(x[k], k - edge, 0), out)
            return out

        half = DEEP if of_last else 0
        one = jnp.where(upper, turn(rhs, half, 0), turn(code, DEEP - half, 0))
        two = jnp.where(upper, turn(diag[...], half, 0), turn(v[...], DEEP - edge, 0))
        ends = []
        for high, lanes in ((False, slice(0, 128)), (True, slice(cols - 128, cols))):
            cut = lambda xs: [x[:, lanes] for x in xs]
            corner = lane_pack(cut(g), cut(c), code[:, lanes], cut([surf, diag]), high)
            ends.append(jnp.where(sub[:, :128] < 5, two[:, lanes], corner if of_last else turn(corner, 5, 0)))
        two = jnp.concatenate([ends[0], two[:, 128 : cols - 128], ends[1]], axis=1)
        return outermost(g), outermost(c), one, two

    first = tiles(g0, c0, l0, b0, s0, d0, v0, False)
    last = tiles(g1, c1, l1, b1, s1, d1, v1, True)
    even = is_even("row")
    for t in range(4):
        a_ref[8 * t : 8 * t + 8, :], b_ref[8 * t : 8 * t + 8, :] = pick(even, last[t], first[t])


def faces(g, c, cu, cv):
    ub, vb = jnp.zeros_like(cu), jnp.zeros_like(cv)
    for k in range(LEV):
        gk, ck = g[k], c[k]
        ub = ub + jnp.where(cu > k + 0.5, next_col(gk) - gk, 0.0) * (next_col(ck) + ck)
        vb = vb + jnp.where(cv > k + 0.5, next_row(gk) - gk, 0.0) * (next_row(ck) + ck)
    return ub, vb


def lane_pack(g, c, code, rest, of_last):
    group = iota(code.shape, 1) // DEEP
    base = DEEP if of_last else 0
    out = jnp.where(group == 16, turn(code, 64 + base, 1), 0.0)
    for by in (8, 16, 32):
        out = out + turn(out, by, 1)
    for k in range(LEV):
        out = jnp.where(group == 2 * k, turn(g[k], 8 * k + base, 1), out)
        out = jnp.where(group == 2 * k + 1, turn(c[k], 8 * k + 4 + base, 1), out)
    for n, x in enumerate(rest):
        out = jnp.where(group == 17 + 2 * n, turn(x, 68 + 8 * n + base, 1), out)
    return out


def pack_cols(g, c, land, bottom, surf, diag, u, a_ref, b_ref, gv, cv, lv, bv, fv, sems):
    cols = surf.shape[1]
    copies = []
    for n, (src, dst) in enumerate(((land, lv), (bottom, bv), (surf, fv), (diag, fv), (u, fv), (g, gv), (c, cv))):
        for end, lanes in enumerate((slice(0, 128), slice(cols - 128, cols))):
            part = src.at[:, :, lanes] if len(src.shape) == 3 else src.at[:, lanes]
            there = dst.at[n - 2, end] if dst is fv else dst.at[end]
            copies.append(pltpu.make_async_copy(part, there, sems.at[n, end]))
    start_all(copies)
    wait_all(copies)
    low, high = [
        lane_pack(
            [gv[end, k] for k in range(LEV)],
            [cv[end, k] for k in range(LEV)],
            code_of(lv[end], bv[end]),
            [fv[n, end] for n in range(3)],
            end == 1,
        )
        for end in range(2)
    ]
    a_ref[...], b_ref[...] = pick(is_even("col"), high, low)


def row_halo(near, far, lanes):
    even = is_even("row")

    def plane(p):
        at = slice(8 * (p // 2), 8 * (p // 2) + 8)
        north, south = pick(even, near[at, lanes], far[at, lanes])
        upper = iota(north.shape, 0) < DEEP
        if p % 2 == 0:
            return jnp.where(upper, north, turn(south, DEEP, 0))
        return jnp.where(upper, turn(north, DEEP, 0), south)

    return plane


def join_cols(a_in, b_in, near, far, a_ref, b_ref):
    rows, width = a_in.shape[0], near.shape[1]
    even = is_even("row")
    packs = []
    for lanes in (slice(width - 128, width), slice(0, 128)):
        north, south = pick(even, near[24:, lanes], far[24:, lanes])
        sub = iota(north.shape, 0)
        packs.append(jnp.where(sub < 3, turn(north, -5, 0), jnp.where(sub < 5, 0.0, south)))
    a_ref[:rows, :] = a_in[...]
    b_ref[:rows, :] = b_in[...]
    a_ref[rows:, :], b_ref[rows:, :] = pick(is_even("col"), *packs)


def rhs_rows(g, c, land, bottom, surf, diag, sent_a, sent_b, near, far, s_ref, code_ref, diag_ref, gv, cv, lv, bv, sv, sems, deep_sems):
    rows, cols = surf.shape
    flat = [
        pltpu.make_async_copy(src, dst, sems.at[n])
        for n, (src, dst) in enumerate(((land, lv), (bottom, bv), (surf, sv), (diag, diag_ref.at[:rows, :])))
    ]
    deep = [
        pltpu.make_async_copy(src.at[k], dst.at[k], deep_sems.at[k, n])
        for k in range(LEV)
        for n, (src, dst) in enumerate(((g, gv), (c, cv)))
    ]
    start_all(flat[:2] + deep + flat[2:])
    even = is_even("row")
    lane, sub = iota((8, cols), 1), iota((8, cols), 0)
    upper = sub < DEEP

    high, low = pick(even, sent_a[...], sent_b[...])
    north, south = pick(even, near[...], far[...])

    def across(below, above, here, there):
        pair = [x[16 + at : 17 + at, :] for x, at in ((below, here), (above, there))]
        open_v = jnp.minimum(*pair) > sub.astype(F32) + 0.5
        total = jnp.where(open_v, above[:8] - below[:8], 0.0) * (above[8:16] + below[8:16])
        for by in (4, 2, 1):
            total = total + turn(total, by, 0)
        return 0.0625 * total

    up = across(high, north, 7, 4)
    down = across(south, low, 7, 4)
    halo = row_halo(near, far, slice(0, cols))
    s_ref[rows:, :] = halo(RHS) + jnp.where(sub == 0, -up, jnp.where(sub == 7, down, 0.0))
    code_ref[rows:, :] = halo(CODE)
    diag_ref[rows:, :] = halo(DIAG)
    wait_all(flat[:2])
    code = code_of(lv[...], bv[...])
    code_ref[:rows, :] = code
    cu = jnp.where(iota(code.shape, 1) < cols - 1, jnp.minimum(code, next_col(code)), 0.0)
    co = jnp.where(iota(code.shape, 0) < rows - 1, jnp.minimum(code, next_row(code)), 0.0)

    class Levels:
        def __init__(self, ref, n):
            self.ref, self.n = ref, n

        def __getitem__(self, k):
            deep[2 * k + self.n].wait()
            return self.ref[k]

    ub, vb = faces(Levels(gv, 0), Levels(cv, 1), cu, co)
    wait_all(flat[2:])
    s = sv[...] + 0.0625 * ((ub - prev_col(ub)) + (vb - prev_row(vb)))
    s_ref[:8, :] = s[:8, :] - jnp.where(sub == 0, down, 0.0)
    s_ref[8 : rows - 8, :] = s[8 : rows - 8, :]
    s_ref[rows - 8 : rows, :] = s[rows - 8 :, :] + jnp.where(sub == 7, up, 0.0)


def col_halo(near, far):
    east, west = pick(is_even("col"), near[...], far[...])
    left = iota(east.shape, 1) < 64

    def plane(at):
        return jnp.where(left, turn(east, -at, 1), turn(west, 124 - at, 1))

    return plane


def krylov(s, code, diag, sent_a, sent_b, near, far, r_ref, p1_ref, p2_ref, mom_ref):
    rows, cols = r_ref.shape
    even = is_even("col")
    high, low = pick(even, sent_a[...], sent_b[...])
    east, west = pick(even, near[...], far[...])
    lane = iota(high.shape, 1)
    own, left = lane % 8 < DEEP, lane < 64

    def strip(one, two):
        return jnp.where(left, one, turn(two, 64, 1))

    gs = strip(*[jnp.where(own, x, turn(y, 4, 1)) for x, y in ((high, east), (west, low))])
    cs = strip(*[jnp.where(own, turn(x, -4, 1), y) for x, y in ((high, east), (west, low))])
    ks = strip(*[jnp.where(own, turn(x, -64, 1), turn(y, -60, 1)) for x, y in ((high, east), (west, low))])
    level = ((lane % 64) // 8).astype(F32) + 0.5
    open_u = (jnp.minimum(ks, next_col(ks)) > level) & (lane % 8 < 7)
    open_v = jnp.minimum(ks, next_row(ks)) > level
    ub = jnp.where(open_u, next_col(gs) - gs, 0.0) * (next_col(cs) + cs)
    vb = jnp.where(open_v, next_row(gs) - gs, 0.0) * (next_row(cs) + cs)
    for by in (8, 16, 32):
        ub = ub + turn(ub, -by, 1)
        vb = vb + turn(vb, -by, 1)
    ub, vb = 0.0625 * ub, 0.0625 * vb
    terms = (ub - prev_col(ub)) + (vb - prev_row(vb))
    halo = col_halo(near, far)
    r_side = jnp.where(left, turn(terms, -4, 1), turn(terms, 60, 1)) + halo(68)
    r = jnp.concatenate(
        [
            s[:, :128] - jnp.where(lane == 0, turn(ub, -67, 1), 0.0),
            s[:, 128 : cols - 128],
            s[:, cols - 128 :] + jnp.where(lane == 127, turn(ub, 124, 1), 0.0),
            r_side,
        ],
        axis=1,
    )
    code = 0.125 * jnp.concatenate([code[...], halo(64)], axis=1)
    dg = jnp.concatenate([diag[...], halo(76)], axis=1)
    cu, cv = jnp.minimum(code, next_col(code)), jnp.minimum(code, next_row(code))

    def shifted(v):
        fu, fv = cu * (v - next_col(v)), cv * (v - next_row(v))
        return (dg - SHIFT) * v + ((fu - prev_col(fu)) + (fv - prev_row(fv)))

    p1 = shifted(r)
    p2 = shifted(p1)
    eu, ev = p2 - next_col(p2), p2 - next_row(p2)
    energy = dg * p2 * p2 + (cu * eu * eu + cv * ev * ev)
    r, p1, p2, energy = [a[:rows, :cols] for a in (r, p1, p2, energy)]
    r_ref[...] = r
    p1_ref[...] = p1
    p2_ref[...] = p2
    lane = iota((8, 128), 1)
    packed = jnp.zeros((8, 128), F32)
    for m, prod in enumerate((r * r, r * p1, p1 * p1, p1 * p2, p2 * p2, energy)):
        tiles = [
            prod[8 * i : 8 * i + 8, 128 * j : 128 * j + 128]
            for i in range(rows // 8)
            for j in range(cols // 128)
        ]
        while len(tiles) > 1:
            tiles = [sum(tiles[i : i + 2][1:], tiles[i]) for i in range(0, len(tiles), 2)]
        part = tiles[0]
        for by in (4, 2, 1):
            part = part + pltpu.roll(part, by, 0)
        for by in (64, 32, 16):
            part = part + pltpu.roll(part, by, 1)
        packed = jnp.where(lane // 16 == m, part, packed)
    for i in range(mom_ref.shape[0] // 8):
        mom_ref[8 * i : 8 * i + 8, :] = packed


def tracer_kernel(g_in, land_in, bottom_in, u_in, v_in, rn, rf, cn, cf, out_ref, g, land, bottom, u, v, out, sems, g_sems, out_sems):
    flat = [
        pltpu.make_async_copy(src, dst, sems.at[n])
        for n, (src, dst) in enumerate(((land_in, land), (bottom_in, bottom), (u_in, u), (v_in, v)))
    ]
    deep = [pltpu.make_async_copy(g_in.at[k], g.at[k], g_sems.at[k]) for k in range(LEV)]
    done = [pltpu.make_async_copy(out.at[k], out_ref.at[k], out_sems.at[k]) for k in range(LEV)]
    start_all(flat + deep)
    wait_all(flat)
    rows, cols = u.shape
    ch = col_halo(cn, cf)
    sub = iota((8, cols), 0)
    north, south = pick(is_even("row"), rn[...], rf[...])

    def wide(own, lane, above, below):
        at = [8 * (x // 8) for x in (above, below)]
        halo = jnp.where(
            sub == 0,
            turn(north[at[0] : at[0] + 8], -(above % 8), 0),
            turn(south[at[1] : at[1] + 8], 7 - below % 8, 0),
        )
        return jnp.concatenate([jnp.concatenate([own, halo], axis=0), ch(lane)], axis=1)

    code = wide(code_of(land[...], bottom[...]), 64, 20, 23)
    cu, cv = jnp.minimum(code, next_col(code)), jnp.minimum(code, next_row(code))
    uw = 0.125 * wide(u[...], 84, 28, 28)
    vw = 0.125 * wide(v[...], 84, 28, 28)
    for k in range(LEV):
        deep[k].wait()
        gk = wide(g[k], 8 * k, k, k)
        pu = jnp.where(cu > k + 0.5, next_col(gk) - gk, 0.0) * uw
        pv = jnp.where(cv > k + 0.5, next_row(gk) - gk, 0.0) * vw
        total = gk + pu + prev_col(pu) + pv + prev_row(pv)
        out[k] = total[:rows, :cols]
        done[k].start()
    wait_all(done)


def two_sum(a, b):
    s = a + b
    t = s - a
    return s, (a - (s - t)) + (b - t)


def quick(a, b):
    s = a + b
    return s, b - (s - a)


def split(a):
    t = a * 4097.0
    high = t - (t - a)
    return high, a - high


def add(x, y):
    s, e = two_sum(x[0], y[0])
    return quick(s, e + (x[1] + y[1]))


def neg(x):
    return -x[0], -x[1]


def mul(x, y):
    p = x[0] * y[0]
    (ah, al), (bh, bl) = split(x[0]), split(y[0])
    e = ((ah * bh - p) + ah * bl + al * bh) + al * bl
    return quick(p, e + (x[0] * y[1] + x[1] * y[0]))


def div(x, y):
    q = x[0] / y[0]
    rest = add(x, neg(mul((q, jnp.zeros_like(q)), y)))
    return quick(q, rest[0] / y[0])


def combine(mom, r, p1, p2, x_ref, x, sems):
    zero = jnp.zeros((8, 128), F32)
    tiles = [(mom[8 * i : 8 * i + 8, :], zero) for i in range(mom.shape[0] // 8)]
    while len(tiles) > 1:
        tiles = [add(tiles[i], tiles[i + 1]) for i in range(0, len(tiles), 2)]
    total = tiles[0]
    for by in (4, 2, 1):
        total = add(total, tuple(pltpu.roll(a, by, 0) for a in total))
    lane = iota((8, 128), 1)
    sums = []
    for m in range(6):
        mine = tuple(jnp.where(lane // 16 == m, a, 0.0) for a in total)
        for by in (64, 32, 16, 8, 4, 2, 1):
            mine = add(mine, tuple(pltpu.roll(a, by, 1) for a in mine))
        sums.append(mine)
    m00, m01, m11, m12, m22, e22 = sums
    a00, a01, a02 = add(m01, m00), add(m11, m01), add(m12, m11)
    a11, a12, a22 = a02, add(m22, m12), e22
    l10 = div(a01, a00)
    l20 = div(a02, a00)
    w11 = add(a11, neg(mul(l10, a01)))
    w12 = add(a12, neg(mul(l10, a02)))
    ok1 = w11[0] > 1e-9 * a11[0]
    l21 = tuple(jnp.where(ok1, a, 0.0) for a in div(w12, w11))
    w22 = add(add(a22, neg(mul(l20, a02))), neg(mul(l21, w12)))
    ok2 = w22[0] > 1e-9 * a22[0]
    b0 = m00
    b1 = add(m01, neg(mul(l10, b0)))
    z1 = tuple(jnp.where(ok1, a, 0.0) for a in div(b1, w11))
    b2 = add(add(m11, neg(mul(l20, b0))), neg(mul(l21, b1)))
    z2 = tuple(jnp.where(ok2, a, 0.0) for a in div(b2, w22))
    y2 = z2
    y1 = add(z1, neg(mul(l21, y2)))
    y0 = add(div(b0, a00), neg(add(mul(l10, y1), mul(l20, y2))))
    rows, cols = r.shape
    bands = sems.shape[0]
    tall = rows // bands
    done = []
    for b in range(bands):
        band = slice(b * tall, (b + 1) * tall)
        for i in range(b * tall // 8, (b + 1) * tall // 8):
            for j in range(cols // 128):
                at = (slice(8 * i, 8 * i + 8), slice(128 * j, 128 * j + 128))
                x[at] = y0[0] * r[at] + (y1[0] * p1[at] + y2[0] * p2[at])
        done.append(pltpu.make_async_copy(x.at[band, :], x_ref.at[band, :], sems.at[b]))
        done[-1].start()
    wait_all(done)


def call(kernel, ins, outs, scratch=(), name=None, cost=None):
    run = pl.pallas_call(
        kernel,
        in_specs=list(ins),
        out_specs=[spec for spec, _ in outs],
        out_shape=[spec.memory_space(shape, F32) for spec, shape in outs],
        scratch_shapes=list(scratch),
        compiler_params=PARAMS,
        cost_estimate=cost,
        name=name,
    )
    return lambda *args: run(*[pltpu.with_memory_space_constraint(x, spec.memory_space) for x, spec in zip(args, ins)])


def shards(tracer_adj_next, tracer, u_east, v_north, surf_adj_next, diag, land, bottom):
    levels, rows, cols = tracer.shape
    size = lax.axis_size("row") * lax.axis_size("col")
    g, c = tracer_adj_next, tracer
    dma = pltpu.SemaphoreType.DMA
    two, wide, side = (rows, cols), (rows + 8, cols), (rows + 8, 128)
    whole = lambda kind=F32: pltpu.VMEM(two, kind)
    edges = [pltpu.VMEM((levels, 8, cols), F32)] * 4 + [pltpu.VMEM((8, cols), jnp.int32)] * 4 + [pltpu.VMEM((8, cols), F32)] * 6
    row_sent = call(
        pack_rows, [HBM] * 7, [(VMEM, (32, cols))] * 2, edges + [dma((14,))], name="pack_rows"
    )(g, c, land, bottom, surf_adj_next, diag, v_north)
    row_got = swap(row_sent, "row")
    deep, ends = pltpu.VMEM(g.shape, F32), (2, levels, rows, 128)
    a, b = call(
        pack_cols,
        [HBM] * 7,
        [(VMEM, (rows, 128))] * 2,
        [pltpu.VMEM(ends, F32)] * 2
        + [pltpu.VMEM((2, rows, 128), jnp.int32)] * 2
        + [pltpu.VMEM((3, 2, rows, 128), F32), dma((7, 2))],
        name="pack_cols",
        cost=pl.CostEstimate(flops=4 * g.size, bytes_accessed=4 * g.size, transcendentals=0),
    )(g, c, land, bottom, surf_adj_next, diag, u_east)
    col_sent = call(join_cols, [VMEM] * 4, [(VMEM, side)] * 2, name="join_cols")(a, b, *row_got)
    col_got = swap(col_sent, "col")
    s, code, dg = call(
        rhs_rows,
        [HBM] * 6 + [VMEM] * 4,
        [(VMEM, wide)] * 3,
        [deep, deep, whole(jnp.int32), whole(jnp.int32), whole(), dma((4,)), dma((levels, 2))],
        name="rhs_rows",
        cost=pl.CostEstimate(flops=24 * g.size, bytes_accessed=8 * g.size, transcendentals=0),
    )(g, c, land, bottom, surf_adj_next, diag, *row_sent, *row_got)
    r, p1, p2, mom = call(
        krylov,
        [VMEM] * 7,
        [(VMEM, two)] * 3 + [(VMEM, (size, 128))],
        name="krylov",
    )(s, code, dg, *col_sent, *col_got)
    mom = lax.all_to_all(mom, ("row", "col"), 0, 0, tiled=True)
    (tracer_adj,) = call(
        tracer_kernel,
        [HBM] * 5 + [VMEM] * 4,
        [(HBM, g.shape)],
        [deep, whole(jnp.int32), whole(jnp.int32), whole(), whole(), deep, dma((4,)), dma((levels,)), dma((levels,))],
        name="tracer",
        cost=pl.CostEstimate(flops=20 * g.size, bytes_accessed=12 * g.size, transcendentals=0),
    )(g, land, bottom, u_east, v_north, *row_got, *col_got)
    (surf_adj,) = call(
        combine,
        [VMEM] * 4,
        [(HBM, two)],
        [whole(), dma((2,))],
        name="combine",
    )(mom, r, p1, p2)
    return tracer_adj, surf_adj


def solution(mesh):
    three, two = P(None, "row", "col"), P("row", "col")
    return jax.shard_map(
        shards,
        mesh=mesh,
        in_specs=(three, three, two, two, two, two, two, two),
        out_specs=(three, two),
        check_vma=False,
    )
```

```python
import functools

import jax
import jax.numpy as jnp
from jax import lax
from jax.experimental import pallas as pl
from jax.experimental.pallas import tpu as pltpu
from jax.sharding import PartitionSpec as P

LEV = 8
DEEP = 4
NEAR = 32
SHIFT = 1.0
F32 = jnp.float32
VMEM = pl.BlockSpec(memory_space=pltpu.VMEM)
HBM = pl.BlockSpec(memory_space=pltpu.HBM)
PARAMS = pltpu.CompilerParams(vmem_limit_bytes=32 * 1024 * 1024)


G, C, RHS, CODE, DIAG = 0, 1, 4, 5, 6


def code_of(land, bottom):
    return jnp.where(land == 1, bottom, 0).astype(F32)


def swap_pairs(axis, first):
    count = lax.axis_size(axis)
    pairs = []
    for low in range(first, count - 1, 2):
        pairs += [(low, low + 1), (low + 1, low)]
    return pairs


def is_even(axis):
    return lax.rem(lax.axis_index(axis), 2) == 0


def iota(shape, dim):
    return lax.broadcasted_iota(jnp.int32, shape, dim)


def turn(x, by, dim):
    by = by % x.shape[dim]
    return pltpu.roll(x, by, dim) if by else x


def next_col(a):
    return turn(a, -1, 1)


def prev_col(a):
    return turn(a, 1, 1)


def next_row(a):
    return turn(a, -1, 0)


def prev_row(a):
    return turn(a, 1, 0)


def pick(even, one, two):
    return jnp.where(even, one, two), jnp.where(even, two, one)


def start_all(copies):
    for copy in copies:
        copy.start()


def wait_all(copies):
    for copy in copies:
        copy.wait()


def pack_rows(g, c, land, bottom, surf, diag, v, a_ref, b_ref, g0, g1, c0, c1, l0, l1, b0, b1, s0, s1, d0, d1, v0, v1, sems):
    rows = surf.shape[0]
    copies = []
    for src, low, high in ((g, g0, g1), (c, c0, c1), (land, l0, l1), (bottom, b0, b1), (surf, s0, s1), (diag, d0, d1), (v, v0, v1)):
        for dst, at in ((low, slice(0, 8)), (high, slice(rows - 8, rows))):
            part = src.at[:, at, :] if len(src.shape) == 3 else src.at[at, :]
            copies.append(pltpu.make_async_copy(part, dst, sems.at[len(copies)]))
    start_all(copies)
    wait_all(copies)

    cols = surf.shape[1]
    lane, sub = iota((8, cols), 1), iota((8, cols), 0)
    upper = sub < DEEP

    def tiles(g, c, land, bottom, surf, diag, v, of_last):
        code = code_of(land[...], bottom[...])
        g, c = [g[k] for k in range(LEV)], [c[k] for k in range(LEV)]
        cu = jnp.where(lane < cols - 1, jnp.minimum(code, next_col(code)), 0.0)
        cv = jnp.where(sub < 7, jnp.minimum(code, next_row(code)), 0.0)
        ub, vb = faces(g, c, cu, cv)
        rhs = surf[...] + 0.0625 * ((ub - prev_col(ub)) + (vb - prev_row(vb)))
        edge = 7 if of_last else 0

        def outermost(x):
            out = turn(x[0], -edge, 0)
            for k in range(1, LEV):
                out = jnp.where(sub == k, turn(x[k], k - edge, 0), out)
            return out

        half = DEEP if of_last else 0
        one = jnp.where(upper, turn(rhs, half, 0), turn(code, DEEP - half, 0))
        two = jnp.where(upper, turn(diag[...], half, 0), turn(v[...], DEEP - edge, 0))
        ends = []
        for high, lanes in ((False, slice(0, 128)), (True, slice(cols - 128, cols))):
            cut = lambda xs: [x[:, lanes] for x in xs]
            corner = lane_pack(cut(g), cut(c), code[:, lanes], cut([surf, diag]), high)
            ends.append(jnp.where(sub[:, :128] < 5, two[:, lanes], corner if of_last else turn(corner, 5, 0)))
        two = jnp.concatenate([ends[0], two[:, 128 : cols - 128], ends[1]], axis=1)
        return outermost(g), outermost(c), one, two

    first = tiles(g0, c0, l0, b0, s0, d0, v0, False)
    last = tiles(g1, c1, l1, b1, s1, d1, v1, True)
    even = is_even("row")
    for t in range(4):
        a_ref[8 * t : 8 * t + 8, :], b_ref[8 * t : 8 * t + 8, :] = pick(even, last[t], first[t])


def faces(g, c, cu, cv):
    ub, vb = jnp.zeros_like(cu), jnp.zeros_like(cv)
    for k in range(LEV):
        gk, ck = g[k], c[k]
        ub = ub + jnp.where(cu > k + 0.5, next_col(gk) - gk, 0.0) * (next_col(ck) + ck)
        vb = vb + jnp.where(cv > k + 0.5, next_row(gk) - gk, 0.0) * (next_row(ck) + ck)
    return ub, vb


def operator(cu, cv, dg):
    west, south = prev_col(cu), prev_row(cv)
    center = (dg - SHIFT) + ((cu + west) + (cv + south))

    def shifted(v):
        sides = (cu * next_col(v) + west * prev_col(v)) + (cv * next_row(v) + south * prev_row(v))
        return center * v - sides

    return shifted


def products(r, cu, cv, dg, rows):
    shifted = operator(cu, cv, dg)
    p1 = shifted(r)
    p2 = shifted(p1)
    eu, ev = p2 - next_col(p2), p2 - next_row(p2)
    energy = dg * p2 * p2 + (cu * eu * eu + cv * ev * ev)
    q, p, o = r[:rows], p1[:rows], p2[:rows]
    return p1, p2, (q * q, q * p, p * p, p * o, o * o, energy[:rows])


def fold(prod, lanes):
    tiles = [prod[8 * i : 8 * i + 8, lanes] for i in range(prod.shape[0] // 8)]
    while len(tiles) > 1:
        tiles = [sum(tiles[i : i + 2][1:], tiles[i]) for i in range(0, len(tiles), 2)]
    return tiles[0]


def lane_pack(g, c, code, rest, of_last):
    group = iota(code.shape, 1) // DEEP
    base, one, two = (DEEP, 0, 1) if of_last else (0, 1, 0)
    places = [(g[k], 2 * k + one) for k in range(LEV)] + [(c[k], 16 + 2 * k + one) for k in range(LEV)]
    places += [(code, 2 * k + two) for k in range(LEV)] + [(x, 16 + 2 * n + two) for n, x in enumerate(rest)]
    if of_last:
        places.append((code, 31))
    out = jnp.zeros_like(code)
    for x, at in places:
        out = jnp.where(group == at, turn(x, DEEP * at + base, 1), out)
    return out


def pack_cols(g, c, land, bottom, surf, diag, u, row_in, a_ref, b_ref, row_ref):
    row_ref[...] = row_in[...]
    cols = surf.shape[1]
    packs = [
        lane_pack(
            [g[k, :, lanes] for k in range(LEV)],
            [c[k, :, lanes] for k in range(LEV)],
            code_of(land[:, lanes], bottom[:, lanes]),
            [x[:, lanes] for x in (surf, diag, u)],
            of_last,
        )
        for of_last, lanes in ((True, slice(cols - 128, cols)), (False, slice(0, 128)))
    ]
    a_ref[...], b_ref[...] = pick(is_even("col"), *packs)


def row_halo(near, far, lanes):
    even = is_even("row")

    def plane(p):
        at = slice(8 * (p // 2), 8 * (p // 2) + 8)
        north, south = pick(even, near[at, lanes], far[at, lanes])
        upper = iota(north.shape, 0) < DEEP
        if p % 2 == 0:
            return jnp.where(upper, north, turn(south, DEEP, 0))
        return jnp.where(upper, turn(north, DEEP, 0), south)

    return plane


def join_cols(of_near, own, near, far, *refs):
    rows, width = own.shape[0], near.shape[1]
    out = refs[-1]
    even = is_even("row")
    packs = []
    for lanes in (slice(width - 128, width), slice(0, 128)):
        north, south = pick(even, near[24:, lanes], far[24:, lanes])
        sub = iota(north.shape, 0)
        packs.append(jnp.where(sub < 3, turn(north, -5, 0), jnp.where(sub < 5, 0.0, south)))
    out[:rows, :] = own[...]
    out[rows:, :] = pick(is_even("col"), *packs)[0 if of_near else 1]


def rhs_rows(g, c, land, bottom, surf, diag, sent_a, sent_b, near, far, r_ref, code_ref, diag_ref, rs_ref, codes_ref, diags_ref):
    rows, cols = surf.shape
    even = is_even("row")
    lane, sub = iota((8, cols), 1), iota((8, cols), 0)
    upper = sub < DEEP

    high, low = pick(even, sent_a[...], sent_b[...])
    north, south = pick(even, near[...], far[...])

    def across(below, above, here, there):
        pair = [x[16 + at : 17 + at, :] for x, at in ((below, here), (above, there))]
        open_v = jnp.minimum(*pair) > sub.astype(F32) + 0.5
        total = jnp.where(open_v, above[:8] - below[:8], 0.0) * (above[8:16] + below[8:16])
        for by in (4, 2, 1):
            total = total + turn(total, by, 0)
        return 0.0625 * total

    up = across(high, north, 7, 4)
    down = across(south, low, 7, 4)
    halo = row_halo(near, far, slice(0, cols))
    r_halo = halo(RHS) + jnp.where(sub == 0, -up, jnp.where(sub == 7, down, 0.0))
    code = code_of(land[...], bottom[...])
    cu = jnp.where(iota(code.shape, 1) < cols - 1, jnp.minimum(code, next_col(code)), 0.0)
    cv = jnp.where(iota(code.shape, 0) < rows - 1, jnp.minimum(code, next_row(code)), 0.0)
    ub, vb = faces(g, c, cu, cv)
    r = surf[...] + 0.0625 * ((ub - prev_col(ub)) + (vb - prev_row(vb)))
    low = r[:8] - jnp.where(sub == 0, down, 0.0)
    high = r[rows - 8 :] + jnp.where(sub == 7, up, 0.0)
    r = jnp.concatenate([low, r[8 : rows - 8], high, r_halo], axis=0)
    code = jnp.concatenate([code, halo(CODE)], axis=0)
    dg = jnp.concatenate([diag[...], halo(DIAG)], axis=0)
    left = iota((rows + 8, 128), 1) < 64
    for x, ref in ((r, rs_ref), (code, codes_ref), (dg, diags_ref)):
        ref[...] = jnp.where(left, turn(x[:, cols - 128 :], -68, 1), turn(x[:, :128], 68, 1))
    r_ref[...] = r
    code_ref[...] = code
    diag_ref[...] = dg


def inner(r_in, code_in, diag_in, r_ref, p1_ref, p2_ref, mom_ref, sem):
    rows, cols = p1_ref.shape
    copy = pltpu.make_async_copy(r_in.at[:rows, :], r_ref, sem)
    copy.start()
    code = 0.125 * code_in[...]
    cu = jnp.where(iota(code.shape, 1) < cols - 1, jnp.minimum(code, next_col(code)), 0.0)
    cv = jnp.minimum(code, next_row(code))
    p1, p2, prods = products(r_in[...], cu, cv, diag_in[...], rows)
    p1_ref[...] = p1[:rows]
    p2_ref[...] = p2[:rows]
    lane = iota((8, 128), 1)
    for m, prod in enumerate(prods):
        parts = [fold(prod, slice(128 * j, 128 * j + 128)) for j in range(cols // 128)]
        parts[0] = jnp.where(lane >= NEAR, parts[0], 0.0)
        parts[-1] = jnp.where(lane < 128 - NEAR, parts[-1], 0.0)
        mom_ref[8 * m : 8 * m + 8, :] = sum(parts[1:], parts[0])
    copy.wait()


def col_halo(near, far):
    east, west = pick(is_even("col"), near[...], far[...])
    left = iota(east.shape, 1) < 64

    def plane(of_east, of_west):
        return jnp.where(left, turn(east, -of_east, 1), turn(west, 124 - of_west, 1))

    return plane


def outer(rs, codes, diags, mom_in, sent_a, sent_b, near, far, r_ref, p1_ref, p2_ref, mom_ref):
    rows = rs.shape[0] - 8
    even = is_even("col")
    high, low = pick(even, sent_a[...], sent_b[...])
    east, west = pick(even, near[...], far[...])
    lane = iota(high.shape, 1)
    place = lane % 8
    own, left = place < DEEP, lane < 64
    level = (lane // 8).astype(F32) + 0.5

    def rhs_terms(first, second, u_from, v_from):
        gc = jnp.where(own, first, second)
        mixed = jnp.where(own, second, first)
        code = turn(mixed, 4, 1)
        one, two = turn(gc, -1, 1) - gc, turn(gc, 63, 1) + turn(gc, 64, 1)
        keep = (place >= u_from) & (place < u_from + 4)
        open_u = (jnp.minimum(code, turn(mixed, 3, 1)) > level) & keep
        ub = jnp.where(open_u, one, 0.0) * two
        one, two = gc - turn(gc, 1, 1), turn(gc, 64, 1) + turn(gc, 65, 1)
        keep = (place > u_from) & (place <= u_from + 4)
        open_u = (jnp.minimum(code, turn(mixed, 5, 1)) > level) & keep
        ub = ub - jnp.where(open_u, one, 0.0) * two
        keep = (place >= v_from) & (place < v_from + 4)
        open_v = (jnp.minimum(code, next_row(code)) > level) & keep
        c = turn(gc, 64, 1)
        vb = jnp.where(open_v, next_row(gc) - gc, 0.0) * (next_row(c) + c)
        return ub + (vb - prev_row(vb))

    at_east = rhs_terms(high, east, 3, 4)
    for by in (8, 16, 32):
        at_east = at_east + turn(at_east, by, 1)
    at_west = rhs_terms(west, low, 0, 0)
    at_west = turn(at_west, 64, 1) + turn(at_west, 56, 1)
    for by in (16, 32):
        at_west = at_west + turn(at_west, -by, 1)

    def filled(x, e, w):
        return jnp.where((lane < 60) | (lane >= 68), x, jnp.where(left, e, w))

    added = jnp.where((lane >= 59) & (lane < 69), jnp.where(left, at_east, at_west), 0.0)
    r = filled(rs[...], turn(east, -4, 1), turn(west, -4, 1)) + 0.0625 * added
    code = 0.125 * filled(codes[...], turn(east, 4, 1), turn(west, 4, 1))
    dg = filled(diags[...], turn(east, -12, 1), turn(west, -12, 1))
    cu, cv = jnp.minimum(code, next_col(code)), jnp.minimum(code, next_row(code))
    p1, p2, prods = products(r, cu, cv, dg, rows)
    r_ref[...] = r
    p1_ref[...] = p1
    p2_ref[...] = p2
    lane = iota((8, 128), 1)
    mine = ((lane >= 60 - NEAR) & (lane < 60)) | ((lane >= 68) & (lane < 68 + NEAR))
    packed = jnp.zeros((8, 128), F32)
    for m, prod in enumerate(prods):
        part = mom_in[8 * m : 8 * m + 8, :] + jnp.where(mine, fold(prod, slice(0, 128)), 0.0)
        for by in (4, 2, 1):
            part = part + turn(part, by, 0)
        part = ((part + turn(part, 16, 1)) + (turn(part, 32, 1) + turn(part, 48, 1))) + (
            (turn(part, 64, 1) + turn(part, 80, 1)) + (turn(part, 96, 1) + turn(part, 112, 1))
        )
        part = (part + turn(part, 4, 1)) + (turn(part, 8, 1) + turn(part, 12, 1))
        packed = jnp.where(lane // 4 == m, part, packed)
    for i in range(mom_ref.shape[0] // 8):
        mom_ref[8 * i : 8 * i + 8, :] = packed


def tracer_kernel(g_in, land_in, bottom_in, u_in, v_in, rn, rf, cn, cf, out_ref, g, land, bottom, u, v, out, sems, g_sems, out_sems):
    flat = [
        pltpu.make_async_copy(src, dst, sems.at[n])
        for n, (src, dst) in enumerate(((land_in, land), (bottom_in, bottom), (u_in, u), (v_in, v)))
    ]
    deep = [pltpu.make_async_copy(g_in.at[k], g.at[k], g_sems.at[k]) for k in range(LEV)]
    done = [pltpu.make_async_copy(out.at[k], out_ref.at[k], out_sems.at[k]) for k in range(LEV)]
    start_all(flat + deep)
    wait_all(flat)
    rows, cols = u.shape
    ch = col_halo(cn, cf)
    sub = iota((8, cols), 0)
    north, south = pick(is_even("row"), rn[...], rf[...])

    def wide(own, lanes, above, below):
        at = [8 * (x // 8) for x in (above, below)]
        halo = jnp.where(
            sub == 0,
            turn(north[at[0] : at[0] + 8], -(above % 8), 0),
            turn(south[at[1] : at[1] + 8], 7 - below % 8, 0),
        )
        return jnp.concatenate([jnp.concatenate([own, halo], axis=0), ch(*lanes)], axis=1)

    code = wide(code_of(land[...], bottom[...]), (0, 4), 20, 23)
    cu, cv = jnp.minimum(code, next_col(code)), jnp.minimum(code, next_row(code))
    uw = 0.125 * wide(u[...], (80, 84), 28, 28)
    vw = 0.125 * wide(v[...], (80, 84), 28, 28)
    for k in range(LEV):
        deep[k].wait()
        gk = wide(g[k], (8 * k + 4, 8 * k), k, k)
        pu = jnp.where(cu > k + 0.5, next_col(gk) - gk, 0.0) * uw
        pv = jnp.where(cv > k + 0.5, next_row(gk) - gk, 0.0) * vw
        total = gk + pu + prev_col(pu) + pv + prev_row(pv)
        out[k] = total[:rows, :cols]
        done[k].start()
    wait_all(done)


def two_sum(a, b):
    s = a + b
    t = s - a
    return s, (a - (s - t)) + (b - t)


def quick(a, b):
    s = a + b
    return s, b - (s - a)


def split(a):
    t = a * 4097.0
    high = t - (t - a)
    return high, a - high


def add(x, y):
    s, e = two_sum(x[0], y[0])
    return quick(s, e + (x[1] + y[1]))


def neg(x):
    return -x[0], -x[1]


def mul(x, y):
    p = x[0] * y[0]
    (ah, al), (bh, bl) = split(x[0]), split(y[0])
    e = ((ah * bh - p) + ah * bl + al * bh) + al * bl
    return quick(p, e + (x[0] * y[1] + x[1] * y[0]))


def div(x, y):
    q = x[0] / y[0]
    rest = add(x, neg(mul((q, jnp.zeros_like(q)), y)))
    return quick(q, rest[0] / y[0])


def combine(mom, r, p1, p2, rs, p1s, p2s, x_ref, x, sems):
    zero = jnp.zeros((8, 128), F32)
    tiles = [(mom[8 * i : 8 * i + 8, :], zero) for i in range(mom.shape[0] // 8)]
    while len(tiles) > 1:
        tiles = [add(tiles[i], tiles[i + 1]) for i in range(0, len(tiles), 2)]
    total = tiles[0]
    for by in (4, 2, 1):
        total = add(total, tuple(pltpu.roll(a, by, 0) for a in total))
    sums = []
    for m in range(6):
        four = [
            tuple(jnp.broadcast_to(a[:, at : at + 1], (8, 128)) for a in total)
            for at in range(4 * m, 4 * m + 4)
        ]
        sums.append(add(add(four[0], four[1]), add(four[2], four[3])))
    m00, m01, m11, m12, m22, e22 = sums
    a00, a01, a02 = add(m01, m00), add(m11, m01), add(m12, m11)
    a11, a12, a22 = a02, add(m22, m12), e22
    l10 = div(a01, a00)
    l20 = div(a02, a00)
    w11 = add(a11, neg(mul(l10, a01)))
    w12 = add(a12, neg(mul(l10, a02)))
    ok1 = w11[0] > 1e-9 * a11[0]
    l21 = tuple(jnp.where(ok1, a, 0.0) for a in div(w12, w11))
    w22 = add(add(a22, neg(mul(l20, a02))), neg(mul(l21, w12)))
    ok2 = w22[0] > 1e-9 * a22[0]
    b0 = m00
    b1 = add(m01, neg(mul(l10, b0)))
    z1 = tuple(jnp.where(ok1, a, 0.0) for a in div(b1, w11))
    b2 = add(add(m11, neg(mul(l20, b0))), neg(mul(l21, b1)))
    z2 = tuple(jnp.where(ok2, a, 0.0) for a in div(b2, w22))
    y2 = z2
    y1 = add(z1, neg(mul(l21, y2)))
    y0 = add(div(b0, a00), neg(add(mul(l10, y1), mul(l20, y2))))
    rows, cols = r.shape
    bands = sems.shape[0]
    tall = rows // bands
    done = []
    for b in range(bands):
        band = slice(b * tall, (b + 1) * tall)
        for i in range(b * tall // 8, (b + 1) * tall // 8):
            at = slice(8 * i, 8 * i + 8)
            lane = iota((8, 128), 1)
            side = y0[0] * rs[at, :] + (y1[0] * p1s[at, :] + y2[0] * p2s[at, :])
            for j in range(cols // 128):
                to = (at, slice(128 * j, 128 * j + 128))
                tile = y0[0] * r[to] + (y1[0] * p1[to] + y2[0] * p2[to])
                if j == 0:
                    tile = jnp.where(lane < NEAR, turn(side, -68, 1), tile)
                if j == cols // 128 - 1:
                    tile = jnp.where(lane >= 128 - NEAR, turn(side, 68, 1), tile)
                x[to] = tile
        done.append(pltpu.make_async_copy(x.at[band, :], x_ref.at[band, :], sems.at[b]))
        done[-1].start()
    wait_all(done)


def call(kernel, ins, outs, scratch=(), name=None, cost=None):
    run = pl.pallas_call(
        kernel,
        in_specs=list(ins),
        out_specs=[spec for spec, _ in outs],
        out_shape=[spec.memory_space(shape, F32) for spec, shape in outs],
        scratch_shapes=list(scratch),
        compiler_params=PARAMS,
        cost_estimate=cost,
        name=name,
    )
    return lambda *args: run(*[pltpu.with_memory_space_constraint(x, spec.memory_space) for x, spec in zip(args, ins)])


def shards(tracer_adj_next, tracer, u_east, v_north, surf_adj_next, diag, land, bottom):
    levels, rows, cols = tracer.shape
    size = lax.axis_size("row") * lax.axis_size("col")
    g, c = tracer_adj_next, tracer
    dma = pltpu.SemaphoreType.DMA
    two, side = (rows, cols), (rows + 8, 128)
    whole = lambda kind=F32: pltpu.VMEM(two, kind)
    edges = [pltpu.VMEM((levels, 8, cols), F32)] * 4 + [pltpu.VMEM((8, cols), jnp.int32)] * 4 + [pltpu.VMEM((8, cols), F32)] * 6
    row_a, row_b = call(
        pack_rows, [HBM] * 7, [(VMEM, (32, cols))] * 2, edges + [dma((14,))], name="pack_rows"
    )(g, c, land, bottom, surf_adj_next, diag, v_north)
    row_far = lax.ppermute(row_b, "row", swap_pairs("row", 1))
    deep = pltpu.VMEM(g.shape, F32)
    a, b, row_a = call(
        pack_cols,
        [VMEM] * 8,
        [(VMEM, (rows, 128))] * 2 + [(VMEM, (32, cols))],
        name="pack_cols",
        cost=pl.CostEstimate(flops=g.size, bytes_accessed=g.size, transcendentals=0),
    )(g, c, land, bottom, surf_adj_next, diag, u_east, row_a)
    row_near = lax.ppermute(row_a, "row", swap_pairs("row", 0))
    row_sent, row_got = (row_a, row_b), (row_near, row_far)
    (b,) = call(functools.partial(join_cols, False), [VMEM] * 3, [(VMEM, side)], name="join_far")(b, *row_got)
    far = lax.ppermute(b, "col", swap_pairs("col", 1))
    *fields, rs, codes, diags = call(
        rhs_rows,
        [VMEM] * 10,
        [(VMEM, (rows + 8, cols))] * 3 + [(VMEM, side)] * 3,
        name="rhs_rows",
        cost=pl.CostEstimate(flops=24 * g.size, bytes_accessed=8 * g.size, transcendentals=0),
    )(g, c, land, bottom, surf_adj_next, diag, *row_sent, *row_got)
    (a,) = call(functools.partial(join_cols, True), [VMEM] * 4, [(VMEM, side)], name="join_near")(a, *row_got, rs)
    near = lax.ppermute(a, "col", swap_pairs("col", 0))
    col_sent, col_got = (a, b), (near, far)
    r, p1, p2, mom = call(
        inner,
        [VMEM] * 3,
        [(HBM, two)] + [(VMEM, two)] * 2 + [(VMEM, (48, 128))],
        [dma],
        name="inner",
        cost=pl.CostEstimate(flops=12 * g.size, bytes_accessed=4 * g.size, transcendentals=0),
    )(*fields)
    *sides, mom = call(outer, [VMEM] * 8, [(VMEM, side)] * 3 + [(VMEM, (size, 128))], name="outer")(
        rs, codes, diags, mom, *col_sent, *col_got
    )
    mom = lax.all_to_all(mom, ("row", "col"), 0, 0, tiled=True)
    (tracer_adj,) = call(
        tracer_kernel,
        [HBM] * 5 + [VMEM] * 4,
        [(HBM, g.shape)],
        [deep, whole(jnp.int32), whole(jnp.int32), whole(), whole(), deep, dma((4,)), dma((levels,)), dma((levels,))],
        name="tracer",
        cost=pl.CostEstimate(flops=20 * g.size, bytes_accessed=12 * g.size, transcendentals=0),
    )(g, land, bottom, u_east, v_north, *row_got, *col_got)
    (surf_adj,) = call(
        combine,
        [VMEM] * 7,
        [(HBM, two)],
        [whole(), dma((2,))],
        name="combine",
    )(mom, r, p1, p2, *sides)
    return tracer_adj, surf_adj


def solution(mesh):
    three, two = P(None, "row", "col"), P("row", "col")
    return jax.shard_map(
        shards,
        mesh=mesh,
        in_specs=(three, three, two, two, two, two, two, two),
        out_specs=(three, two),
        check_vma=False,
    )
```

```python
import functools

import jax
import jax.numpy as jnp
from jax import lax
from jax.experimental import pallas as pl
from jax.experimental.pallas import tpu as pltpu
from jax.sharding import PartitionSpec as P

LEV = 8
DEEP = 4
NEAR = 32
SHIFT = 1.0
F32 = jnp.float32
VMEM = pl.BlockSpec(memory_space=pltpu.VMEM)
HBM = pl.BlockSpec(memory_space=pltpu.HBM)
PARAMS = pltpu.CompilerParams(vmem_limit_bytes=32 * 1024 * 1024)


G, C, RHS, CODE, DIAG = 0, 1, 4, 5, 6


def code_of(land, bottom):
    return jnp.where(land == 1, bottom, 0).astype(F32)


def swap_pairs(axis, first):
    count = lax.axis_size(axis)
    pairs = []
    for low in range(first, count - 1, 2):
        pairs += [(low, low + 1), (low + 1, low)]
    return pairs


def is_even(axis):
    return lax.rem(lax.axis_index(axis), 2) == 0


def iota(shape, dim):
    return lax.broadcasted_iota(jnp.int32, shape, dim)


def turn(x, by, dim):
    by = by % x.shape[dim]
    return pltpu.roll(x, by, dim) if by else x


def next_col(a):
    return turn(a, -1, 1)


def prev_col(a):
    return turn(a, 1, 1)


def next_row(a):
    return turn(a, -1, 0)


def prev_row(a):
    return turn(a, 1, 0)


def pick(even, one, two):
    return jnp.where(even, one, two), jnp.where(even, two, one)


def start_all(copies):
    for copy in copies:
        copy.start()


def wait_all(copies):
    for copy in copies:
        copy.wait()


def pack_rows(g, c, land, bottom, surf, diag, v, a_ref, b_ref, g0, g1, c0, c1, l0, l1, b0, b1, s0, s1, d0, d1, v0, v1, sems):
    rows = surf.shape[0]
    copies = []
    for src, low, high in ((g, g0, g1), (c, c0, c1), (land, l0, l1), (bottom, b0, b1), (surf, s0, s1), (diag, d0, d1), (v, v0, v1)):
        for dst, at in ((low, slice(0, 8)), (high, slice(rows - 8, rows))):
            part = src.at[:, at, :] if len(src.shape) == 3 else src.at[at, :]
            copies.append(pltpu.make_async_copy(part, dst, sems.at[len(copies)]))
    start_all(copies)
    wait_all(copies)

    cols = surf.shape[1]
    lane, sub = iota((8, cols), 1), iota((8, cols), 0)
    upper = sub < DEEP
    codes = [code_of(l0[...], b0[...]), code_of(l1[...], b1[...])]
    both = [jnp.where(upper, g0[k], g1[k]) for k in range(LEV)], [jnp.where(upper, c0[k], c1[k]) for k in range(LEV)]
    code = jnp.where(upper, *codes)
    cu = jnp.where(lane < cols - 1, jnp.minimum(code, next_col(code)), 0.0)
    ub = faces(*both, cu, next_col)
    ub = ub - prev_col(ub)
    corners = []
    for high, lanes in ((False, slice(0, 128)), (True, slice(cols - 128, cols))):
        cut = lambda xs: [x[:, lanes] for x in xs]
        rest = [jnp.where(upper, s0[...], s1[...]), jnp.where(upper, d0[...], d1[...])]
        corners.append(lane_pack(cut(both[0]), cut(both[1]), code[:, lanes], cut(rest), high))

    def tiles(g, c, code, surf, diag, v, of_last):
        g, c = [g[k] for k in range(LEV)], [c[k] for k in range(LEV)]
        cv = jnp.where(sub < 7, jnp.minimum(code, next_row(code)), 0.0)
        vb = faces(g, c, cv, next_row)
        rhs = surf[...] + 0.0625 * (ub + (vb - prev_row(vb)))
        edge = 7 if of_last else 0

        def outermost(x):
            out = turn(x[0], -edge, 0)
            for k in range(1, LEV):
                out = jnp.where(sub == k, turn(x[k], k - edge, 0), out)
            return out

        half = DEEP if of_last else 0
        one = jnp.where(upper, turn(rhs, half, 0), turn(code, DEEP - half, 0))
        two = jnp.where(upper, turn(diag[...], half, 0), turn(v[...], DEEP - edge, 0))
        ends = [
            jnp.where(sub[:, :128] < 5, two[:, lanes], corner if of_last else turn(corner, 5, 0))
            for corner, lanes in zip(corners, (slice(0, 128), slice(cols - 128, cols)))
        ]
        two = jnp.concatenate([ends[0], two[:, 128 : cols - 128], ends[1]], axis=1)
        return outermost(g), outermost(c), one, two

    first = tiles(g0, c0, codes[0], s0, d0, v0, False)
    last = tiles(g1, c1, codes[1], s1, d1, v1, True)
    even = is_even("row")
    for t in range(4):
        a_ref[8 * t : 8 * t + 8, :], b_ref[8 * t : 8 * t + 8, :] = pick(even, last[t], first[t])


def faces(g, c, coupling, step):
    total = jnp.zeros_like(coupling)
    for k in range(LEV):
        gk, ck = g[k], c[k]
        total = total + jnp.where(coupling > k + 0.5, step(gk) - gk, 0.0) * (step(ck) + ck)
    return total


def operator(cu, cv, dg):
    west, south = prev_col(cu), prev_row(cv)
    center = (dg - SHIFT) + ((cu + west) + (cv + south))

    def shifted(v):
        sides = (cu * next_col(v) + west * prev_col(v)) + (cv * next_row(v) + south * prev_row(v))
        return center * v - sides

    return shifted


def products(r, cu, cv, dg, rows):
    shifted = operator(cu, cv, dg)
    p1 = shifted(r)
    p2 = shifted(p1)
    eu, ev = p2 - next_col(p2), p2 - next_row(p2)
    energy = dg * p2 * p2 + (cu * eu * eu + cv * ev * ev)
    q, p, o = r[:rows], p1[:rows], p2[:rows]
    return p1, p2, (q * q, q * p, p * p, p * o, o * o, energy[:rows])


def fold(prod, lanes):
    tiles = [prod[8 * i : 8 * i + 8, lanes] for i in range(prod.shape[0] // 8)]
    while len(tiles) > 1:
        tiles = [sum(tiles[i : i + 2][1:], tiles[i]) for i in range(0, len(tiles), 2)]
    return tiles[0]


def lane_pack(g, c, code, rest, of_last):
    group = iota(code.shape, 1) // DEEP
    base, one, two = (DEEP, 0, 1) if of_last else (0, 1, 0)
    places = [(g[k], 2 * k + one) for k in range(LEV)] + [(c[k], 16 + 2 * k + one) for k in range(LEV)]
    places += [(x, 16 + 2 * n + two) for n, x in enumerate(rest)]
    if of_last:
        places.append((code, 31))
    out = jnp.where(group == two, turn(code, DEEP * two + base, 1), 0.0)
    for by in (8, 16, 32):
        out = out + turn(out, by, 1)
    for x, at in places:
        out = jnp.where(group == at, turn(x, DEEP * at + base, 1), out)
    return out


def pack_cols(g, c, land, bottom, surf, diag, u, row_in, a_ref, b_ref, row_ref):
    row_ref[...] = row_in[...]
    cols = surf.shape[1]
    packs = [
        lane_pack(
            [g[k, :, lanes] for k in range(LEV)],
            [c[k, :, lanes] for k in range(LEV)],
            code_of(land[:, lanes], bottom[:, lanes]),
            [x[:, lanes] for x in (surf, diag, u)],
            of_last,
        )
        for of_last, lanes in ((True, slice(cols - 128, cols)), (False, slice(0, 128)))
    ]
    a_ref[...], b_ref[...] = pick(is_even("col"), *packs)


def row_halo(near, far, lanes):
    even = is_even("row")

    def plane(p):
        at = slice(8 * (p // 2), 8 * (p // 2) + 8)
        north, south = pick(even, near[at, lanes], far[at, lanes])
        upper = iota(north.shape, 0) < DEEP
        if p % 2 == 0:
            return jnp.where(upper, north, turn(south, DEEP, 0))
        return jnp.where(upper, turn(north, DEEP, 0), south)

    return plane


def join_cols(of_near, own, near, far, *refs):
    rows, width = own.shape[0], near.shape[1]
    out = refs[-1]
    even = is_even("row")
    packs = []
    for lanes in (slice(width - 128, width), slice(0, 128)):
        north, south = pick(even, near[24:, lanes], far[24:, lanes])
        sub = iota(north.shape, 0)
        packs.append(jnp.where(sub < 3, turn(north, -5, 0), jnp.where(sub < 5, 0.0, south)))
    out[:rows, :] = own[...]
    out[rows:, :] = pick(is_even("col"), *packs)[0 if of_near else 1]


def local_rhs(g, c, land, bottom, surf, r_ref, code_ref):
    rows, cols = surf.shape
    code = code_of(land[...], bottom[...])
    code_ref[...] = code
    cu = jnp.where(iota(code.shape, 1) < cols - 1, jnp.minimum(code, next_col(code)), 0.0)
    cv = jnp.where(iota(code.shape, 0) < rows - 1, jnp.minimum(code, next_row(code)), 0.0)
    ub, vb = faces(g, c, cu, next_col), faces(g, c, cv, next_row)
    r_ref[...] = surf[...] + 0.0625 * ((ub - prev_col(ub)) + (vb - prev_row(vb)))


def inner(r_in, code_in, diag, sent_a, sent_b, near, far, r_ref, p1_ref, p2_ref, mom_ref, rs_ref, codes_ref, diags_ref, r_own, sem):
    rows, cols = diag.shape
    even = is_even("row")
    lane, sub = iota((8, cols), 1), iota((8, cols), 0)
    high, low = pick(even, sent_a[...], sent_b[...])
    north, south = pick(even, near[...], far[...])

    def across(below, above, here, there):
        pair = [x[16 + at : 17 + at, :] for x, at in ((below, here), (above, there))]
        open_v = jnp.minimum(*pair) > sub.astype(F32) + 0.5
        total = jnp.where(open_v, above[:8] - below[:8], 0.0) * (above[8:16] + below[8:16])
        for by in (4, 2, 1):
            total = total + turn(total, by, 0)
        return 0.0625 * total

    up = across(high, north, 7, 4)
    down = across(south, low, 7, 4)
    halo = row_halo(near, far, slice(0, cols))
    r_halo = halo(RHS) + jnp.where(sub == 0, -up, jnp.where(sub == 7, down, 0.0))
    low = r_in[:8] - jnp.where(sub == 0, down, 0.0)
    high = r_in[rows - 8 :] + jnp.where(sub == 7, up, 0.0)
    r = jnp.concatenate([low, r_in[8 : rows - 8], high, r_halo], axis=0)
    r_own[...] = r[:rows]
    copy = pltpu.make_async_copy(r_own, r_ref, sem)
    copy.start()
    code = jnp.concatenate([code_in[...], halo(CODE)], axis=0)
    dg = jnp.concatenate([diag[...], halo(DIAG)], axis=0)
    left = iota((rows + 8, 128), 1) < 64
    for x, ref in ((r, rs_ref), (code, codes_ref), (dg, diags_ref)):
        ref[...] = jnp.where(left, turn(x[:, cols - 128 :], -68, 1), turn(x[:, :128], 68, 1))
    code = 0.125 * code
    cu = jnp.where(iota(code.shape, 1) < cols - 1, jnp.minimum(code, next_col(code)), 0.0)
    cv = jnp.minimum(code, next_row(code))
    p1, p2, prods = products(r, cu, cv, dg, rows)
    p1_ref[...] = p1[:rows]
    p2_ref[...] = p2[:rows]
    lane = iota((8, 128), 1)
    for m, prod in enumerate(prods):
        parts = [fold(prod, slice(128 * j, 128 * j + 128)) for j in range(cols // 128)]
        parts[0] = jnp.where(lane >= NEAR, parts[0], 0.0)
        parts[-1] = jnp.where(lane < 128 - NEAR, parts[-1], 0.0)
        mom_ref[8 * m : 8 * m + 8, :] = sum(parts[1:], parts[0])
    copy.wait()


def col_halo(near, far):
    east, west = pick(is_even("col"), near[...], far[...])
    left = iota(east.shape, 1) < 64

    def plane(of_east, of_west):
        return jnp.where(left, turn(east, -of_east, 1), turn(west, 124 - of_west, 1))

    return plane


def outer(rs, codes, diags, mom_in, sent_a, sent_b, near, far, r_ref, p1_ref, p2_ref, mom_ref):
    rows = rs.shape[0] - 8
    even = is_even("col")
    high, low = pick(even, sent_a[...], sent_b[...])
    east, west = pick(even, near[...], far[...])
    lane = iota(high.shape, 1)
    place = lane % 8
    own, left = place < DEEP, lane < 64
    at_east, at_west = jnp.where(own, high, east), jnp.where(own, west, low)

    def shared(op):
        minus, plus = [op(x) - x for x in (at_east, at_west)], [op(x) + x for x in (at_east, at_west)]
        return jnp.where(left, minus[0], turn(minus[1], 64, 1)), jnp.where(left, turn(plus[0], 64, 1), plus[1])

    code = jnp.where(left, turn(jnp.where(own, east, high), 4, 1), turn(jnp.where(own, low, west), 68, 1))
    level = ((lane % 64) // 8).astype(F32) + 0.5
    side = jnp.where(left, 0, 4)
    keep_u = (place + side >= 3 + side // 4) & (place + side < 7 + side // 4)
    keep_v = (place + side >= 4) & (place + side < 8)
    one, two = shared(next_col)
    ub = jnp.where((jnp.minimum(code, next_col(code)) > level) & keep_u, one, 0.0) * two
    one, two = shared(next_row)
    vb = jnp.where((jnp.minimum(code, next_row(code)) > level) & keep_v, one, 0.0) * two
    total = 0.0625 * ((ub - prev_col(ub)) + (vb - prev_row(vb)))
    for by in (8, 16, 32):
        total = total + turn(total, -by, 1)

    def filled(x, at):
        return jnp.where((lane < 60) | (lane >= 68), x, turn(came, 60 - at, 1))

    came = jnp.where(own, east, west)
    added = jnp.where((lane >= 59) & (lane < 69), jnp.where(left, turn(total, 56, 1), total), 0.0)
    r = filled(rs[...], 64) + added
    code = 0.125 * filled(codes[...], 56)
    dg = filled(diags[...], 72)
    cu, cv = jnp.minimum(code, next_col(code)), jnp.minimum(code, next_row(code))
    p1, p2, prods = products(r, cu, cv, dg, rows)
    r_ref[...] = r
    p1_ref[...] = p1
    p2_ref[...] = p2
    lane = iota((8, 128), 1)
    mine = ((lane >= 60 - NEAR) & (lane < 60)) | ((lane >= 68) & (lane < 68 + NEAR))
    packed = jnp.zeros((8, 128), F32)
    for m, prod in enumerate(prods):
        part = mom_in[8 * m : 8 * m + 8, :] + jnp.where(mine, fold(prod, slice(0, 128)), 0.0)
        for by in (4, 2, 1):
            part = part + turn(part, by, 0)
        part = ((part + turn(part, 16, 1)) + (turn(part, 32, 1) + turn(part, 48, 1))) + (
            (turn(part, 64, 1) + turn(part, 80, 1)) + (turn(part, 96, 1) + turn(part, 112, 1))
        )
        part = (part + turn(part, 4, 1)) + (turn(part, 8, 1) + turn(part, 12, 1))
        packed = jnp.where(lane // 4 == m, part, packed)
    for i in range(mom_ref.shape[0] // 8):
        mom_ref[8 * i : 8 * i + 8, :] = packed


def tracer_kernel(g_in, land_in, bottom_in, u_in, v_in, rn, rf, cn, cf, out_ref, g, land, bottom, u, v, out, sems, g_sems, out_sems):
    flat = [
        pltpu.make_async_copy(src, dst, sems.at[n])
        for n, (src, dst) in enumerate(((land_in, land), (bottom_in, bottom), (u_in, u), (v_in, v)))
    ]
    deep = [pltpu.make_async_copy(g_in.at[k], g.at[k], g_sems.at[k]) for k in range(LEV)]
    done = [pltpu.make_async_copy(out.at[k], out_ref.at[k], out_sems.at[k]) for k in range(LEV)]
    start_all(flat + deep)
    wait_all(flat)
    rows, cols = u.shape
    ch = col_halo(cn, cf)
    sub = iota((8, cols), 0)
    north, south = pick(is_even("row"), rn[...], rf[...])

    def wide(own, lanes, above, below):
        at = [8 * (x // 8) for x in (above, below)]
        halo = jnp.where(
            sub == 0,
            turn(north[at[0] : at[0] + 8], -(above % 8), 0),
            turn(south[at[1] : at[1] + 8], 7 - below % 8, 0),
        )
        return jnp.concatenate([jnp.concatenate([own, halo], axis=0), ch(*lanes)], axis=1)

    code = wide(code_of(land[...], bottom[...]), (0, 4), 20, 23)
    cu, cv = jnp.minimum(code, next_col(code)), jnp.minimum(code, next_row(code))
    uw = 0.125 * wide(u[...], (80, 84), 28, 28)
    vw = 0.125 * wide(v[...], (80, 84), 28, 28)
    for k in range(LEV):
        deep[k].wait()
        gk = wide(g[k], (8 * k + 4, 8 * k), k, k)
        pu = jnp.where(cu > k + 0.5, next_col(gk) - gk, 0.0) * uw
        pv = jnp.where(cv > k + 0.5, next_row(gk) - gk, 0.0) * vw
        total = gk + pu + prev_col(pu) + pv + prev_row(pv)
        out[k] = total[:rows, :cols]
        done[k].start()
    wait_all(done)


def two_sum(a, b):
    s = a + b
    t = s - a
    return s, (a - (s - t)) + (b - t)


def quick(a, b):
    s = a + b
    return s, b - (s - a)


def split(a):
    t = a * 4097.0
    high = t - (t - a)
    return high, a - high


def add(x, y):
    s, e = two_sum(x[0], y[0])
    return quick(s, e + (x[1] + y[1]))


def neg(x):
    return -x[0], -x[1]


def mul(x, y):
    p = x[0] * y[0]
    (ah, al), (bh, bl) = split(x[0]), split(y[0])
    e = ((ah * bh - p) + ah * bl + al * bh) + al * bl
    return quick(p, e + (x[0] * y[1] + x[1] * y[0]))


def div(x, y):
    q = x[0] / y[0]
    rest = add(x, neg(mul((q, jnp.zeros_like(q)), y)))
    return quick(q, rest[0] / y[0])


def combine(mom, r, p1, p2, rs, p1s, p2s, x_ref, x, sems):
    zero = jnp.zeros((8, 128), F32)
    tiles = [(mom[8 * i : 8 * i + 8, :], zero) for i in range(mom.shape[0] // 8)]
    while len(tiles) > 1:
        tiles = [add(tiles[i], tiles[i + 1]) for i in range(0, len(tiles), 2)]
    total = tiles[0]
    for by in (4, 2, 1):
        total = add(total, tuple(pltpu.roll(a, by, 0) for a in total))
    sums = []
    for m in range(6):
        four = [
            tuple(jnp.broadcast_to(a[:, at : at + 1], (8, 128)) for a in total)
            for at in range(4 * m, 4 * m + 4)
        ]
        sums.append(add(add(four[0], four[1]), add(four[2], four[3])))
    m00, m01, m11, m12, m22, e22 = sums
    a00, a01, a02 = add(m01, m00), add(m11, m01), add(m12, m11)
    a11, a12, a22 = a02, add(m22, m12), e22
    l10 = div(a01, a00)
    l20 = div(a02, a00)
    w11 = add(a11, neg(mul(l10, a01)))
    w12 = add(a12, neg(mul(l10, a02)))
    ok1 = w11[0] > 1e-9 * a11[0]
    l21 = tuple(jnp.where(ok1, a, 0.0) for a in div(w12, w11))
    w22 = add(add(a22, neg(mul(l20, a02))), neg(mul(l21, w12)))
    ok2 = w22[0] > 1e-9 * a22[0]
    b0 = m00
    b1 = add(m01, neg(mul(l10, b0)))
    z1 = tuple(jnp.where(ok1, a, 0.0) for a in div(b1, w11))
    b2 = add(add(m11, neg(mul(l20, b0))), neg(mul(l21, b1)))
    z2 = tuple(jnp.where(ok2, a, 0.0) for a in div(b2, w22))
    y2 = z2
    y1 = add(z1, neg(mul(l21, y2)))
    y0 = add(div(b0, a00), neg(add(mul(l10, y1), mul(l20, y2))))
    rows, cols = r.shape
    bands = sems.shape[0]
    tall = rows // bands
    done = []
    for b in range(bands):
        band = slice(b * tall, (b + 1) * tall)
        for i in range(b * tall // 8, (b + 1) * tall // 8):
            at = slice(8 * i, 8 * i + 8)
            lane = iota((8, 128), 1)
            side = y0[0] * rs[at, :] + (y1[0] * p1s[at, :] + y2[0] * p2s[at, :])
            for j in range(cols // 128):
                to = (at, slice(128 * j, 128 * j + 128))
                tile = y0[0] * r[to] + (y1[0] * p1[to] + y2[0] * p2[to])
                if j == 0:
                    tile = jnp.where(lane < NEAR, turn(side, -68, 1), tile)
                if j == cols // 128 - 1:
                    tile = jnp.where(lane >= 128 - NEAR, turn(side, 68, 1), tile)
                x[to] = tile
        done.append(pltpu.make_async_copy(x.at[band, :], x_ref.at[band, :], sems.at[b]))
        done[-1].start()
    wait_all(done)


def call(kernel, ins, outs, scratch=(), name=None, cost=None):
    run = pl.pallas_call(
        kernel,
        in_specs=list(ins),
        out_specs=[spec for spec, _ in outs],
        out_shape=[spec.memory_space(shape, F32) for spec, shape in outs],
        scratch_shapes=list(scratch),
        compiler_params=PARAMS,
        cost_estimate=cost,
        name=name,
    )
    return lambda *args: run(*[pltpu.with_memory_space_constraint(x, spec.memory_space) for x, spec in zip(args, ins)])


def shards(tracer_adj_next, tracer, u_east, v_north, surf_adj_next, diag, land, bottom):
    levels, rows, cols = tracer.shape
    size = lax.axis_size("row") * lax.axis_size("col")
    g, c = tracer_adj_next, tracer
    dma = pltpu.SemaphoreType.DMA
    two, side = (rows, cols), (rows + 8, 128)
    whole = lambda kind=F32: pltpu.VMEM(two, kind)
    edges = [pltpu.VMEM((levels, 8, cols), F32)] * 4 + [pltpu.VMEM((8, cols), jnp.int32)] * 4 + [pltpu.VMEM((8, cols), F32)] * 6
    row_a, row_b = call(
        pack_rows, [HBM] * 7, [(VMEM, (32, cols))] * 2, edges + [dma((14,))], name="pack_rows"
    )(g, c, land, bottom, surf_adj_next, diag, v_north)
    row_far = lax.ppermute(row_b, "row", swap_pairs("row", 1))
    deep = pltpu.VMEM(g.shape, F32)
    a, b, row_a = call(
        pack_cols,
        [VMEM] * 8,
        [(VMEM, (rows, 128))] * 2 + [(VMEM, (32, cols))],
        name="pack_cols",
        cost=pl.CostEstimate(flops=g.size, bytes_accessed=g.size, transcendentals=0),
    )(g, c, land, bottom, surf_adj_next, diag, u_east, row_a)
    row_near = lax.ppermute(row_a, "row", swap_pairs("row", 0))
    row_sent, row_got = (row_a, row_b), (row_near, row_far)
    rhs, code = call(
        local_rhs,
        [VMEM] * 5,
        [(VMEM, two)] * 2,
        name="local_rhs",
        cost=pl.CostEstimate(flops=24 * g.size, bytes_accessed=8 * g.size, transcendentals=0),
    )(g, c, land, bottom, surf_adj_next)
    (b,) = call(functools.partial(join_cols, False), [VMEM] * 3, [(VMEM, side)], name="join_far")(b, *row_got)
    far = lax.ppermute(b, "col", swap_pairs("col", 1))
    r, p1, p2, mom, rs, codes, diags = call(
        inner,
        [VMEM] * 7,
        [(HBM, two)] + [(VMEM, two)] * 2 + [(VMEM, (48, 128))] + [(VMEM, side)] * 3,
        [whole(), dma],
        name="inner",
        cost=pl.CostEstimate(flops=24 * g.size, bytes_accessed=8 * g.size, transcendentals=0),
    )(rhs, code, diag, *row_sent, *row_got)
    (a,) = call(functools.partial(join_cols, True), [VMEM] * 4, [(VMEM, side)], name="join_near")(a, *row_got, rs)
    near = lax.ppermute(a, "col", swap_pairs("col", 0))
    col_sent, col_got = (a, b), (near, far)
    *sides, mom = call(outer, [VMEM] * 8, [(VMEM, side)] * 3 + [(VMEM, (size, 128))], name="outer")(
        rs, codes, diags, mom, *col_sent, *col_got
    )
    mom = lax.all_to_all(mom, ("row", "col"), 0, 0, tiled=True)
    (tracer_adj,) = call(
        tracer_kernel,
        [HBM] * 5 + [VMEM] * 4,
        [(HBM, g.shape)],
        [deep, whole(jnp.int32), whole(jnp.int32), whole(), whole(), deep, dma((4,)), dma((levels,)), dma((levels,))],
        name="tracer",
        cost=pl.CostEstimate(flops=20 * g.size, bytes_accessed=12 * g.size, transcendentals=0),
    )(g, land, bottom, u_east, v_north, *row_got, *col_got)
    (surf_adj,) = call(
        combine,
        [VMEM] * 7,
        [(HBM, two)],
        [whole(), dma((2,))],
        name="combine",
    )(mom, r, p1, p2, *sides)
    return tracer_adj, surf_adj


def solution(mesh):
    three, two = P(None, "row", "col"), P("row", "col")
    return jax.shard_map(
        shards,
        mesh=mesh,
        in_specs=(three, three, two, two, two, two, two, two),
        out_specs=(three, two),
        check_vma=False,
    )
```

```python
import functools

import jax
import jax.numpy as jnp
from jax import lax
from jax.experimental import pallas as pl
from jax.experimental.pallas import tpu as pltpu
from jax.sharding import PartitionSpec as P

LEV = 8
DEEP = 4
NEAR = 32
SHIFT = 1.0
F32 = jnp.float32
VMEM = pl.BlockSpec(memory_space=pltpu.VMEM)
HBM = pl.BlockSpec(memory_space=pltpu.HBM)
PARAMS = pltpu.CompilerParams(vmem_limit_bytes=32 * 1024 * 1024)


G, C, RHS, CODE, DIAG = 0, 1, 4, 5, 6


def code_of(land, bottom):
    return jnp.where(land == 1, bottom, 0).astype(F32)


def swap_pairs(axis, first):
    count = lax.axis_size(axis)
    pairs = []
    for low in range(first, count - 1, 2):
        pairs += [(low, low + 1), (low + 1, low)]
    return pairs


def is_even(axis):
    return lax.rem(lax.axis_index(axis), 2) == 0


def iota(shape, dim):
    return lax.broadcasted_iota(jnp.int32, shape, dim)


def turn(x, by, dim):
    by = by % x.shape[dim]
    return pltpu.roll(x, by, dim) if by else x


def next_col(a):
    return turn(a, -1, 1)


def prev_col(a):
    return turn(a, 1, 1)


def next_row(a):
    return turn(a, -1, 0)


def prev_row(a):
    return turn(a, 1, 0)


def pick(even, one, two):
    return jnp.where(even, one, two), jnp.where(even, two, one)


def start_all(copies):
    for copy in copies:
        copy.start()


def wait_all(copies):
    for copy in copies:
        copy.wait()


def pack_rows(g, c, land, bottom, surf, diag, v, a_ref, b_ref, g0, g1, c0, c1, l0, l1, b0, b1, s0, s1, d0, d1, v0, v1, sems):
    rows = surf.shape[0]
    copies = []
    for src, low, high in ((g, g0, g1), (c, c0, c1), (land, l0, l1), (bottom, b0, b1), (surf, s0, s1), (diag, d0, d1), (v, v0, v1)):
        for dst, at in ((low, slice(0, 8)), (high, slice(rows - 8, rows))):
            part = src.at[:, at, :] if len(src.shape) == 3 else src.at[at, :]
            copies.append(pltpu.make_async_copy(part, dst, sems.at[len(copies)]))
    start_all(copies)
    wait_all(copies)

    cols = surf.shape[1]
    lane, sub = iota((8, cols), 1), iota((8, cols), 0)
    upper = sub < DEEP
    codes = [code_of(l0[...], b0[...]), code_of(l1[...], b1[...])]
    both = [jnp.where(upper, g0[k], g1[k]) for k in range(LEV)], [jnp.where(upper, c0[k], c1[k]) for k in range(LEV)]
    code = jnp.where(upper, *codes)
    cu = jnp.where(lane < cols - 1, jnp.minimum(code, next_col(code)), 0.0)
    ub = faces(*both, cu, next_col)
    ub = ub - prev_col(ub)
    cut = lambda x: [x[:, :128], x[:, cols - 128 :]]
    rest = [jnp.where(upper, s0[...], s1[...]), jnp.where(upper, d0[...], d1[...])]
    corners = lane_packs([cut(x) for x in both[0]], [cut(x) for x in both[1]], cut(code), [cut(x) for x in rest])

    def tiles(g, c, code, surf, diag, v, of_last):
        g, c = [g[k] for k in range(LEV)], [c[k] for k in range(LEV)]
        cv = jnp.where(sub < 7, jnp.minimum(code, next_row(code)), 0.0)
        vb = faces(g, c, cv, next_row)
        rhs = surf[...] + 0.0625 * (ub + (vb - prev_row(vb)))
        edge = 7 if of_last else 0

        def outermost(x):
            out = turn(x[0], -edge, 0)
            for k in range(1, LEV):
                out = jnp.where(sub == k, turn(x[k], k - edge, 0), out)
            return out

        half = DEEP if of_last else 0
        one = jnp.where(upper, turn(rhs, half, 0), turn(code, DEEP - half, 0))
        two = jnp.where(upper, turn(diag[...], half, 0), turn(v[...], DEEP - edge, 0))
        ends = [
            jnp.where(sub[:, :128] < 5, two[:, lanes], corner if of_last else turn(corner, 5, 0))
            for corner, lanes in zip(corners, (slice(0, 128), slice(cols - 128, cols)))
        ]
        two = jnp.concatenate([ends[0], two[:, 128 : cols - 128], ends[1]], axis=1)
        return outermost(g), outermost(c), one, two

    first = tiles(g0, c0, codes[0], s0, d0, v0, False)
    last = tiles(g1, c1, codes[1], s1, d1, v1, True)
    even = is_even("row")
    for t in range(4):
        a_ref[8 * t : 8 * t + 8, :], b_ref[8 * t : 8 * t + 8, :] = pick(even, last[t], first[t])


def faces(g, c, coupling, step):
    total = jnp.zeros_like(coupling)
    for k in range(LEV):
        gk, ck = g[k], c[k]
        total = total + jnp.where(coupling > k + 0.5, step(gk) - gk, 0.0) * (step(ck) + ck)
    return total


def operator(cu, cv, dg):
    west, south = prev_col(cu), prev_row(cv)
    center = (dg - SHIFT) + ((cu + west) + (cv + south))

    def shifted(v):
        sides = (cu * next_col(v) + west * prev_col(v)) + (cv * next_row(v) + south * prev_row(v))
        return center * v - sides

    return shifted


def products(r, cu, cv, dg, rows):
    shifted = operator(cu, cv, dg)
    p1 = shifted(r)
    p2 = shifted(p1)
    eu, ev = p2 - next_col(p2), p2 - next_row(p2)
    energy = dg * p2 * p2 + (cu * eu * eu + cv * ev * ev)
    q, p, o = r[:rows], p1[:rows], p2[:rows]
    return p1, p2, (q * q, q * p, p * p, p * o, o * o, energy[:rows])


def fold(prod, lanes):
    tiles = [prod[8 * i : 8 * i + 8, lanes] for i in range(prod.shape[0] // 8)]
    while len(tiles) > 1:
        tiles = [sum(tiles[i : i + 2][1:], tiles[i]) for i in range(0, len(tiles), 2)]
    return tiles[0]


def lane_packs(g, c, code, rest):
    lane = iota(code[0].shape, 1)
    group, left, own = lane // DEEP, lane < 64, lane % 8 < DEEP
    one = jnp.zeros_like(code[0])
    for k in range(LEV):
        for (first, last), at in ((g[k], 8 * k), (c[k], 64 + 8 * k)):
            one = jnp.where(lane // 8 == at // 8, turn(jnp.where(left, first, last), at + DEEP, 1), one)
    two = jnp.where(group == 0, code[0], jnp.where(group == 1, turn(code[1], 8, 1), 0.0))
    for by in (8, 16, 32):
        two = two + turn(two, by, 1)
    two = jnp.where(group == 31, code[1], two)
    for n, (first, last) in enumerate(rest):
        two = jnp.where(group == 16 + 2 * n, turn(first, 64 + 8 * n, 1), two)
        two = jnp.where(group == 17 + 2 * n, turn(last, 72 + 8 * n, 1), two)
    return jnp.where(own, two, one), jnp.where(own, one, two)


def pack_cols(g, c, land, bottom, surf, diag, u, row_in, a_ref, b_ref, row_ref):
    row_ref[...] = row_in[...]
    cols = surf.shape[1]
    ends = slice(0, 128), slice(cols - 128, cols)
    low, high = lane_packs(
        [[g[k, :, lanes] for lanes in ends] for k in range(LEV)],
        [[c[k, :, lanes] for lanes in ends] for k in range(LEV)],
        [code_of(land[:, lanes], bottom[:, lanes]) for lanes in ends],
        [[x[:, lanes] for lanes in ends] for x in (surf, diag, u)],
    )
    a_ref[...], b_ref[...] = pick(is_even("col"), high, low)


def row_halo(near, far, lanes):
    even = is_even("row")

    def plane(p):
        at = slice(8 * (p // 2), 8 * (p // 2) + 8)
        north, south = pick(even, near[at, lanes], far[at, lanes])
        upper = iota(north.shape, 0) < DEEP
        if p % 2 == 0:
            return jnp.where(upper, north, turn(south, DEEP, 0))
        return jnp.where(upper, turn(north, DEEP, 0), south)

    return plane


def join_cols(of_near, own, near, far, *refs):
    rows, width = own.shape[0], near.shape[1]
    out = refs[-1]
    even = is_even("row")
    packs = []
    for lanes in (slice(width - 128, width), slice(0, 128)):
        north, south = pick(even, near[24:, lanes], far[24:, lanes])
        sub = iota(north.shape, 0)
        packs.append(jnp.where(sub < 3, turn(north, -5, 0), jnp.where(sub < 5, 0.0, south)))
    out[:rows, :] = own[...]
    out[rows:, :] = pick(is_even("col"), *packs)[0 if of_near else 1]


def local_rhs(g, c, land, bottom, surf, r_ref, code_ref):
    rows, cols = surf.shape
    code = code_of(land[...], bottom[...])
    code_ref[...] = code
    cu = jnp.where(iota(code.shape, 1) < cols - 1, jnp.minimum(code, next_col(code)), 0.0)
    cv = jnp.where(iota(code.shape, 0) < rows - 1, jnp.minimum(code, next_row(code)), 0.0)
    ub, vb = faces(g, c, cu, next_col), faces(g, c, cv, next_row)
    r_ref[...] = surf[...] + 0.0625 * ((ub - prev_col(ub)) + (vb - prev_row(vb)))


def inner(r_in, code_in, diag, sent_a, sent_b, near, far, r_ref, p1_ref, p2_ref, mom_ref, rs_ref, codes_ref, diags_ref, r_own, sem):
    rows, cols = diag.shape
    even = is_even("row")
    lane, sub = iota((8, cols), 1), iota((8, cols), 0)
    high, low = pick(even, sent_a[...], sent_b[...])
    north, south = pick(even, near[...], far[...])

    def across(below, above, here, there):
        pair = [x[16 + at : 17 + at, :] for x, at in ((below, here), (above, there))]
        open_v = jnp.minimum(*pair) > sub.astype(F32) + 0.5
        total = jnp.where(open_v, above[:8] - below[:8], 0.0) * (above[8:16] + below[8:16])
        for by in (4, 2, 1):
            total = total + turn(total, by, 0)
        return 0.0625 * total

    up = across(high, north, 7, 4)
    down = across(south, low, 7, 4)
    halo = row_halo(near, far, slice(0, cols))
    r_halo = halo(RHS) + jnp.where(sub == 0, -up, jnp.where(sub == 7, down, 0.0))
    low = r_in[:8] - jnp.where(sub == 0, down, 0.0)
    high = r_in[rows - 8 :] + jnp.where(sub == 7, up, 0.0)
    r = jnp.concatenate([low, r_in[8 : rows - 8], high, r_halo], axis=0)
    r_own[...] = r[:rows]
    copy = pltpu.make_async_copy(r_own, r_ref, sem)
    copy.start()
    code = jnp.concatenate([code_in[...], halo(CODE)], axis=0)
    dg = jnp.concatenate([diag[...], halo(DIAG)], axis=0)
    left = iota((rows + 8, 128), 1) < 64
    for x, ref in ((r, rs_ref), (code, codes_ref), (dg, diags_ref)):
        ref[...] = jnp.where(left, turn(x[:, cols - 128 :], -68, 1), turn(x[:, :128], 68, 1))
    code = 0.125 * code
    cu = jnp.where(iota(code.shape, 1) < cols - 1, jnp.minimum(code, next_col(code)), 0.0)
    cv = jnp.minimum(code, next_row(code))
    p1, p2, prods = products(r, cu, cv, dg, rows)
    p1_ref[...] = p1[:rows]
    p2_ref[...] = p2[:rows]
    lane = iota((8, 128), 1)
    for m, prod in enumerate(prods):
        parts = [fold(prod, slice(128 * j, 128 * j + 128)) for j in range(cols // 128)]
        parts[0] = jnp.where(lane >= NEAR, parts[0], 0.0)
        parts[-1] = jnp.where(lane < 128 - NEAR, parts[-1], 0.0)
        mom_ref[8 * m : 8 * m + 8, :] = sum(parts[1:], parts[0])
    copy.wait()


def col_halo(near, far):
    east, west = pick(is_even("col"), near[...], far[...])
    left = iota(east.shape, 1) < 64

    def plane(of_east, of_west):
        return jnp.where(left, turn(east, -of_east, 1), turn(west, 124 - of_west, 1))

    return plane


def outer(rs, codes, diags, mom_in, sent_a, sent_b, near, far, r_ref, p1_ref, p2_ref, mom_ref):
    rows = rs.shape[0] - 8
    even = is_even("col")
    high, low = pick(even, sent_a[...], sent_b[...])
    east, west = pick(even, near[...], far[...])
    lane = iota(high.shape, 1)
    place = lane % 8
    own, left = place < DEEP, lane < 64
    at_east, at_west = jnp.where(own, high, east), jnp.where(own, west, low)

    def shared(op):
        minus, plus = [op(x) - x for x in (at_east, at_west)], [op(x) + x for x in (at_east, at_west)]
        return jnp.where(left, minus[0], turn(minus[1], 64, 1)), jnp.where(left, turn(plus[0], 64, 1), plus[1])

    code = jnp.where(left, turn(jnp.where(own, east, high), 4, 1), turn(jnp.where(own, low, west), 68, 1))
    level = ((lane % 64) // 8).astype(F32) + 0.5
    side = jnp.where(left, 0, 4)
    keep_u = (place + side >= 3 + side // 4) & (place + side < 7 + side // 4)
    keep_v = (place + side >= 4) & (place + side < 8)
    one, two = shared(next_col)
    ub = jnp.where((jnp.minimum(code, next_col(code)) > level) & keep_u, one, 0.0) * two
    one, two = shared(next_row)
    vb = jnp.where((jnp.minimum(code, next_row(code)) > level) & keep_v, one, 0.0) * two
    total = 0.0625 * ((ub - prev_col(ub)) + (vb - prev_row(vb)))
    for by in (8, 16, 32):
        total = total + turn(total, -by, 1)

    def filled(x, at):
        return jnp.where((lane < 60) | (lane >= 68), x, turn(came, 60 - at, 1))

    came = jnp.where(own, east, west)
    added = jnp.where((lane >= 59) & (lane < 69), jnp.where(left, turn(total, 56, 1), total), 0.0)
    r = filled(rs[...], 64) + added
    code = 0.125 * filled(codes[...], 56)
    dg = filled(diags[...], 72)
    cu, cv = jnp.minimum(code, next_col(code)), jnp.minimum(code, next_row(code))
    p1, p2, prods = products(r, cu, cv, dg, rows)
    r_ref[...] = r
    p1_ref[...] = p1
    p2_ref[...] = p2
    lane = iota((8, 128), 1)
    mine = ((lane >= 60 - NEAR) & (lane < 60)) | ((lane >= 68) & (lane < 68 + NEAR))
    sub = iota((8, 128), 0)
    sums = jnp.zeros((8, 128), F32)
    for m, prod in enumerate(prods):
        part = mom_in[8 * m : 8 * m + 8, :] + jnp.where(mine, fold(prod, slice(0, 128)), 0.0)
        for by in (4, 2, 1):
            part = part + turn(part, by, 0)
        sums = jnp.where(sub == m, part, sums)
    sums = ((sums + turn(sums, 16, 1)) + (turn(sums, 32, 1) + turn(sums, 48, 1))) + (
        (turn(sums, 64, 1) + turn(sums, 80, 1)) + (turn(sums, 96, 1) + turn(sums, 112, 1))
    )
    sums = (sums + turn(sums, 4, 1)) + (turn(sums, 8, 1) + turn(sums, 12, 1))
    packed = jnp.zeros((8, 128), F32)
    for m in range(len(prods)):
        packed = jnp.where(lane // 4 == m, jnp.broadcast_to(sums[m : m + 1, :], (8, 128)), packed)
    for i in range(mom_ref.shape[0] // 8):
        mom_ref[8 * i : 8 * i + 8, :] = packed


def tracer_kernel(g_in, land_in, bottom_in, u_in, v_in, rn, rf, cn, cf, out_ref, g, land, bottom, u, v, out, sems, g_sems, out_sems):
    flat = [
        pltpu.make_async_copy(src, dst, sems.at[n])
        for n, (src, dst) in enumerate(((land_in, land), (bottom_in, bottom), (u_in, u), (v_in, v)))
    ]
    deep = [pltpu.make_async_copy(g_in.at[k], g.at[k], g_sems.at[k]) for k in range(LEV)]
    done = [pltpu.make_async_copy(out.at[k], out_ref.at[k], out_sems.at[k]) for k in range(LEV)]
    start_all(flat + deep)
    wait_all(flat)
    rows, cols = u.shape
    ch = col_halo(cn, cf)
    sub = iota((8, cols), 0)
    north, south = pick(is_even("row"), rn[...], rf[...])

    def wide(own, lanes, above, below):
        at = [8 * (x // 8) for x in (above, below)]
        halo = jnp.where(
            sub == 0,
            turn(north[at[0] : at[0] + 8], -(above % 8), 0),
            turn(south[at[1] : at[1] + 8], 7 - below % 8, 0),
        )
        return jnp.concatenate([jnp.concatenate([own, halo], axis=0), ch(*lanes)], axis=1)

    code = wide(code_of(land[...], bottom[...]), (0, 4), 20, 23)
    cu, cv = jnp.minimum(code, next_col(code)), jnp.minimum(code, next_row(code))
    uw = 0.125 * wide(u[...], (80, 84), 28, 28)
    vw = 0.125 * wide(v[...], (80, 84), 28, 28)
    for k in range(LEV):
        deep[k].wait()
        gk = wide(g[k], (8 * k + 4, 8 * k), k, k)
        pu = jnp.where(cu > k + 0.5, next_col(gk) - gk, 0.0) * uw
        pv = jnp.where(cv > k + 0.5, next_row(gk) - gk, 0.0) * vw
        total = gk + pu + prev_col(pu) + pv + prev_row(pv)
        out[k] = total[:rows, :cols]
        done[k].start()
    wait_all(done)


def two_sum(a, b):
    s = a + b
    t = s - a
    return s, (a - (s - t)) + (b - t)


def quick(a, b):
    s = a + b
    return s, b - (s - a)


def split(a):
    t = a * 4097.0
    high = t - (t - a)
    return high, a - high


def add(x, y):
    s, e = two_sum(x[0], y[0])
    return quick(s, e + (x[1] + y[1]))


def neg(x):
    return -x[0], -x[1]


def mul(x, y):
    p = x[0] * y[0]
    (ah, al), (bh, bl) = split(x[0]), split(y[0])
    e = ((ah * bh - p) + ah * bl + al * bh) + al * bl
    return quick(p, e + (x[0] * y[1] + x[1] * y[0]))


def div(x, y):
    q = x[0] / y[0]
    rest = add(x, neg(mul((q, jnp.zeros_like(q)), y)))
    return quick(q, rest[0] / y[0])


def combine(mom, r, p1, p2, rs, p1s, p2s, x_ref, x, sems):
    zero = jnp.zeros((8, 128), F32)
    tiles = [(mom[8 * i : 8 * i + 8, :], zero) for i in range(mom.shape[0] // 8)]
    while len(tiles) > 1:
        tiles = [add(tiles[i], tiles[i + 1]) for i in range(0, len(tiles), 2)]
    total = tiles[0]
    for by in (4, 2, 1):
        total = add(total, tuple(pltpu.roll(a, by, 0) for a in total))
    sums = []
    for m in range(6):
        four = [
            tuple(jnp.broadcast_to(a[:, at : at + 1], (8, 128)) for a in total)
            for at in range(4 * m, 4 * m + 4)
        ]
        sums.append(add(add(four[0], four[1]), add(four[2], four[3])))
    m00, m01, m11, m12, m22, e22 = sums
    a00, a01, a02 = add(m01, m00), add(m11, m01), add(m12, m11)
    a11, a12, a22 = a02, add(m22, m12), e22
    l10 = div(a01, a00)
    l20 = div(a02, a00)
    w11 = add(a11, neg(mul(l10, a01)))
    w12 = add(a12, neg(mul(l10, a02)))
    ok1 = w11[0] > 1e-9 * a11[0]
    l21 = tuple(jnp.where(ok1, a, 0.0) for a in div(w12, w11))
    w22 = add(add(a22, neg(mul(l20, a02))), neg(mul(l21, w12)))
    ok2 = w22[0] > 1e-9 * a22[0]
    b0 = m00
    b1 = add(m01, neg(mul(l10, b0)))
    z1 = tuple(jnp.where(ok1, a, 0.0) for a in div(b1, w11))
    b2 = add(add(m11, neg(mul(l20, b0))), neg(mul(l21, b1)))
    z2 = tuple(jnp.where(ok2, a, 0.0) for a in div(b2, w22))
    y2 = z2
    y1 = add(z1, neg(mul(l21, y2)))
    y0 = add(div(b0, a00), neg(add(mul(l10, y1), mul(l20, y2))))
    rows, cols = r.shape
    bands = sems.shape[0]
    tall = rows // bands
    done = []
    for b in range(bands):
        band = slice(b * tall, (b + 1) * tall)
        for i in range(b * tall // 8, (b + 1) * tall // 8):
            at = slice(8 * i, 8 * i + 8)
            lane = iota((8, 128), 1)
            side = y0[0] * rs[at, :] + (y1[0] * p1s[at, :] + y2[0] * p2s[at, :])
            for j in range(cols // 128):
                to = (at, slice(128 * j, 128 * j + 128))
                tile = y0[0] * r[to] + (y1[0] * p1[to] + y2[0] * p2[to])
                if j == 0:
                    tile = jnp.where(lane < NEAR, turn(side, -68, 1), tile)
                if j == cols // 128 - 1:
                    tile = jnp.where(lane >= 128 - NEAR, turn(side, 68, 1), tile)
                x[to] = tile
        done.append(pltpu.make_async_copy(x.at[band, :], x_ref.at[band, :], sems.at[b]))
        done[-1].start()
    wait_all(done)


def call(kernel, ins, outs, scratch=(), name=None, cost=None):
    run = pl.pallas_call(
        kernel,
        in_specs=list(ins),
        out_specs=[spec for spec, _ in outs],
        out_shape=[spec.memory_space(shape, F32) for spec, shape in outs],
        scratch_shapes=list(scratch),
        compiler_params=PARAMS,
        cost_estimate=cost,
        name=name,
    )
    return lambda *args: run(*[pltpu.with_memory_space_constraint(x, spec.memory_space) for x, spec in zip(args, ins)])


def shards(tracer_adj_next, tracer, u_east, v_north, surf_adj_next, diag, land, bottom):
    levels, rows, cols = tracer.shape
    size = lax.axis_size("row") * lax.axis_size("col")
    g, c = tracer_adj_next, tracer
    dma = pltpu.SemaphoreType.DMA
    two, side = (rows, cols), (rows + 8, 128)
    whole = lambda kind=F32: pltpu.VMEM(two, kind)
    edges = [pltpu.VMEM((levels, 8, cols), F32)] * 4 + [pltpu.VMEM((8, cols), jnp.int32)] * 4 + [pltpu.VMEM((8, cols), F32)] * 6
    row_a, row_b = call(
        pack_rows, [HBM] * 7, [(VMEM, (32, cols))] * 2, edges + [dma((14,))], name="pack_rows"
    )(g, c, land, bottom, surf_adj_next, diag, v_north)
    row_far = lax.ppermute(row_b, "row", swap_pairs("row", 1))
    deep = pltpu.VMEM(g.shape, F32)
    a, b, row_a = call(
        pack_cols,
        [VMEM] * 8,
        [(VMEM, (rows, 128))] * 2 + [(VMEM, (32, cols))],
        name="pack_cols",
        cost=pl.CostEstimate(flops=g.size, bytes_accessed=g.size, transcendentals=0),
    )(g, c, land, bottom, surf_adj_next, diag, u_east, row_a)
    row_near = lax.ppermute(row_a, "row", swap_pairs("row", 0))
    row_sent, row_got = (row_a, row_b), (row_near, row_far)
    rhs, code = call(
        local_rhs,
        [VMEM] * 5,
        [(VMEM, two)] * 2,
        name="local_rhs",
        cost=pl.CostEstimate(flops=24 * g.size, bytes_accessed=8 * g.size, transcendentals=0),
    )(g, c, land, bottom, surf_adj_next)
    (b,) = call(functools.partial(join_cols, False), [VMEM] * 3, [(VMEM, side)], name="join_far")(b, *row_got)
    far = lax.ppermute(b, "col", swap_pairs("col", 1))
    r, p1, p2, mom, rs, codes, diags = call(
        inner,
        [VMEM] * 7,
        [(HBM, two)] + [(VMEM, two)] * 2 + [(VMEM, (48, 128))] + [(VMEM, side)] * 3,
        [whole(), dma],
        name="inner",
        cost=pl.CostEstimate(flops=24 * g.size, bytes_accessed=8 * g.size, transcendentals=0),
    )(rhs, code, diag, *row_sent, *row_got)
    (a,) = call(functools.partial(join_cols, True), [VMEM] * 4, [(VMEM, side)], name="join_near")(a, *row_got, rs)
    near = lax.ppermute(a, "col", swap_pairs("col", 0))
    col_sent, col_got = (a, b), (near, far)
    *sides, mom = call(outer, [VMEM] * 8, [(VMEM, side)] * 3 + [(VMEM, (size, 128))], name="outer")(
        rs, codes, diags, mom, *col_sent, *col_got
    )
    mom = lax.all_to_all(mom, ("row", "col"), 0, 0, tiled=True)
    (tracer_adj,) = call(
        tracer_kernel,
        [HBM] * 5 + [VMEM] * 4,
        [(HBM, g.shape)],
        [deep, whole(jnp.int32), whole(jnp.int32), whole(), whole(), deep, dma((4,)), dma((levels,)), dma((levels,))],
        name="tracer",
        cost=pl.CostEstimate(flops=20 * g.size, bytes_accessed=12 * g.size, transcendentals=0),
    )(g, land, bottom, u_east, v_north, *row_got, *col_got)
    (surf_adj,) = call(
        combine,
        [VMEM] * 7,
        [(HBM, two)],
        [whole(), dma((2,))],
        name="combine",
    )(mom, r, p1, p2, *sides)
    return tracer_adj, surf_adj


def solution(mesh):
    three, two = P(None, "row", "col"), P("row", "col")
    return jax.shard_map(
        shards,
        mesh=mesh,
        in_specs=(three, three, two, two, two, two, two, two),
        out_specs=(three, two),
        check_vma=False,
    )
```

```python
import functools

import jax
import jax.numpy as jnp
from jax import lax
from jax.experimental import pallas as pl
from jax.experimental.pallas import tpu as pltpu
from jax.sharding import PartitionSpec as P

LEV = 8
DEEP = 4
NEAR = 32
SHIFT = 1.0
F32 = jnp.float32
VMEM = pl.BlockSpec(memory_space=pltpu.VMEM)
HBM = pl.BlockSpec(memory_space=pltpu.HBM)
PARAMS = pltpu.CompilerParams(vmem_limit_bytes=32 * 1024 * 1024)


G, C, RHS, CODE, DIAG = 0, 1, 4, 5, 6


def code_of(land, bottom):
    return jnp.where(land == 1, bottom, 0).astype(F32)


def swap_pairs(axis, first):
    count = lax.axis_size(axis)
    pairs = []
    for low in range(first, count - 1, 2):
        pairs += [(low, low + 1), (low + 1, low)]
    return pairs


def is_even(axis):
    return lax.rem(lax.axis_index(axis), 2) == 0


def iota(shape, dim):
    return lax.broadcasted_iota(jnp.int32, shape, dim)


def turn(x, by, dim):
    by = by % x.shape[dim]
    return pltpu.roll(x, by, dim) if by else x


def next_col(a):
    return turn(a, -1, 1)


def prev_col(a):
    return turn(a, 1, 1)


def next_row(a):
    return turn(a, -1, 0)


def prev_row(a):
    return turn(a, 1, 0)


def pick(even, one, two):
    return jnp.where(even, one, two), jnp.where(even, two, one)


def start_all(copies):
    for copy in copies:
        copy.start()


def wait_all(copies):
    for copy in copies:
        copy.wait()


def pack_rows(g, c, land, bottom, surf, diag, v, a_ref, b_ref, g0, g1, c0, c1, l0, l1, b0, b1, s0, s1, d0, d1, v0, v1, sems):
    rows = surf.shape[0]
    copies = []
    for src, low, high in ((g, g0, g1), (c, c0, c1), (land, l0, l1), (bottom, b0, b1), (surf, s0, s1), (diag, d0, d1), (v, v0, v1)):
        for dst, at in ((low, slice(0, 8)), (high, slice(rows - 8, rows))):
            part = src.at[:, at, :] if len(src.shape) == 3 else src.at[at, :]
            copies.append(pltpu.make_async_copy(part, dst, sems.at[len(copies)]))
    start_all(copies)
    wait_all(copies)

    cols = surf.shape[1]
    lane, sub = iota((8, cols), 1), iota((8, cols), 0)
    upper = sub < DEEP
    codes = [code_of(l0[...], b0[...]), code_of(l1[...], b1[...])]
    both = [jnp.where(upper, g0[k], g1[k]) for k in range(LEV)], [jnp.where(upper, c0[k], c1[k]) for k in range(LEV)]
    code = jnp.where(upper, *codes)
    cu = jnp.where(lane < cols - 1, jnp.minimum(code, next_col(code)), 0.0)
    ub = faces(*both, cu, next_col)
    ub = ub - prev_col(ub)
    cut = lambda x: [x[:, :128], x[:, cols - 128 :]]
    diags = jnp.where(upper, d0[...], d1[...])
    corners = lane_packs([cut(x) for x in both[0]], [cut(x) for x in both[1]], cut(code), cut(diags))

    def tiles(g, c, code, surf, diag, v, of_last):
        g, c = [g[k] for k in range(LEV)], [c[k] for k in range(LEV)]
        cv = jnp.where(sub < 7, jnp.minimum(code, next_row(code)), 0.0)
        vb = faces(g, c, cv, next_row)
        rhs = surf[...] + 0.0625 * (ub + (vb - prev_row(vb)))
        edge = 7 if of_last else 0

        def outermost(x):
            out = turn(x[0], -edge, 0)
            for k in range(1, LEV):
                out = jnp.where(sub == k, turn(x[k], k - edge, 0), out)
            return out

        half = DEEP if of_last else 0
        one = jnp.where(upper, turn(rhs, half, 0), turn(code, DEEP - half, 0))
        two = jnp.where(upper, turn(diag[...], half, 0), turn(v[...], DEEP - edge, 0))
        ends = [
            jnp.where(sub[:, :128] < 5, two[:, lanes], corner if of_last else turn(corner, 5, 0))
            for corner, lanes in zip(corners, (slice(0, 128), slice(cols - 128, cols)))
        ]
        two = jnp.concatenate([ends[0], two[:, 128 : cols - 128], ends[1]], axis=1)
        return outermost(g), outermost(c), one, two

    first = tiles(g0, c0, codes[0], s0, d0, v0, False)
    last = tiles(g1, c1, codes[1], s1, d1, v1, True)
    even = is_even("row")
    for t in range(4):
        a_ref[8 * t : 8 * t + 8, :], b_ref[8 * t : 8 * t + 8, :] = pick(even, last[t], first[t])


def faces(g, c, coupling, step):
    total = jnp.zeros_like(coupling)
    for k in range(LEV):
        gk, ck = g[k], c[k]
        total = total + jnp.where(coupling > k + 0.5, step(gk) - gk, 0.0) * (step(ck) + ck)
    return total


def operator(cu, cv, dg):
    west, south = prev_col(cu), prev_row(cv)
    center = (dg - SHIFT) + ((cu + west) + (cv + south))

    def shifted(v):
        sides = (cu * next_col(v) + west * prev_col(v)) + (cv * next_row(v) + south * prev_row(v))
        return center * v - sides

    return shifted


def products(r, cu, cv, dg, rows):
    shifted = operator(cu, cv, dg)
    p1 = shifted(r)
    p2 = shifted(p1)
    eu, ev = p2 - next_col(p2), p2 - next_row(p2)
    energy = dg * p2 * p2 + (cu * eu * eu + cv * ev * ev)
    q, p, o = r[:rows], p1[:rows], p2[:rows]
    return p1, p2, (q * q, q * p, p * p, p * o, o * o, energy[:rows])


def fold(prod, lanes):
    tiles = [prod[8 * i : 8 * i + 8, lanes] for i in range(prod.shape[0] // 8)]
    while len(tiles) > 1:
        tiles = [sum(tiles[i : i + 2][1:], tiles[i]) for i in range(0, len(tiles), 2)]
    return tiles[0]


def lane_packs(g, c, code, diag, u=None):
    lane = iota(code[0].shape, 1)
    packs = []
    for end, edge in ((0, 0), (1, 127)):
        out = jnp.where(lane == 16, turn(code[end], 16 - edge, 1), 0.0)
        for by in (1, 2, 4):
            out = out + turn(out, by, 1)
        places = [(g[k], edge, k, 1) for k in range(LEV)] + [(c[k], edge, 8 + k, 1) for k in range(LEV)]
        places += [(code, 125, 24, 2), (diag, 126, 29, 2)] if end else [(code, 1, 24, 2), (diag, 0, 26, 2)]
        if end and u is not None:
            places.append((u, 127, 31, 1))
        for x, at, to, width in places:
            out = jnp.where((lane >= to) & (lane < to + width), turn(x[end], to - at, 1), out)
        packs.append(out)
    return packs


def pack_cols(g, c, land, bottom, surf, diag, u, row_in, a_ref, b_ref, row_ref):
    row_ref[...] = row_in[...]
    cols = surf.shape[1]
    ends = slice(0, 128), slice(cols - 128, cols)
    low, high = lane_packs(
        [[g[k, :, lanes] for lanes in ends] for k in range(LEV)],
        [[c[k, :, lanes] for lanes in ends] for k in range(LEV)],
        [code_of(land[:, lanes], bottom[:, lanes]) for lanes in ends],
        *[[x[:, lanes] for lanes in ends] for x in (diag, u)],
    )
    a_ref[...], b_ref[...] = pick(is_even("col"), high, low)


def row_halo(near, far, lanes):
    even = is_even("row")

    def plane(p):
        at = slice(8 * (p // 2), 8 * (p // 2) + 8)
        north, south = pick(even, near[at, lanes], far[at, lanes])
        upper = iota(north.shape, 0) < DEEP
        if p % 2 == 0:
            return jnp.where(upper, north, turn(south, DEEP, 0))
        return jnp.where(upper, turn(north, DEEP, 0), south)

    return plane


def with_rows(r, sent_a, sent_b, near, far, lanes):
    rows = r.shape[0]
    even = is_even("row")
    high, low = pick(even, sent_a[:, lanes], sent_b[:, lanes])
    north, south = pick(even, near[:, lanes], far[:, lanes])
    sub = iota((8, r.shape[1]), 0)

    def across(below, above):
        open_v = jnp.minimum(below[23:24], above[20:21]) > sub.astype(F32) + 0.5
        total = jnp.where(open_v, above[:8] - below[:8], 0.0) * (above[8:16] + below[8:16])
        for by in (4, 2, 1):
            total = total + turn(total, by, 0)
        return 0.0625 * total

    up, down = across(high, north), across(south, low)
    halo = row_halo(near, far, lanes)(RHS) + jnp.where(sub == 0, -up, jnp.where(sub == 7, down, 0.0))
    first = r[:8] - jnp.where(sub == 0, down, 0.0)
    last = r[rows - 8 :] + jnp.where(sub == 7, up, 0.0)
    return jnp.concatenate([first, r[8 : rows - 8], last, halo], axis=0)


def join_cols(of_near, own, r, sent_a, sent_b, near, far, *refs):
    rows, width = r.shape
    out = refs[-1]
    north, south = pick(is_even("row"), near[24:, :], far[24:, :])
    sub = iota((8, 128), 0)
    halos, sides = [], []
    for lanes in (slice(width - 128, width), slice(0, 128)):
        halos.append(jnp.where(sub < 3, turn(north[:, lanes], -5, 0), jnp.where(sub < 5, 0.0, south[:, lanes])))
        sides.append(with_rows(r[:, lanes], sent_a, sent_b, near, far, lanes))
    which = 0 if of_near else 1
    even = is_even("col")
    last = even if of_near else jnp.logical_not(even)
    full = jnp.concatenate([own[...], pick(even, *halos)[which]], axis=0)
    rhs = turn(pick(even, *sides)[which], 29, 1)
    lane = iota(full.shape, 1)
    start = jnp.where(last, 26, 29)
    full = jnp.where((lane >= start) & (lane < start + 3), rhs, full)
    tall = rows // 4
    block = iota((tall, 128), 1) // 32
    folded = full[:tall]
    for b in range(1, 4):
        folded = jnp.where(block == b, turn(full[b * tall : (b + 1) * tall], 32 * b, 1), folded)
    out[:tall, :] = folded
    out[tall:, :] = full[rows:]


def unfold(x, by):
    tall = x.shape[0] - 8
    blocks = [turn(x[:tall], by - 32 * b, 1) for b in range(4)]
    return jnp.concatenate(blocks + [turn(x[tall:], by, 1)], axis=0)


def local_rhs(g, c, land, bottom, surf, r_ref, code_ref):
    rows, cols = surf.shape
    code = code_of(land[...], bottom[...])
    code_ref[...] = code
    cu = jnp.where(iota(code.shape, 1) < cols - 1, jnp.minimum(code, next_col(code)), 0.0)
    cv = jnp.where(iota(code.shape, 0) < rows - 1, jnp.minimum(code, next_row(code)), 0.0)
    ub, vb = faces(g, c, cu, next_col), faces(g, c, cv, next_row)
    r_ref[...] = surf[...] + 0.0625 * ((ub - prev_col(ub)) + (vb - prev_row(vb)))


def inner(r_in, code_in, diag, sent_a, sent_b, near, far, r_ref, p1_ref, p2_ref, mom_ref, rs_ref, codes_ref, diags_ref, r_own, sem):
    rows, cols = diag.shape
    halo = row_halo(near, far, slice(0, cols))
    r = with_rows(r_in[...], sent_a, sent_b, near, far, slice(0, cols))
    r_own[...] = r[:rows]
    copy = pltpu.make_async_copy(r_own, r_ref, sem)
    copy.start()
    code = jnp.concatenate([code_in[...], halo(CODE)], axis=0)
    dg = jnp.concatenate([diag[...], halo(DIAG)], axis=0)
    left = iota((rows + 8, 128), 1) < 64
    for x, ref in ((r, rs_ref), (code, codes_ref), (dg, diags_ref)):
        ref[...] = jnp.where(left, turn(x[:, cols - 128 :], -68, 1), turn(x[:, :128], 68, 1))
    code = 0.125 * code
    cu = jnp.where(iota(code.shape, 1) < cols - 1, jnp.minimum(code, next_col(code)), 0.0)
    cv = jnp.minimum(code, next_row(code))
    p1, p2, prods = products(r, cu, cv, dg, rows)
    p1_ref[...] = p1[:rows]
    p2_ref[...] = p2[:rows]
    lane = iota((8, 128), 1)
    for m, prod in enumerate(prods):
        parts = [fold(prod, slice(128 * j, 128 * j + 128)) for j in range(cols // 128)]
        parts[0] = jnp.where(lane >= NEAR, parts[0], 0.0)
        parts[-1] = jnp.where(lane < 128 - NEAR, parts[-1], 0.0)
        mom_ref[8 * m : 8 * m + 8, :] = sum(parts[1:], parts[0])
    copy.wait()


def col_halo(near, far):
    east, west = pick(is_even("col"), near[...], far[...])

    def plane(at):
        tile = unfold(east, -at)
        return jnp.where(iota(tile.shape, 1) < 64, tile, unfold(west, 127 - at))

    return plane


def outer(rs, codes, diags, mom_in, sent_a, sent_b, near, far, r_ref, p1_ref, p2_ref, mom_ref):
    rows = rs.shape[0] - 8
    even = is_even("col")
    high, low = pick(even, sent_a[...], sent_b[...])
    east, west = pick(even, near[...], far[...])
    at = iota(high.shape, 1) % 32

    def between(first, end, x):
        return jnp.where((at >= first) & (at < end), x, 0.0)

    def across(below, above, to):
        open_u = turn(jnp.minimum(below, above), -16, 1) > at.astype(F32) + 0.5
        total = between(0, 8, jnp.where(open_u, above - below, 0.0) * turn(above + below, -8, 1))
        moved = [turn(total, to + 1 - k, 1) for k in range(LEV + 1)]
        pairs = [moved[k] + moved[k + 1] for k in range(1, LEV - 1, 2)]
        shared = (pairs[0] + pairs[1]) + (pairs[2] + moved[LEV - 1])
        one, two = shared + moved[LEV], shared + moved[0]
        first = to % 32
        return 0.0625 * (between(first, first + 1, one) - between(first + 1, first + 2, two))

    def placed(x, e, w, by):
        came = unfold(e + w, by)
        lane = iota(came.shape, 1)
        return jnp.where((lane < 60) | (lane >= 68), x, came), came

    _, added = placed(
        0.0, across(high, east, 28) + between(29, 32, east), across(west, low, 36) + turn(between(26, 29, west), 8, 1), 31
    )
    lane = iota(added.shape, 1)
    r = jnp.where((lane < 60) | (lane >= 68), rs[...], 0.0) + jnp.where((lane >= 59) & (lane < 69), added, 0.0)
    nearest = jnp.where(at == 26, turn(west, 3, 1), west)
    code, _ = placed(codes[...], between(23, 26, east), turn(between(24, 27, nearest), 4, 1), 37)
    code = 0.125 * code
    dg, _ = placed(diags[...], between(26, 28, east), turn(between(29, 31, west), 3, 1), 34)
    cu, cv = jnp.minimum(code, next_col(code)), jnp.minimum(code, next_row(code))
    p1, p2, prods = products(r, cu, cv, dg, rows)
    r_ref[...] = r
    p1_ref[...] = p1
    p2_ref[...] = p2
    lane = iota((8, 128), 1)
    mine = ((lane >= 60 - NEAR) & (lane < 60)) | ((lane >= 68) & (lane < 68 + NEAR))
    sub = iota((8, 128), 0)
    sums = jnp.zeros((8, 128), F32)
    for m, prod in enumerate(prods):
        part = mom_in[8 * m : 8 * m + 8, :] + jnp.where(mine, fold(prod, slice(0, 128)), 0.0)
        for by in (4, 2, 1):
            part = part + turn(part, by, 0)
        sums = jnp.where(sub == m, part, sums)
    sums = ((sums + turn(sums, 16, 1)) + (turn(sums, 32, 1) + turn(sums, 48, 1))) + (
        (turn(sums, 64, 1) + turn(sums, 80, 1)) + (turn(sums, 96, 1) + turn(sums, 112, 1))
    )
    sums = (sums + turn(sums, 4, 1)) + (turn(sums, 8, 1) + turn(sums, 12, 1))
    packed = jnp.zeros((8, 128), F32)
    for m in range(len(prods)):
        packed = jnp.where(lane // 4 == m, jnp.broadcast_to(sums[m : m + 1, :], (8, 128)), packed)
    for i in range(mom_ref.shape[0] // 8):
        mom_ref[8 * i : 8 * i + 8, :] = packed


def tracer_kernel(g_in, land_in, bottom_in, u_in, v_in, rn, rf, cn, cf, out_ref, g, land, bottom, u, v, out, sems, g_sems, out_sems):
    flat = [
        pltpu.make_async_copy(src, dst, sems.at[n])
        for n, (src, dst) in enumerate(((land_in, land), (bottom_in, bottom), (u_in, u), (v_in, v)))
    ]
    deep = [pltpu.make_async_copy(g_in.at[k], g.at[k], g_sems.at[k]) for k in range(LEV)]
    done = [pltpu.make_async_copy(out.at[k], out_ref.at[k], out_sems.at[k]) for k in range(LEV)]
    start_all(flat + deep)
    wait_all(flat)
    rows, cols = u.shape
    ch = col_halo(cn, cf)
    sub = iota((8, cols), 0)
    north, south = pick(is_even("row"), rn[...], rf[...])

    def wide(own, lane, above, below):
        at = [8 * (x // 8) for x in (above, below)]
        halo = jnp.where(
            sub == 0,
            turn(north[at[0] : at[0] + 8], -(above % 8), 0),
            turn(south[at[1] : at[1] + 8], 7 - below % 8, 0),
        )
        return jnp.concatenate([jnp.concatenate([own, halo], axis=0), ch(lane)], axis=1)

    code = wide(code_of(land[...], bottom[...]), 23, 20, 23)
    cu, cv = jnp.minimum(code, next_col(code)), jnp.minimum(code, next_row(code))
    uw = 0.125 * wide(u[...], 31, 28, 28)
    vw = 0.125 * wide(v[...], 31, 28, 28)
    for k in range(LEV):
        deep[k].wait()
        gk = wide(g[k], k, k, k)
        pu = jnp.where(cu > k + 0.5, next_col(gk) - gk, 0.0) * uw
        pv = jnp.where(cv > k + 0.5, next_row(gk) - gk, 0.0) * vw
        total = gk + pu + prev_col(pu) + pv + prev_row(pv)
        out[k] = total[:rows, :cols]
        done[k].start()
    wait_all(done)


def two_sum(a, b):
    s = a + b
    t = s - a
    return s, (a - (s - t)) + (b - t)


def quick(a, b):
    s = a + b
    return s, b - (s - a)


def split(a):
    t = a * 4097.0
    high = t - (t - a)
    return high, a - high


def add(x, y):
    s, e = two_sum(x[0], y[0])
    return quick(s, e + (x[1] + y[1]))


def neg(x):
    return -x[0], -x[1]


def mul(x, y):
    p = x[0] * y[0]
    (ah, al), (bh, bl) = split(x[0]), split(y[0])
    e = ((ah * bh - p) + ah * bl + al * bh) + al * bl
    return quick(p, e + (x[0] * y[1] + x[1] * y[0]))


def div(x, y):
    q = x[0] / y[0]
    rest = add(x, neg(mul((q, jnp.zeros_like(q)), y)))
    return quick(q, rest[0] / y[0])


def combine(mom, r, p1, p2, rs, p1s, p2s, x_ref, x, sems):
    zero = jnp.zeros((8, 128), F32)
    tiles = [(mom[8 * i : 8 * i + 8, :], zero) for i in range(mom.shape[0] // 8)]
    while len(tiles) > 1:
        tiles = [add(tiles[i], tiles[i + 1]) for i in range(0, len(tiles), 2)]
    total = tiles[0]
    for by in (4, 2, 1):
        total = add(total, tuple(pltpu.roll(a, by, 0) for a in total))
    sums = []
    for m in range(6):
        four = [
            tuple(jnp.broadcast_to(a[:, at : at + 1], (8, 128)) for a in total)
            for at in range(4 * m, 4 * m + 4)
        ]
        sums.append(add(add(four[0], four[1]), add(four[2], four[3])))
    m00, m01, m11, m12, m22, e22 = sums
    a00, a01, a02 = add(m01, m00), add(m11, m01), add(m12, m11)
    a11, a12, a22 = a02, add(m22, m12), e22
    l10 = div(a01, a00)
    l20 = div(a02, a00)
    w11 = add(a11, neg(mul(l10, a01)))
    w12 = add(a12, neg(mul(l10, a02)))
    ok1 = w11[0] > 1e-9 * a11[0]
    l21 = tuple(jnp.where(ok1, a, 0.0) for a in div(w12, w11))
    w22 = add(add(a22, neg(mul(l20, a02))), neg(mul(l21, w12)))
    ok2 = w22[0] > 1e-9 * a22[0]
    b0 = m00
    b1 = add(m01, neg(mul(l10, b0)))
    z1 = tuple(jnp.where(ok1, a, 0.0) for a in div(b1, w11))
    b2 = add(add(m11, neg(mul(l20, b0))), neg(mul(l21, b1)))
    z2 = tuple(jnp.where(ok2, a, 0.0) for a in div(b2, w22))
    y2 = z2
    y1 = add(z1, neg(mul(l21, y2)))
    y0 = add(div(b0, a00), neg(add(mul(l10, y1), mul(l20, y2))))
    rows, cols = r.shape
    bands = sems.shape[0]
    tall = rows // bands
    done = []
    for b in range(bands):
        band = slice(b * tall, (b + 1) * tall)
        for i in range(b * tall // 8, (b + 1) * tall // 8):
            at = slice(8 * i, 8 * i + 8)
            lane = iota((8, 128), 1)
            side = y0[0] * rs[at, :] + (y1[0] * p1s[at, :] + y2[0] * p2s[at, :])
            for j in range(cols // 128):
                to = (at, slice(128 * j, 128 * j + 128))
                tile = y0[0] * r[to] + (y1[0] * p1[to] + y2[0] * p2[to])
                if j == 0:
                    tile = jnp.where(lane < NEAR, turn(side, -68, 1), tile)
                if j == cols // 128 - 1:
                    tile = jnp.where(lane >= 128 - NEAR, turn(side, 68, 1), tile)
                x[to] = tile
        done.append(pltpu.make_async_copy(x.at[band, :], x_ref.at[band, :], sems.at[b]))
        done[-1].start()
    wait_all(done)


def call(kernel, ins, outs, scratch=(), name=None, cost=None):
    run = pl.pallas_call(
        kernel,
        in_specs=list(ins),
        out_specs=[spec for spec, _ in outs],
        out_shape=[spec.memory_space(shape, F32) for spec, shape in outs],
        scratch_shapes=list(scratch),
        compiler_params=PARAMS,
        cost_estimate=cost,
        name=name,
    )
    return lambda *args: run(*[pltpu.with_memory_space_constraint(x, spec.memory_space) for x, spec in zip(args, ins)])


def shards(tracer_adj_next, tracer, u_east, v_north, surf_adj_next, diag, land, bottom):
    levels, rows, cols = tracer.shape
    size = lax.axis_size("row") * lax.axis_size("col")
    g, c = tracer_adj_next, tracer
    dma = pltpu.SemaphoreType.DMA
    two, side = (rows, cols), (rows + 8, 128)
    whole = lambda kind=F32: pltpu.VMEM(two, kind)
    edges = [pltpu.VMEM((levels, 8, cols), F32)] * 4 + [pltpu.VMEM((8, cols), jnp.int32)] * 4 + [pltpu.VMEM((8, cols), F32)] * 6
    row_a, row_b = call(
        pack_rows, [HBM] * 7, [(VMEM, (32, cols))] * 2, edges + [dma((14,))], name="pack_rows"
    )(g, c, land, bottom, surf_adj_next, diag, v_north)
    row_far = lax.ppermute(row_b, "row", swap_pairs("row", 1))
    deep = pltpu.VMEM(g.shape, F32)
    a, b, row_a = call(
        pack_cols,
        [VMEM] * 8,
        [(VMEM, (rows, 128))] * 2 + [(VMEM, (32, cols))],
        name="pack_cols",
        cost=pl.CostEstimate(flops=g.size, bytes_accessed=g.size, transcendentals=0),
    )(g, c, land, bottom, surf_adj_next, diag, u_east, row_a)
    row_near = lax.ppermute(row_a, "row", swap_pairs("row", 0))
    row_sent, row_got = (row_a, row_b), (row_near, row_far)
    rhs, code = call(
        local_rhs,
        [VMEM] * 5,
        [(VMEM, two)] * 2,
        name="local_rhs",
        cost=pl.CostEstimate(flops=24 * g.size, bytes_accessed=8 * g.size, transcendentals=0),
    )(g, c, land, bottom, surf_adj_next)
    sent = (rows // 4 + 8, 128)
    (b,) = call(functools.partial(join_cols, False), [VMEM] * 6, [(VMEM, sent)], name="join_far")(
        b, rhs, *row_sent, *row_got
    )
    far = lax.ppermute(b, "col", swap_pairs("col", 1))
    r, p1, p2, mom, rs, codes, diags = call(
        inner,
        [VMEM] * 7,
        [(HBM, two)] + [(VMEM, two)] * 2 + [(VMEM, (48, 128))] + [(VMEM, side)] * 3,
        [whole(), dma],
        name="inner",
        cost=pl.CostEstimate(flops=24 * g.size, bytes_accessed=8 * g.size, transcendentals=0),
    )(rhs, code, diag, *row_sent, *row_got)
    (a,) = call(functools.partial(join_cols, True), [VMEM] * 7, [(VMEM, sent)], name="join_near")(
        a, rhs, *row_sent, *row_got, rs
    )
    near = lax.ppermute(a, "col", swap_pairs("col", 0))
    col_sent, col_got = (a, b), (near, far)
    *sides, mom = call(outer, [VMEM] * 8, [(VMEM, side)] * 3 + [(VMEM, (size, 128))], name="outer")(
        rs, codes, diags, mom, *col_sent, *col_got
    )
    mom = lax.all_to_all(mom, ("row", "col"), 0, 0, tiled=True)
    (tracer_adj,) = call(
        tracer_kernel,
        [HBM] * 5 + [VMEM] * 4,
        [(HBM, g.shape)],
        [deep, whole(jnp.int32), whole(jnp.int32), whole(), whole(), deep, dma((4,)), dma((levels,)), dma((levels,))],
        name="tracer",
        cost=pl.CostEstimate(flops=20 * g.size, bytes_accessed=12 * g.size, transcendentals=0),
    )(g, land, bottom, u_east, v_north, *row_got, *col_got)
    (surf_adj,) = call(
        combine,
        [VMEM] * 7,
        [(HBM, two)],
        [whole(), dma((2,))],
        name="combine",
    )(mom, r, p1, p2, *sides)
    return tracer_adj, surf_adj


def solution(mesh):
    three, two = P(None, "row", "col"), P("row", "col")
    return jax.shard_map(
        shards,
        mesh=mesh,
        in_specs=(three, three, two, two, two, two, two, two),
        out_specs=(three, two),
        check_vma=False,
    )
```

```python
import functools

import jax
import jax.numpy as jnp
from jax import lax
from jax.experimental import pallas as pl
from jax.experimental.pallas import tpu as pltpu
from jax.sharding import PartitionSpec as P

LEV = 8
DEEP = 4
NEAR = 32
SHIFT = 1.0
F32 = jnp.float32
VMEM = pl.BlockSpec(memory_space=pltpu.VMEM)
HBM = pl.BlockSpec(memory_space=pltpu.HBM)
PARAMS = pltpu.CompilerParams(vmem_limit_bytes=32 * 1024 * 1024)


G, C, RHS, CODE, DIAG = 0, 1, 4, 5, 6


def code_of(land, bottom):
    return jnp.where(land == 1, bottom, 0).astype(F32)


def swap_pairs(axis, first):
    count = lax.axis_size(axis)
    pairs = []
    for low in range(first, count - 1, 2):
        pairs += [(low, low + 1), (low + 1, low)]
    return pairs


def is_even(axis):
    return lax.rem(lax.axis_index(axis), 2) == 0


def iota(shape, dim):
    return lax.broadcasted_iota(jnp.int32, shape, dim)


def turn(x, by, dim):
    by = by % x.shape[dim]
    return pltpu.roll(x, by, dim) if by else x


def next_col(a):
    return turn(a, -1, 1)


def prev_col(a):
    return turn(a, 1, 1)


def next_row(a):
    return turn(a, -1, 0)


def prev_row(a):
    return turn(a, 1, 0)


def pick(even, one, two):
    return jnp.where(even, one, two), jnp.where(even, two, one)


def start_all(copies):
    for copy in copies:
        copy.start()


def wait_all(copies):
    for copy in copies:
        copy.wait()


def pack_rows(g, c, land, bottom, surf, diag, v, a_ref, b_ref, g0, g1, c0, c1, l0, l1, b0, b1, s0, s1, d0, d1, v0, v1, sems):
    rows = surf.shape[0]
    copies = []
    for src, low, high in ((g, g0, g1), (c, c0, c1), (land, l0, l1), (bottom, b0, b1), (surf, s0, s1), (diag, d0, d1), (v, v0, v1)):
        for dst, at in ((low, slice(0, 8)), (high, slice(rows - 8, rows))):
            part = src.at[:, at, :] if len(src.shape) == 3 else src.at[at, :]
            copies.append(pltpu.make_async_copy(part, dst, sems.at[len(copies)]))
    start_all(copies)
    wait_all(copies)

    cols = surf.shape[1]
    lane, sub = iota((8, cols), 1), iota((8, cols), 0)
    upper = sub < DEEP
    codes = [code_of(l0[...], b0[...]), code_of(l1[...], b1[...])]
    both = [jnp.where(upper, g0[k], g1[k]) for k in range(LEV)], [jnp.where(upper, c0[k], c1[k]) for k in range(LEV)]
    code = jnp.where(upper, *codes)
    cu = jnp.where(lane < cols - 1, jnp.minimum(code, next_col(code)), 0.0)
    ub = faces(*both, cu, next_col)
    ub = ub - prev_col(ub)
    cut = lambda x: [x[:, :128], x[:, cols - 128 :]]
    diags = jnp.where(upper, d0[...], d1[...])
    corners = [
        lane_pack(end, [cut(x)[end] for x in both[0]], [cut(x)[end] for x in both[1]], cut(code)[end], cut(diags)[end])
        for end in range(2)
    ]

    def tiles(g, c, code, surf, diag, v, of_last):
        g, c = [g[k] for k in range(LEV)], [c[k] for k in range(LEV)]
        cv = jnp.where(sub < 7, jnp.minimum(code, next_row(code)), 0.0)
        vb = faces(g, c, cv, next_row)
        rhs = surf[...] + 0.0625 * (ub + (vb - prev_row(vb)))
        edge = 7 if of_last else 0

        def outermost(x):
            out = turn(x[0], -edge, 0)
            for k in range(1, LEV):
                out = jnp.where(sub == k, turn(x[k], k - edge, 0), out)
            return out

        half = DEEP if of_last else 0
        one = jnp.where(upper, turn(rhs, half, 0), turn(code, DEEP - half, 0))
        two = jnp.where(upper, turn(diag[...], half, 0), turn(v[...], DEEP - edge, 0))
        ends = [
            jnp.where(sub[:, :128] < 5, two[:, lanes], corner if of_last else turn(corner, 5, 0))
            for corner, lanes in zip(corners, (slice(0, 128), slice(cols - 128, cols)))
        ]
        two = jnp.concatenate([ends[0], two[:, 128 : cols - 128], ends[1]], axis=1)
        return outermost(g), outermost(c), one, two

    first = tiles(g0, c0, codes[0], s0, d0, v0, False)
    last = tiles(g1, c1, codes[1], s1, d1, v1, True)
    even = is_even("row")
    for t in range(4):
        a_ref[8 * t : 8 * t + 8, :], b_ref[8 * t : 8 * t + 8, :] = pick(even, last[t], first[t])


def faces(g, c, coupling, step):
    total = jnp.zeros_like(coupling)
    for k in range(LEV):
        gk, ck = g[k], c[k]
        total = total + jnp.where(coupling > k + 0.5, step(gk) - gk, 0.0) * (step(ck) + ck)
    return total


def operator(cu, cv, dg):
    west, south = prev_col(cu), prev_row(cv)
    center = (dg - SHIFT) + ((cu + west) + (cv + south))

    def shifted(v):
        sides = (cu * next_col(v) + west * prev_col(v)) + (cv * next_row(v) + south * prev_row(v))
        return center * v - sides

    return shifted


def products(r, cu, cv, dg, rows):
    shifted = operator(cu, cv, dg)
    p1 = shifted(r)
    p2 = shifted(p1)
    eu, ev = p2 - next_col(p2), p2 - next_row(p2)
    energy = dg * p2 * p2 + (cu * eu * eu + cv * ev * ev)
    q, p, o = r[:rows], p1[:rows], p2[:rows]
    return p1, p2, (q * q, q * p, p * p, p * o, o * o, energy[:rows])


def fold(prod, lanes):
    tiles = [prod[8 * i : 8 * i + 8, lanes] for i in range(prod.shape[0] // 8)]
    while len(tiles) > 1:
        tiles = [sum(tiles[i : i + 2][1:], tiles[i]) for i in range(0, len(tiles), 2)]
    return tiles[0]


def lane_pack(end, g, c, code, diag, u=None):
    lane = iota(code.shape, 1)
    edge = 127 if end else 0
    out = jnp.where(lane == 16, turn(code, 16 - edge, 1), 0.0)
    for by in (1, 2, 4):
        out = out + turn(out, by, 1)
    places = [(g[k], edge, k, 1) for k in range(LEV)] + [(c[k], edge, 8 + k, 1) for k in range(LEV)]
    places += [(code, 125, 24, 2), (diag, 126, 29, 2)] if end else [(code, 1, 24, 2), (diag, 0, 26, 2)]
    if u is not None:
        places.append((u, 127, 31, 1))
    for x, at, to, width in places:
        out = jnp.where((lane >= to) & (lane < to + width), turn(x, to - at, 1), out)
    return out


def codes_of(land, bottom, row_in, code_ref, row_ref):
    row_ref[...] = row_in[...]
    code_ref[...] = code_of(land[...], bottom[...])


def row_halo(near, far, lanes):
    even = is_even("row")

    def plane(p):
        at = slice(8 * (p // 2), 8 * (p // 2) + 8)
        north, south = pick(even, near[at, lanes], far[at, lanes])
        upper = iota(north.shape, 0) < DEEP
        if p % 2 == 0:
            return jnp.where(upper, north, turn(south, DEEP, 0))
        return jnp.where(upper, turn(north, DEEP, 0), south)

    return plane


def with_rows(r, sent_a, sent_b, near, far, lanes):
    rows = r.shape[0]
    even = is_even("row")
    high, low = pick(even, sent_a[:, lanes], sent_b[:, lanes])
    north, south = pick(even, near[:, lanes], far[:, lanes])
    sub = iota((8, r.shape[1]), 0)

    def across(below, above):
        open_v = jnp.minimum(below[23:24], above[20:21]) > sub.astype(F32) + 0.5
        total = jnp.where(open_v, above[:8] - below[:8], 0.0) * (above[8:16] + below[8:16])
        for by in (4, 2, 1):
            total = total + turn(total, by, 0)
        return 0.0625 * total

    up, down = across(high, north), across(south, low)
    halo = row_halo(near, far, lanes)(RHS) + jnp.where(sub == 0, -up, jnp.where(sub == 7, down, 0.0))
    first = r[:8] - jnp.where(sub == 0, down, 0.0)
    last = r[rows - 8 :] + jnp.where(sub == 7, up, 0.0)
    return jnp.concatenate([first, r[8 : rows - 8], last, halo], axis=0)


def join_cols(of_near, high, low, r, sent_a, sent_b, near, far, *refs):
    rows, width = r.shape
    out = refs[-1]
    north, south = pick(is_even("row"), near[24:, :], far[24:, :])
    sub = iota((8, 128), 0)
    halos, sides = [], []
    for lanes in (slice(width - 128, width), slice(0, 128)):
        halos.append(jnp.where(sub < 3, turn(north[:, lanes], -5, 0), jnp.where(sub < 5, 0.0, south[:, lanes])))
        sides.append(with_rows(r[:, lanes], sent_a, sent_b, near, far, lanes))
    which = 0 if of_near else 1
    even = is_even("col")
    last = even if of_near else jnp.logical_not(even)
    own = pick(even, high[...], low[...])[which]
    full = jnp.concatenate([own, pick(even, *halos)[which]], axis=0)
    rhs = turn(pick(even, *sides)[which], 29, 1)
    lane = iota(full.shape, 1)
    start = jnp.where(last, 26, 29)
    full = jnp.where((lane >= start) & (lane < start + 3), rhs, full)
    tall = rows // 4
    block = iota((tall, 128), 1) // 32
    folded = full[:tall]
    for b in range(1, 4):
        folded = jnp.where(block == b, turn(full[b * tall : (b + 1) * tall], 32 * b, 1), folded)
    out[:tall, :] = folded
    out[tall:, :] = full[rows:]


def unfold(x, by):
    tall = x.shape[0] - 8
    blocks = [turn(x[:tall], by - 32 * b, 1) for b in range(4)]
    return jnp.concatenate(blocks + [turn(x[tall:], by, 1)], axis=0)


def local_rhs(g, c, code_in, surf, diag, u, r_ref, first_ref, last_ref):
    rows, cols = surf.shape
    code = code_in[...]
    cu = jnp.where(iota(code.shape, 1) < cols - 1, jnp.minimum(code, next_col(code)), 0.0)
    cv = jnp.where(iota(code.shape, 0) < rows - 1, jnp.minimum(code, next_row(code)), 0.0)
    ub, vb = faces(g, c, cu, next_col), faces(g, c, cv, next_row)
    r_ref[...] = surf[...] + 0.0625 * ((ub - prev_col(ub)) + (vb - prev_row(vb)))
    for end, (tile, ref) in enumerate(((slice(0, 128), first_ref), (slice(cols - 128, cols), last_ref))):
        gs, cs = [g[k, :, tile] for k in range(LEV)], [c[k, :, tile] for k in range(LEV)]
        ref[...] = lane_pack(end, gs, cs, code[:, tile], diag[:, tile], u[:, tile] if end else None)


def inner(r_in, code_in, diag, sent_a, sent_b, near, far, r_ref, p1_ref, p2_ref, mom_ref, rs_ref, codes_ref, diags_ref, r_own, sem):
    rows, cols = diag.shape
    halo = row_halo(near, far, slice(0, cols))
    r = with_rows(r_in[...], sent_a, sent_b, near, far, slice(0, cols))
    r_own[...] = r[:rows]
    copy = pltpu.make_async_copy(r_own, r_ref, sem)
    copy.start()
    code = jnp.concatenate([code_in[...], halo(CODE)], axis=0)
    dg = jnp.concatenate([diag[...], halo(DIAG)], axis=0)
    left = iota((rows + 8, 128), 1) < 64
    for x, ref in ((r, rs_ref), (code, codes_ref), (dg, diags_ref)):
        ref[...] = jnp.where(left, turn(x[:, cols - 128 :], -68, 1), turn(x[:, :128], 68, 1))
    code = 0.125 * code
    cu = jnp.where(iota(code.shape, 1) < cols - 1, jnp.minimum(code, next_col(code)), 0.0)
    cv = jnp.minimum(code, next_row(code))
    p1, p2, prods = products(r, cu, cv, dg, rows)
    p1_ref[...] = p1[:rows]
    p2_ref[...] = p2[:rows]
    lane = iota((8, 128), 1)
    for m, prod in enumerate(prods):
        parts = [fold(prod, slice(128 * j, 128 * j + 128)) for j in range(cols // 128)]
        parts[0] = jnp.where(lane >= NEAR, parts[0], 0.0)
        parts[-1] = jnp.where(lane < 128 - NEAR, parts[-1], 0.0)
        mom_ref[8 * m : 8 * m + 8, :] = sum(parts[1:], parts[0])
    copy.wait()


def col_halo(near, far):
    east, west = pick(is_even("col"), near[...], far[...])

    def plane(at):
        tile = unfold(east, -at)
        return jnp.where(iota(tile.shape, 1) < 64, tile, unfold(west, 127 - at))

    return plane


def outer(rs, codes, diags, mom_in, sent_a, sent_b, near, far, r_ref, p1_ref, p2_ref, mom_ref):
    rows = rs.shape[0] - 8
    even = is_even("col")
    high, low = pick(even, sent_a[...], sent_b[...])
    east, west = pick(even, near[...], far[...])
    at = iota(high.shape, 1) % 32

    def between(first, end, x):
        return jnp.where((at >= first) & (at < end), x, 0.0)

    def across(below, above, to):
        open_u = turn(jnp.minimum(below, above), -16, 1) > at.astype(F32) + 0.5
        total = between(0, 8, jnp.where(open_u, above - below, 0.0) * turn(above + below, -8, 1))
        moved = [turn(total, to + 1 - k, 1) for k in range(LEV + 1)]
        pairs = [moved[k] + moved[k + 1] for k in range(1, LEV - 1, 2)]
        shared = (pairs[0] + pairs[1]) + (pairs[2] + moved[LEV - 1])
        one, two = shared + moved[LEV], shared + moved[0]
        first = to % 32
        return 0.0625 * (between(first, first + 1, one) - between(first + 1, first + 2, two))

    def placed(x, e, w, by):
        came = unfold(e + w, by)
        lane = iota(came.shape, 1)
        return jnp.where((lane < 60) | (lane >= 68), x, came), came

    _, added = placed(
        0.0, across(high, east, 28) + between(29, 32, east), across(west, low, 36) + turn(between(26, 29, west), 8, 1), 31
    )
    lane = iota(added.shape, 1)
    r = jnp.where((lane < 60) | (lane >= 68), rs[...], 0.0) + jnp.where((lane >= 59) & (lane < 69), added, 0.0)
    nearest = jnp.where(at == 26, turn(west, 3, 1), west)
    code, _ = placed(codes[...], between(23, 26, east), turn(between(24, 27, nearest), 4, 1), 37)
    code = 0.125 * code
    dg, _ = placed(diags[...], between(26, 28, east), turn(between(29, 31, west), 3, 1), 34)
    cu, cv = jnp.minimum(code, next_col(code)), jnp.minimum(code, next_row(code))
    p1, p2, prods = products(r, cu, cv, dg, rows)
    r_ref[...] = r
    p1_ref[...] = p1
    p2_ref[...] = p2
    lane = iota((8, 128), 1)
    mine = ((lane >= 60 - NEAR) & (lane < 60)) | ((lane >= 68) & (lane < 68 + NEAR))
    sub = iota((8, 128), 0)
    sums = jnp.zeros((8, 128), F32)
    for m, prod in enumerate(prods):
        part = mom_in[8 * m : 8 * m + 8, :] + jnp.where(mine, fold(prod, slice(0, 128)), 0.0)
        for by in (4, 2, 1):
            part = part + turn(part, by, 0)
        sums = jnp.where(sub == m, part, sums)
    sums = ((sums + turn(sums, 16, 1)) + (turn(sums, 32, 1) + turn(sums, 48, 1))) + (
        (turn(sums, 64, 1) + turn(sums, 80, 1)) + (turn(sums, 96, 1) + turn(sums, 112, 1))
    )
    sums = (sums + turn(sums, 4, 1)) + (turn(sums, 8, 1) + turn(sums, 12, 1))
    packed = jnp.zeros((8, 128), F32)
    for m in range(len(prods)):
        packed = jnp.where(lane // 4 == m, jnp.broadcast_to(sums[m : m + 1, :], (8, 128)), packed)
    for i in range(mom_ref.shape[0] // 8):
        mom_ref[8 * i : 8 * i + 8, :] = packed


def tracer_kernel(g_in, land_in, bottom_in, u_in, v_in, rn, rf, cn, cf, out_ref, g, land, bottom, u, v, out, sems, g_sems, out_sems):
    flat = [
        pltpu.make_async_copy(src, dst, sems.at[n])
        for n, (src, dst) in enumerate(((land_in, land), (bottom_in, bottom), (u_in, u), (v_in, v)))
    ]
    deep = [pltpu.make_async_copy(g_in.at[k], g.at[k], g_sems.at[k]) for k in range(LEV)]
    done = [pltpu.make_async_copy(out.at[k], out_ref.at[k], out_sems.at[k]) for k in range(LEV)]
    start_all(flat + deep)
    wait_all(flat)
    rows, cols = u.shape
    ch = col_halo(cn, cf)
    sub = iota((8, cols), 0)
    north, south = pick(is_even("row"), rn[...], rf[...])

    def wide(own, lane, above, below):
        at = [8 * (x // 8) for x in (above, below)]
        halo = jnp.where(
            sub == 0,
            turn(north[at[0] : at[0] + 8], -(above % 8), 0),
            turn(south[at[1] : at[1] + 8], 7 - below % 8, 0),
        )
        return jnp.concatenate([jnp.concatenate([own, halo], axis=0), ch(lane)], axis=1)

    code = wide(code_of(land[...], bottom[...]), 23, 20, 23)
    cu, cv = jnp.minimum(code, next_col(code)), jnp.minimum(code, next_row(code))
    uw = 0.125 * wide(u[...], 31, 28, 28)
    vw = 0.125 * wide(v[...], 31, 28, 28)
    for k in range(LEV):
        deep[k].wait()
        gk = wide(g[k], k, k, k)
        pu = jnp.where(cu > k + 0.5, next_col(gk) - gk, 0.0) * uw
        pv = jnp.where(cv > k + 0.5, next_row(gk) - gk, 0.0) * vw
        total = gk + pu + prev_col(pu) + pv + prev_row(pv)
        out[k] = total[:rows, :cols]
        done[k].start()
    wait_all(done)


def two_sum(a, b):
    s = a + b
    t = s - a
    return s, (a - (s - t)) + (b - t)


def quick(a, b):
    s = a + b
    return s, b - (s - a)


def split(a):
    t = a * 4097.0
    high = t - (t - a)
    return high, a - high


def add(x, y):
    s, e = two_sum(x[0], y[0])
    return quick(s, e + (x[1] + y[1]))


def neg(x):
    return -x[0], -x[1]


def mul(x, y):
    p = x[0] * y[0]
    (ah, al), (bh, bl) = split(x[0]), split(y[0])
    e = ((ah * bh - p) + ah * bl + al * bh) + al * bl
    return quick(p, e + (x[0] * y[1] + x[1] * y[0]))


def div(x, y):
    q = x[0] / y[0]
    rest = add(x, neg(mul((q, jnp.zeros_like(q)), y)))
    return quick(q, rest[0] / y[0])


def combine(mom, r, p1, p2, rs, p1s, p2s, x_ref, x, sems):
    zero = jnp.zeros((8, 128), F32)
    tiles = [(mom[8 * i : 8 * i + 8, :], zero) for i in range(mom.shape[0] // 8)]
    while len(tiles) > 1:
        tiles = [add(tiles[i], tiles[i + 1]) for i in range(0, len(tiles), 2)]
    total = tiles[0]
    for by in (4, 2, 1):
        total = add(total, tuple(pltpu.roll(a, by, 0) for a in total))
    sums = []
    for m in range(6):
        four = [
            tuple(jnp.broadcast_to(a[:, at : at + 1], (8, 128)) for a in total)
            for at in range(4 * m, 4 * m + 4)
        ]
        sums.append(add(add(four[0], four[1]), add(four[2], four[3])))
    m00, m01, m11, m12, m22, e22 = sums
    a00, a01, a02 = add(m01, m00), add(m11, m01), add(m12, m11)
    a11, a12, a22 = a02, add(m22, m12), e22
    l10 = div(a01, a00)
    l20 = div(a02, a00)
    w11 = add(a11, neg(mul(l10, a01)))
    w12 = add(a12, neg(mul(l10, a02)))
    ok1 = w11[0] > 1e-9 * a11[0]
    l21 = tuple(jnp.where(ok1, a, 0.0) for a in div(w12, w11))
    w22 = add(add(a22, neg(mul(l20, a02))), neg(mul(l21, w12)))
    ok2 = w22[0] > 1e-9 * a22[0]
    b0 = m00
    b1 = add(m01, neg(mul(l10, b0)))
    z1 = tuple(jnp.where(ok1, a, 0.0) for a in div(b1, w11))
    b2 = add(add(m11, neg(mul(l20, b0))), neg(mul(l21, b1)))
    z2 = tuple(jnp.where(ok2, a, 0.0) for a in div(b2, w22))
    y2 = z2
    y1 = add(z1, neg(mul(l21, y2)))
    y0 = add(div(b0, a00), neg(add(mul(l10, y1), mul(l20, y2))))
    rows, cols = r.shape
    bands = sems.shape[0]
    tall = rows // bands
    done = []
    for b in range(bands):
        band = slice(b * tall, (b + 1) * tall)
        for i in range(b * tall // 8, (b + 1) * tall // 8):
            at = slice(8 * i, 8 * i + 8)
            lane = iota((8, 128), 1)
            side = y0[0] * rs[at, :] + (y1[0] * p1s[at, :] + y2[0] * p2s[at, :])
            for j in range(cols // 128):
                to = (at, slice(128 * j, 128 * j + 128))
                tile = y0[0] * r[to] + (y1[0] * p1[to] + y2[0] * p2[to])
                if j == 0:
                    tile = jnp.where(lane < NEAR, turn(side, -68, 1), tile)
                if j == cols // 128 - 1:
                    tile = jnp.where(lane >= 128 - NEAR, turn(side, 68, 1), tile)
                x[to] = tile
        done.append(pltpu.make_async_copy(x.at[band, :], x_ref.at[band, :], sems.at[b]))
        done[-1].start()
    wait_all(done)


def call(kernel, ins, outs, scratch=(), name=None, cost=None):
    run = pl.pallas_call(
        kernel,
        in_specs=list(ins),
        out_specs=[spec for spec, _ in outs],
        out_shape=[spec.memory_space(shape, F32) for spec, shape in outs],
        scratch_shapes=list(scratch),
        compiler_params=PARAMS,
        cost_estimate=cost,
        name=name,
    )
    return lambda *args: run(*[pltpu.with_memory_space_constraint(x, spec.memory_space) for x, spec in zip(args, ins)])


def shards(tracer_adj_next, tracer, u_east, v_north, surf_adj_next, diag, land, bottom):
    levels, rows, cols = tracer.shape
    size = lax.axis_size("row") * lax.axis_size("col")
    g, c = tracer_adj_next, tracer
    dma = pltpu.SemaphoreType.DMA
    two, side = (rows, cols), (rows + 8, 128)
    whole = lambda kind=F32: pltpu.VMEM(two, kind)
    edges = [pltpu.VMEM((levels, 8, cols), F32)] * 4 + [pltpu.VMEM((8, cols), jnp.int32)] * 4 + [pltpu.VMEM((8, cols), F32)] * 6
    row_a, row_b = call(
        pack_rows, [HBM] * 7, [(VMEM, (32, cols))] * 2, edges + [dma((14,))], name="pack_rows"
    )(g, c, land, bottom, surf_adj_next, diag, v_north)
    row_far = lax.ppermute(row_b, "row", swap_pairs("row", 1))
    deep = pltpu.VMEM(g.shape, F32)
    code, row_a = call(
        codes_of,
        [VMEM] * 3,
        [(VMEM, two), (VMEM, (32, cols))],
        name="codes_of",
        cost=pl.CostEstimate(flops=g.size, bytes_accessed=g.size, transcendentals=0),
    )(land, bottom, row_a)
    row_near = lax.ppermute(row_a, "row", swap_pairs("row", 0))
    row_sent, row_got = (row_a, row_b), (row_near, row_far)
    rhs, low, high = call(
        local_rhs,
        [VMEM] * 6,
        [(VMEM, two)] + [(VMEM, (rows, 128))] * 2,
        name="local_rhs",
        cost=pl.CostEstimate(flops=24 * g.size, bytes_accessed=8 * g.size, transcendentals=0),
    )(g, c, code, surf_adj_next, diag, u_east)
    sent = (rows // 4 + 8, 128)
    (b,) = call(functools.partial(join_cols, False), [VMEM] * 7, [(VMEM, sent)], name="join_far")(
        high, low, rhs, *row_sent, *row_got
    )
    far = lax.ppermute(b, "col", swap_pairs("col", 1))
    r, p1, p2, mom, rs, codes, diags = call(
        inner,
        [VMEM] * 7,
        [(HBM, two)] + [(VMEM, two)] * 2 + [(VMEM, (48, 128))] + [(VMEM, side)] * 3,
        [whole(), dma],
        name="inner",
        cost=pl.CostEstimate(flops=24 * g.size, bytes_accessed=8 * g.size, transcendentals=0),
    )(rhs, code, diag, *row_sent, *row_got)
    (a,) = call(functools.partial(join_cols, True), [VMEM] * 8, [(VMEM, sent)], name="join_near")(
        high, low, rhs, *row_sent, *row_got, rs
    )
    near = lax.ppermute(a, "col", swap_pairs("col", 0))
    col_sent, col_got = (a, b), (near, far)
    *sides, mom = call(outer, [VMEM] * 8, [(VMEM, side)] * 3 + [(VMEM, (size, 128))], name="outer")(
        rs, codes, diags, mom, *col_sent, *col_got
    )
    mom = lax.all_to_all(mom, ("row", "col"), 0, 0, tiled=True)
    (tracer_adj,) = call(
        tracer_kernel,
        [HBM] * 5 + [VMEM] * 4,
        [(HBM, g.shape)],
        [deep, whole(jnp.int32), whole(jnp.int32), whole(), whole(), deep, dma((4,)), dma((levels,)), dma((levels,))],
        name="tracer",
        cost=pl.CostEstimate(flops=20 * g.size, bytes_accessed=12 * g.size, transcendentals=0),
    )(g, land, bottom, u_east, v_north, *row_got, *col_got)
    (surf_adj,) = call(
        combine,
        [VMEM] * 7,
        [(HBM, two)],
        [whole(), dma((2,))],
        name="combine",
    )(mom, r, p1, p2, *sides)
    return tracer_adj, surf_adj


def solution(mesh):
    three, two = P(None, "row", "col"), P("row", "col")
    return jax.shard_map(
        shards,
        mesh=mesh,
        in_specs=(three, three, two, two, two, two, two, two),
        out_specs=(three, two),
        check_vma=False,
    )
```

```python
import functools

import jax
import jax.numpy as jnp
from jax import lax
from jax.experimental import pallas as pl
from jax.experimental.pallas import tpu as pltpu
from jax.sharding import PartitionSpec as P

LEV = 8
DEEP = 4
NEAR = 32
SHIFT = 1.0
F32 = jnp.float32
VMEM = pl.BlockSpec(memory_space=pltpu.VMEM)
HBM = pl.BlockSpec(memory_space=pltpu.HBM)
PARAMS = pltpu.CompilerParams(vmem_limit_bytes=32 * 1024 * 1024)


G, C, RHS, CODE, DIAG = 0, 1, 4, 5, 6


def code_of(land, bottom):
    return jnp.where(land == 1, bottom, 0).astype(F32)


def swap_pairs(axis, first):
    count = lax.axis_size(axis)
    pairs = []
    for low in range(first, count - 1, 2):
        pairs += [(low, low + 1), (low + 1, low)]
    return pairs


def is_even(axis):
    return lax.rem(lax.axis_index(axis), 2) == 0


def iota(shape, dim):
    return lax.broadcasted_iota(jnp.int32, shape, dim)


def turn(x, by, dim):
    by = by % x.shape[dim]
    return pltpu.roll(x, by, dim) if by else x


def next_col(a):
    return turn(a, -1, 1)


def prev_col(a):
    return turn(a, 1, 1)


def next_row(a):
    return turn(a, -1, 0)


def prev_row(a):
    return turn(a, 1, 0)


def pick(even, one, two):
    return jnp.where(even, one, two), jnp.where(even, two, one)


def start_all(copies):
    for copy in copies:
        copy.start()


def wait_all(copies):
    for copy in copies:
        copy.wait()


def pack_rows(g, c, land, bottom, surf, diag, v, a_ref, b_ref, g0, g1, c0, c1, l0, l1, b0, b1, s0, s1, d0, d1, v0, v1, sems):
    rows = surf.shape[0]
    copies = []
    for src, low, high in ((g, g0, g1), (c, c0, c1), (land, l0, l1), (bottom, b0, b1), (surf, s0, s1), (diag, d0, d1), (v, v0, v1)):
        for dst, at in ((low, slice(0, 8)), (high, slice(rows - 8, rows))):
            part = src.at[:, at, :] if len(src.shape) == 3 else src.at[at, :]
            copies.append(pltpu.make_async_copy(part, dst, sems.at[len(copies)]))
    start_all(copies)
    wait_all(copies)

    cols = surf.shape[1]
    lane, sub = iota((8, cols), 1), iota((8, cols), 0)
    upper = sub < DEEP
    codes = [code_of(l0[...], b0[...]), code_of(l1[...], b1[...])]
    both = [jnp.where(upper, g0[k], g1[k]) for k in range(LEV)], [jnp.where(upper, c0[k], c1[k]) for k in range(LEV)]
    code = jnp.where(upper, *codes)
    cu = jnp.where(lane < cols - 1, jnp.minimum(code, next_col(code)), 0.0)
    ub = faces(*both, cu, next_col)
    ub = ub - prev_col(ub)
    cut = lambda x: [x[:, :128], x[:, cols - 128 :]]
    diags = jnp.where(upper, d0[...], d1[...])
    corners = [
        lane_pack(end, [cut(x)[end] for x in both[0]], [cut(x)[end] for x in both[1]], cut(code)[end], cut(diags)[end])
        for end in range(2)
    ]

    def tiles(g, c, code, surf, diag, v, of_last):
        g, c = [g[k] for k in range(LEV)], [c[k] for k in range(LEV)]
        cv = jnp.where(sub < 7, jnp.minimum(code, next_row(code)), 0.0)
        vb = faces(g, c, cv, next_row)
        rhs = surf[...] + 0.0625 * (ub + (vb - prev_row(vb)))
        edge = 7 if of_last else 0

        def outermost(x):
            out = turn(x[0], -edge, 0)
            for k in range(1, LEV):
                out = jnp.where(sub == k, turn(x[k], k - edge, 0), out)
            return out

        half = DEEP if of_last else 0
        one = jnp.where(upper, turn(rhs, half, 0), turn(code, DEEP - half, 0))
        two = jnp.where(upper, turn(diag[...], half, 0), turn(v[...], DEEP - edge, 0))
        ends = [
            jnp.where(sub[:, :128] < 5, two[:, lanes], corner if of_last else turn(corner, 5, 0))
            for corner, lanes in zip(corners, (slice(0, 128), slice(cols - 128, cols)))
        ]
        two = jnp.concatenate([ends[0], two[:, 128 : cols - 128], ends[1]], axis=1)
        return outermost(g), outermost(c), one, two

    first = tiles(g0, c0, codes[0], s0, d0, v0, False)
    last = tiles(g1, c1, codes[1], s1, d1, v1, True)
    even = is_even("row")
    for t in range(4):
        a_ref[8 * t : 8 * t + 8, :], b_ref[8 * t : 8 * t + 8, :] = pick(even, last[t], first[t])


def faces(g, c, coupling, step):
    total = jnp.zeros_like(coupling)
    for k in range(LEV):
        gk, ck = g[k], c[k]
        total = total + jnp.where(coupling > k + 0.5, step(gk) - gk, 0.0) * (step(ck) + ck)
    return total


def operator(cu, cv, dg):
    west, south = prev_col(cu), prev_row(cv)
    center = (dg - SHIFT) + ((cu + west) + (cv + south))

    def shifted(v):
        sides = (cu * next_col(v) + west * prev_col(v)) + (cv * next_row(v) + south * prev_row(v))
        return center * v - sides

    return shifted


def products(r, cu, cv, dg, rows):
    shifted = operator(cu, cv, dg)
    p1 = shifted(r)
    p2 = shifted(p1)
    eu, ev = p2 - next_col(p2), p2 - next_row(p2)
    energy = dg * p2 * p2 + (cu * eu * eu + cv * ev * ev)
    q, p, o = r[:rows], p1[:rows], p2[:rows]
    return p1, p2, (q * q, q * p, p * p, p * o, o * o, energy[:rows])


def fold(prod, lanes):
    tiles = [prod[8 * i : 8 * i + 8, lanes] for i in range(prod.shape[0] // 8)]
    while len(tiles) > 1:
        tiles = [sum(tiles[i : i + 2][1:], tiles[i]) for i in range(0, len(tiles), 2)]
    return tiles[0]


def lane_pack(end, g, c, code, diag, u=None):
    lane = iota(code.shape, 1)
    edge = 127 if end else 0
    out = jnp.where(lane == 16, turn(code, 16 - edge, 1), 0.0)
    for by in (1, 2, 4):
        out = out + turn(out, by, 1)
    places = [(g[k], edge, k, 1) for k in range(LEV)] + [(c[k], edge, 8 + k, 1) for k in range(LEV)]
    places += [(code, 125, 24, 2), (diag, 126, 29, 2)] if end else [(code, 1, 24, 2), (diag, 0, 26, 2)]
    if u is not None:
        places.append((u, 127, 31, 1))
    for x, at, to, width in places:
        out = jnp.where((lane >= to) & (lane < to + width), turn(x, to - at, 1), out)
    return out


def codes_of(land, bottom, row_in, code_ref, row_ref):
    row_ref[...] = row_in[...]
    code_ref[...] = code_of(land[...], bottom[...])


def row_halo(near, far, lanes):
    even = is_even("row")

    def plane(p):
        at = slice(8 * (p // 2), 8 * (p // 2) + 8)
        north, south = pick(even, near[at, lanes], far[at, lanes])
        upper = iota(north.shape, 0) < DEEP
        if p % 2 == 0:
            return jnp.where(upper, north, turn(south, DEEP, 0))
        return jnp.where(upper, turn(north, DEEP, 0), south)

    return plane


def with_rows(r, sent_a, sent_b, near, far, lanes):
    rows = r.shape[0]
    even = is_even("row")
    high, low = pick(even, sent_a[:, lanes], sent_b[:, lanes])
    north, south = pick(even, near[:, lanes], far[:, lanes])
    sub = iota((8, r.shape[1]), 0)

    def across(below, above):
        open_v = jnp.minimum(below[23:24], above[20:21]) > sub.astype(F32) + 0.5
        total = jnp.where(open_v, above[:8] - below[:8], 0.0) * (above[8:16] + below[8:16])
        for by in (4, 2, 1):
            total = total + turn(total, by, 0)
        return 0.0625 * total

    up, down = across(high, north), across(south, low)
    halo = row_halo(near, far, lanes)(RHS) + jnp.where(sub == 0, -up, jnp.where(sub == 7, down, 0.0))
    first = r[:8] - jnp.where(sub == 0, down, 0.0)
    last = r[rows - 8 :] + jnp.where(sub == 7, up, 0.0)
    return jnp.concatenate([first, r[8 : rows - 8], last, halo], axis=0)


def join_cols(of_near, high, low, r, sent_a, sent_b, near, far, *refs):
    rows, width = r.shape
    out = refs[-1]
    north, south = pick(is_even("row"), near[24:, :], far[24:, :])
    sub = iota((8, 128), 0)
    halos, sides = [], []
    for lanes in (slice(width - 128, width), slice(0, 128)):
        halos.append(jnp.where(sub < 3, turn(north[:, lanes], -5, 0), jnp.where(sub < 5, 0.0, south[:, lanes])))
        sides.append(with_rows(r[:, lanes], sent_a, sent_b, near, far, lanes))
    which = 0 if of_near else 1
    even = is_even("col")
    last = even if of_near else jnp.logical_not(even)
    own = pick(even, high[...], low[...])[which]
    full = jnp.concatenate([own, pick(even, *halos)[which]], axis=0)
    rhs = turn(pick(even, *sides)[which], 29, 1)
    lane = iota(full.shape, 1)
    start = jnp.where(last, 26, 29)
    full = jnp.where((lane >= start) & (lane < start + 3), rhs, full)
    tall = rows // 4
    block = iota((tall, 128), 1) // 32
    folded = full[:tall]
    for b in range(1, 4):
        folded = jnp.where(block == b, turn(full[b * tall : (b + 1) * tall], 32 * b, 1), folded)
    out[:tall, :] = folded
    out[tall:, :] = full[rows:]


def unfold(x, by):
    tall = x.shape[0] - 8
    blocks = [turn(x[:tall], by - 32 * b, 1) for b in range(4)]
    return jnp.concatenate(blocks + [turn(x[tall:], by, 1)], axis=0)


def local_rhs(g, c, code_in, surf, diag, u, r_ref, first_ref, last_ref):
    rows, cols = surf.shape
    code = code_in[...]
    cu = jnp.where(iota(code.shape, 1) < cols - 1, jnp.minimum(code, next_col(code)), 0.0)
    cv = jnp.where(iota(code.shape, 0) < rows - 1, jnp.minimum(code, next_row(code)), 0.0)
    ub, vb = faces(g, c, cu, next_col), faces(g, c, cv, next_row)
    r_ref[...] = surf[...] + 0.0625 * ((ub - prev_col(ub)) + (vb - prev_row(vb)))
    for end, (tile, ref) in enumerate(((slice(0, 128), first_ref), (slice(cols - 128, cols), last_ref))):
        gs, cs = [g[k, :, tile] for k in range(LEV)], [c[k, :, tile] for k in range(LEV)]
        ref[...] = lane_pack(end, gs, cs, code[:, tile], diag[:, tile], u[:, tile] if end else None)


def ends_of(r_in, code_in, diag, sent_a, sent_b, near, far, rs_ref, codes_ref, diags_ref):
    rows, cols = diag.shape
    halo = row_halo(near, far, slice(0, cols))
    r = with_rows(r_in[...], sent_a, sent_b, near, far, slice(0, cols))
    code = jnp.concatenate([code_in[...], halo(CODE)], axis=0)
    dg = jnp.concatenate([diag[...], halo(DIAG)], axis=0)
    left = iota((rows + 8, 128), 1) < 64
    for x, ref in ((r, rs_ref), (code, codes_ref), (dg, diags_ref)):
        ref[...] = jnp.where(left, turn(x[:, cols - 128 :], -68, 1), turn(x[:, :128], 68, 1))


def inner(r_in, code_in, diag, sent_a, sent_b, near, far, r_ref, p1_ref, p2_ref, mom_ref, r_own, sem):
    rows, cols = diag.shape
    halo = row_halo(near, far, slice(0, cols))
    r = with_rows(r_in[...], sent_a, sent_b, near, far, slice(0, cols))
    r_own[...] = r[:rows]
    copy = pltpu.make_async_copy(r_own, r_ref, sem)
    copy.start()
    code = jnp.concatenate([code_in[...], halo(CODE)], axis=0)
    dg = jnp.concatenate([diag[...], halo(DIAG)], axis=0)
    code = 0.125 * code
    cu = jnp.where(iota(code.shape, 1) < cols - 1, jnp.minimum(code, next_col(code)), 0.0)
    cv = jnp.minimum(code, next_row(code))
    p1, p2, prods = products(r, cu, cv, dg, rows)
    p1_ref[...] = p1[:rows]
    p2_ref[...] = p2[:rows]
    lane = iota((8, 128), 1)
    for m, prod in enumerate(prods):
        parts = [fold(prod, slice(128 * j, 128 * j + 128)) for j in range(cols // 128)]
        parts[0] = jnp.where(lane >= NEAR, parts[0], 0.0)
        parts[-1] = jnp.where(lane < 128 - NEAR, parts[-1], 0.0)
        mom_ref[8 * m : 8 * m + 8, :] = sum(parts[1:], parts[0])
    copy.wait()


def col_halo(near, far):
    east, west = pick(is_even("col"), near[...], far[...])

    def plane(at):
        tile = unfold(east, -at)
        return jnp.where(iota(tile.shape, 1) < 64, tile, unfold(west, 127 - at))

    return plane


def outer(rs, codes, diags, mom_in, sent_a, sent_b, near, far, r_ref, p1_ref, p2_ref, mom_ref):
    rows = rs.shape[0] - 8
    even = is_even("col")
    high, low = pick(even, sent_a[...], sent_b[...])
    east, west = pick(even, near[...], far[...])
    at = iota(high.shape, 1) % 32

    def between(first, end, x):
        return jnp.where((at >= first) & (at < end), x, 0.0)

    def across(below, above, to):
        open_u = turn(jnp.minimum(below, above), -16, 1) > at.astype(F32) + 0.5
        total = between(0, 8, jnp.where(open_u, above - below, 0.0) * turn(above + below, -8, 1))
        moved = [turn(total, to + 1 - k, 1) for k in range(LEV + 1)]
        pairs = [moved[k] + moved[k + 1] for k in range(1, LEV - 1, 2)]
        shared = (pairs[0] + pairs[1]) + (pairs[2] + moved[LEV - 1])
        one, two = shared + moved[LEV], shared + moved[0]
        first = to % 32
        return 0.0625 * (between(first, first + 1, one) - between(first + 1, first + 2, two))

    def placed(x, e, w, by):
        came = unfold(e + w, by)
        lane = iota(came.shape, 1)
        return jnp.where((lane < 60) | (lane >= 68), x, came), came

    _, added = placed(
        0.0, across(high, east, 28) + between(29, 32, east), across(west, low, 36) + turn(between(26, 29, west), 8, 1), 31
    )
    lane = iota(added.shape, 1)
    r = jnp.where((lane < 60) | (lane >= 68), rs[...], 0.0) + jnp.where((lane >= 59) & (lane < 69), added, 0.0)
    nearest = jnp.where(at == 26, turn(west, 3, 1), west)
    code, _ = placed(codes[...], between(23, 26, east), turn(between(24, 27, nearest), 4, 1), 37)
    code = 0.125 * code
    dg, _ = placed(diags[...], between(26, 28, east), turn(between(29, 31, west), 3, 1), 34)
    cu, cv = jnp.minimum(code, next_col(code)), jnp.minimum(code, next_row(code))
    p1, p2, prods = products(r, cu, cv, dg, rows)
    r_ref[...] = r
    p1_ref[...] = p1
    p2_ref[...] = p2
    lane = iota((8, 128), 1)
    mine = ((lane >= 60 - NEAR) & (lane < 60)) | ((lane >= 68) & (lane < 68 + NEAR))
    sub = iota((8, 128), 0)
    sums = jnp.zeros((8, 128), F32)
    for m, prod in enumerate(prods):
        part = mom_in[8 * m : 8 * m + 8, :] + jnp.where(mine, fold(prod, slice(0, 128)), 0.0)
        for by in (4, 2, 1):
            part = part + turn(part, by, 0)
        sums = jnp.where(sub == m, part, sums)
    sums = ((sums + turn(sums, 16, 1)) + (turn(sums, 32, 1) + turn(sums, 48, 1))) + (
        (turn(sums, 64, 1) + turn(sums, 80, 1)) + (turn(sums, 96, 1) + turn(sums, 112, 1))
    )
    sums = (sums + turn(sums, 4, 1)) + (turn(sums, 8, 1) + turn(sums, 12, 1))
    packed = jnp.zeros((8, 128), F32)
    for m in range(len(prods)):
        packed = jnp.where(lane // 4 == m, jnp.broadcast_to(sums[m : m + 1, :], (8, 128)), packed)
    for i in range(mom_ref.shape[0] // 8):
        mom_ref[8 * i : 8 * i + 8, :] = packed


def tracer_kernel(g_in, land_in, bottom_in, u_in, v_in, rn, rf, cn, cf, out_ref, g, land, bottom, u, v, out, sems, g_sems, out_sems):
    flat = [
        pltpu.make_async_copy(src, dst, sems.at[n])
        for n, (src, dst) in enumerate(((land_in, land), (bottom_in, bottom), (u_in, u), (v_in, v)))
    ]
    deep = [pltpu.make_async_copy(g_in.at[k], g.at[k], g_sems.at[k]) for k in range(LEV)]
    done = [pltpu.make_async_copy(out.at[k], out_ref.at[k], out_sems.at[k]) for k in range(LEV)]
    start_all(flat + deep)
    wait_all(flat)
    rows, cols = u.shape
    ch = col_halo(cn, cf)
    sub = iota((8, cols), 0)
    north, south = pick(is_even("row"), rn[...], rf[...])

    def wide(own, lane, above, below):
        at = [8 * (x // 8) for x in (above, below)]
        halo = jnp.where(
            sub == 0,
            turn(north[at[0] : at[0] + 8], -(above % 8), 0),
            turn(south[at[1] : at[1] + 8], 7 - below % 8, 0),
        )
        return jnp.concatenate([jnp.concatenate([own, halo], axis=0), ch(lane)], axis=1)

    code = wide(code_of(land[...], bottom[...]), 23, 20, 23)
    cu, cv = jnp.minimum(code, next_col(code)), jnp.minimum(code, next_row(code))
    uw = 0.125 * wide(u[...], 31, 28, 28)
    vw = 0.125 * wide(v[...], 31, 28, 28)
    for k in range(LEV):
        deep[k].wait()
        gk = wide(g[k], k, k, k)
        pu = jnp.where(cu > k + 0.5, next_col(gk) - gk, 0.0) * uw
        pv = jnp.where(cv > k + 0.5, next_row(gk) - gk, 0.0) * vw
        total = gk + pu + prev_col(pu) + pv + prev_row(pv)
        out[k] = total[:rows, :cols]
        done[k].start()
    wait_all(done)


def two_sum(a, b):
    s = a + b
    t = s - a
    return s, (a - (s - t)) + (b - t)


def quick(a, b):
    s = a + b
    return s, b - (s - a)


def split(a):
    t = a * 4097.0
    high = t - (t - a)
    return high, a - high


def add(x, y):
    s, e = two_sum(x[0], y[0])
    return quick(s, e + (x[1] + y[1]))


def neg(x):
    return -x[0], -x[1]


def mul(x, y):
    p = x[0] * y[0]
    (ah, al), (bh, bl) = split(x[0]), split(y[0])
    e = ((ah * bh - p) + ah * bl + al * bh) + al * bl
    return quick(p, e + (x[0] * y[1] + x[1] * y[0]))


def div(x, y):
    q = x[0] / y[0]
    rest = add(x, neg(mul((q, jnp.zeros_like(q)), y)))
    return quick(q, rest[0] / y[0])


def combine(mom, r, p1, p2, rs, p1s, p2s, x_ref, x, sems):
    zero = jnp.zeros((8, 128), F32)
    tiles = [(mom[8 * i : 8 * i + 8, :], zero) for i in range(mom.shape[0] // 8)]
    while len(tiles) > 1:
        tiles = [add(tiles[i], tiles[i + 1]) for i in range(0, len(tiles), 2)]
    total = tiles[0]
    for by in (4, 2, 1):
        total = add(total, tuple(pltpu.roll(a, by, 0) for a in total))
    sums = []
    for m in range(6):
        four = [
            tuple(jnp.broadcast_to(a[:, at : at + 1], (8, 128)) for a in total)
            for at in range(4 * m, 4 * m + 4)
        ]
        sums.append(add(add(four[0], four[1]), add(four[2], four[3])))
    m00, m01, m11, m12, m22, e22 = sums
    a00, a01, a02 = add(m01, m00), add(m11, m01), add(m12, m11)
    a11, a12, a22 = a02, add(m22, m12), e22
    l10 = div(a01, a00)
    l20 = div(a02, a00)
    w11 = add(a11, neg(mul(l10, a01)))
    w12 = add(a12, neg(mul(l10, a02)))
    ok1 = w11[0] > 1e-9 * a11[0]
    l21 = tuple(jnp.where(ok1, a, 0.0) for a in div(w12, w11))
    w22 = add(add(a22, neg(mul(l20, a02))), neg(mul(l21, w12)))
    ok2 = w22[0] > 1e-9 * a22[0]
    b0 = m00
    b1 = add(m01, neg(mul(l10, b0)))
    z1 = tuple(jnp.where(ok1, a, 0.0) for a in div(b1, w11))
    b2 = add(add(m11, neg(mul(l20, b0))), neg(mul(l21, b1)))
    z2 = tuple(jnp.where(ok2, a, 0.0) for a in div(b2, w22))
    y2 = z2
    y1 = add(z1, neg(mul(l21, y2)))
    y0 = add(div(b0, a00), neg(add(mul(l10, y1), mul(l20, y2))))
    rows, cols = r.shape
    bands = sems.shape[0]
    tall = rows // bands
    done = []
    for b in range(bands):
        band = slice(b * tall, (b + 1) * tall)
        for i in range(b * tall // 8, (b + 1) * tall // 8):
            at = slice(8 * i, 8 * i + 8)
            lane = iota((8, 128), 1)
            side = y0[0] * rs[at, :] + (y1[0] * p1s[at, :] + y2[0] * p2s[at, :])
            for j in range(cols // 128):
                to = (at, slice(128 * j, 128 * j + 128))
                tile = y0[0] * r[to] + (y1[0] * p1[to] + y2[0] * p2[to])
                if j == 0:
                    tile = jnp.where(lane < NEAR, turn(side, -68, 1), tile)
                if j == cols // 128 - 1:
                    tile = jnp.where(lane >= 128 - NEAR, turn(side, 68, 1), tile)
                x[to] = tile
        done.append(pltpu.make_async_copy(x.at[band, :], x_ref.at[band, :], sems.at[b]))
        done[-1].start()
    wait_all(done)


def call(kernel, ins, outs, scratch=(), name=None, cost=None):
    run = pl.pallas_call(
        kernel,
        in_specs=list(ins),
        out_specs=[spec for spec, _ in outs],
        out_shape=[spec.memory_space(shape, F32) for spec, shape in outs],
        scratch_shapes=list(scratch),
        compiler_params=PARAMS,
        cost_estimate=cost,
        name=name,
    )
    return lambda *args: run(*[pltpu.with_memory_space_constraint(x, spec.memory_space) for x, spec in zip(args, ins)])


def shards(tracer_adj_next, tracer, u_east, v_north, surf_adj_next, diag, land, bottom):
    levels, rows, cols = tracer.shape
    size = lax.axis_size("row") * lax.axis_size("col")
    g, c = tracer_adj_next, tracer
    dma = pltpu.SemaphoreType.DMA
    two, side = (rows, cols), (rows + 8, 128)
    whole = lambda kind=F32: pltpu.VMEM(two, kind)
    edges = [pltpu.VMEM((levels, 8, cols), F32)] * 4 + [pltpu.VMEM((8, cols), jnp.int32)] * 4 + [pltpu.VMEM((8, cols), F32)] * 6
    row_a, row_b = call(
        pack_rows, [HBM] * 7, [(VMEM, (32, cols))] * 2, edges + [dma((14,))], name="pack_rows"
    )(g, c, land, bottom, surf_adj_next, diag, v_north)
    row_far = lax.ppermute(row_b, "row", swap_pairs("row", 1))
    deep = pltpu.VMEM(g.shape, F32)
    code, row_a = call(
        codes_of,
        [VMEM] * 3,
        [(VMEM, two), (VMEM, (32, cols))],
        name="codes_of",
        cost=pl.CostEstimate(flops=g.size, bytes_accessed=g.size, transcendentals=0),
    )(land, bottom, row_a)
    row_near = lax.ppermute(row_a, "row", swap_pairs("row", 0))
    row_sent, row_got = (row_a, row_b), (row_near, row_far)
    rhs, low, high = call(
        local_rhs,
        [VMEM] * 6,
        [(VMEM, two)] + [(VMEM, (rows, 128))] * 2,
        name="local_rhs",
        cost=pl.CostEstimate(flops=24 * g.size, bytes_accessed=8 * g.size, transcendentals=0),
    )(g, c, code, surf_adj_next, diag, u_east)
    sent = (rows // 4 + 8, 128)
    (b,) = call(functools.partial(join_cols, False), [VMEM] * 7, [(VMEM, sent)], name="join_far")(
        high, low, rhs, *row_sent, *row_got
    )
    far = lax.ppermute(b, "col", swap_pairs("col", 1))
    fields = (rhs, code, diag, *row_sent, *row_got)
    rs, codes, diags = call(ends_of, [VMEM] * 7, [(VMEM, side)] * 3, name="ends_of")(*fields)
    (a,) = call(functools.partial(join_cols, True), [VMEM] * 8, [(VMEM, sent)], name="join_near")(
        high, low, rhs, *row_sent, *row_got, rs
    )
    near = lax.ppermute(a, "col", swap_pairs("col", 0))
    col_sent, col_got = (a, b), (near, far)
    r, p1, p2, mom = call(
        inner,
        [VMEM] * 7,
        [(HBM, two)] + [(VMEM, two)] * 2 + [(VMEM, (48, 128))],
        [whole(), dma],
        name="inner",
        cost=pl.CostEstimate(flops=24 * g.size, bytes_accessed=8 * g.size, transcendentals=0),
    )(*fields)
    *sides, mom = call(outer, [VMEM] * 8, [(VMEM, side)] * 3 + [(VMEM, (size, 128))], name="outer")(
        rs, codes, diags, mom, *col_sent, *col_got
    )
    mom = lax.all_to_all(mom, ("row", "col"), 0, 0, tiled=True)
    (tracer_adj,) = call(
        tracer_kernel,
        [HBM] * 5 + [VMEM] * 4,
        [(HBM, g.shape)],
        [deep, whole(jnp.int32), whole(jnp.int32), whole(), whole(), deep, dma((4,)), dma((levels,)), dma((levels,))],
        name="tracer",
        cost=pl.CostEstimate(flops=20 * g.size, bytes_accessed=12 * g.size, transcendentals=0),
    )(g, land, bottom, u_east, v_north, *row_got, *col_got)
    (surf_adj,) = call(
        combine,
        [VMEM] * 7,
        [(HBM, two)],
        [whole(), dma((2,))],
        name="combine",
    )(mom, r, p1, p2, *sides)
    return tracer_adj, surf_adj


def solution(mesh):
    three, two = P(None, "row", "col"), P("row", "col")
    return jax.shard_map(
        shards,
        mesh=mesh,
        in_specs=(three, three, two, two, two, two, two, two),
        out_specs=(three, two),
        check_vma=False,
    )
```

```python
import functools

import jax
import jax.numpy as jnp
from jax import lax
from jax.experimental import pallas as pl
from jax.experimental.pallas import tpu as pltpu
from jax.sharding import PartitionSpec as P

LEV = 8
DEEP = 4
NEAR = 32
SHIFT = 1.0
F32 = jnp.float32
VMEM = pl.BlockSpec(memory_space=pltpu.VMEM)
HBM = pl.BlockSpec(memory_space=pltpu.HBM)
PARAMS = pltpu.CompilerParams(vmem_limit_bytes=32 * 1024 * 1024)


G, C, RHS, CODE, DIAG = 0, 1, 4, 5, 6


def code_of(land, bottom):
    return jnp.where(land == 1, bottom, 0).astype(F32)


def swap_pairs(axis, first):
    count = lax.axis_size(axis)
    pairs = []
    for low in range(first, count - 1, 2):
        pairs += [(low, low + 1), (low + 1, low)]
    return pairs


def is_even(axis):
    return lax.rem(lax.axis_index(axis), 2) == 0


def iota(shape, dim):
    return lax.broadcasted_iota(jnp.int32, shape, dim)


def turn(x, by, dim):
    by = by % x.shape[dim]
    return pltpu.roll(x, by, dim) if by else x


def next_col(a):
    return turn(a, -1, 1)


def prev_col(a):
    return turn(a, 1, 1)


def next_row(a):
    return turn(a, -1, 0)


def prev_row(a):
    return turn(a, 1, 0)


def pick(even, one, two):
    return jnp.where(even, one, two), jnp.where(even, two, one)


def start_all(copies):
    for copy in copies:
        copy.start()


def wait_all(copies):
    for copy in copies:
        copy.wait()


def pack_rows(g, c, land, bottom, surf, diag, v, a_ref, b_ref, g0, g1, c0, c1, l0, l1, b0, b1, s0, s1, d0, d1, v0, v1, sems):
    rows = surf.shape[0]
    copies = []
    for src, low, high in ((g, g0, g1), (c, c0, c1), (land, l0, l1), (bottom, b0, b1), (surf, s0, s1), (diag, d0, d1), (v, v0, v1)):
        for dst, at in ((low, slice(0, 8)), (high, slice(rows - 8, rows))):
            part = src.at[:, at, :] if len(src.shape) == 3 else src.at[at, :]
            copies.append(pltpu.make_async_copy(part, dst, sems.at[len(copies)]))
    start_all(copies)
    wait_all(copies)

    cols = surf.shape[1]
    lane, sub = iota((8, cols), 1), iota((8, cols), 0)
    upper = sub < DEEP
    codes = [code_of(l0[...], b0[...]), code_of(l1[...], b1[...])]
    both = [jnp.where(upper, g0[k], g1[k]) for k in range(LEV)], [jnp.where(upper, c0[k], c1[k]) for k in range(LEV)]
    code = jnp.where(upper, *codes)
    cu = jnp.where(lane < cols - 1, jnp.minimum(code, next_col(code)), 0.0)
    ub = faces(*both, cu, next_col)
    ub = ub - prev_col(ub)
    cut = lambda x: [x[:, :128], x[:, cols - 128 :]]
    diags = jnp.where(upper, d0[...], d1[...])
    corners = [
        lane_pack(end, [cut(x)[end] for x in both[0]], [cut(x)[end] for x in both[1]], cut(code)[end], cut(diags)[end])
        for end in range(2)
    ]

    def tiles(g, c, code, surf, diag, v, of_last):
        g, c = [g[k] for k in range(LEV)], [c[k] for k in range(LEV)]
        cv = jnp.where(sub < 7, jnp.minimum(code, next_row(code)), 0.0)
        vb = faces(g, c, cv, next_row)
        rhs = surf[...] + 0.0625 * (ub + (vb - prev_row(vb)))
        edge = 7 if of_last else 0

        def outermost(x):
            out = turn(x[0], -edge, 0)
            for k in range(1, LEV):
                out = jnp.where(sub == k, turn(x[k], k - edge, 0), out)
            return out

        half = DEEP if of_last else 0
        one = jnp.where(upper, turn(rhs, half, 0), turn(code, DEEP - half, 0))
        two = jnp.where(upper, turn(diag[...], half, 0), turn(v[...], DEEP - edge, 0))
        ends = [
            jnp.where(sub[:, :128] < 5, two[:, lanes], corner if of_last else turn(corner, 5, 0))
            for corner, lanes in zip(corners, (slice(0, 128), slice(cols - 128, cols)))
        ]
        two = jnp.concatenate([ends[0], two[:, 128 : cols - 128], ends[1]], axis=1)
        return outermost(g), outermost(c), one, two

    first = tiles(g0, c0, codes[0], s0, d0, v0, False)
    last = tiles(g1, c1, codes[1], s1, d1, v1, True)
    even = is_even("row")
    for t in range(4):
        a_ref[8 * t : 8 * t + 8, :], b_ref[8 * t : 8 * t + 8, :] = pick(even, last[t], first[t])


def faces(g, c, coupling, step):
    total = jnp.zeros_like(coupling)
    for k in range(LEV):
        gk, ck = g[k], c[k]
        total = total + jnp.where(coupling > k + 0.5, step(gk) - gk, 0.0) * (step(ck) + ck)
    return total


def operator(cu, cv, dg):
    west, south = prev_col(cu), prev_row(cv)
    center = (dg - SHIFT) + ((cu + west) + (cv + south))

    def shifted(v):
        sides = (cu * next_col(v) + west * prev_col(v)) + (cv * next_row(v) + south * prev_row(v))
        return center * v - sides

    return shifted


def products(r, cu, cv, dg, rows):
    shifted = operator(cu, cv, dg)
    p1 = shifted(r)
    p2 = shifted(p1)
    eu, ev = p2 - next_col(p2), p2 - next_row(p2)
    energy = dg * p2 * p2 + (cu * eu * eu + cv * ev * ev)
    q, p, o = r[:rows], p1[:rows], p2[:rows]
    return p1, p2, (q * q, q * p, p * p, p * o, o * o, energy[:rows])


def fold(prod, lanes):
    tiles = [prod[8 * i : 8 * i + 8, lanes] for i in range(prod.shape[0] // 8)]
    while len(tiles) > 1:
        tiles = [sum(tiles[i : i + 2][1:], tiles[i]) for i in range(0, len(tiles), 2)]
    return tiles[0]


def lane_pack(end, g, c, code, diag, u=None):
    lane = iota(code.shape, 1)
    edge = 127 if end else 0
    out = jnp.where(lane == 16, turn(code, 16 - edge, 1), 0.0)
    for by in (1, 2, 4):
        out = out + turn(out, by, 1)
    places = [(g[k], edge, k, 1) for k in range(LEV)] + [(c[k], edge, 8 + k, 1) for k in range(LEV)]
    places += [(code, 125, 24, 2), (diag, 126, 29, 2)] if end else [(code, 1, 24, 2), (diag, 0, 26, 2)]
    if u is not None:
        places.append((u, 127, 31, 1))
    for x, at, to, width in places:
        out = jnp.where((lane >= to) & (lane < to + width), turn(x, to - at, 1), out)
    return out


def codes_of(land, bottom, row_in, code_ref, row_ref):
    row_ref[...] = row_in[...]
    code_ref[...] = code_of(land[...], bottom[...])


def row_halo(near, far, lanes):
    even = is_even("row")

    def plane(p):
        at = slice(8 * (p // 2), 8 * (p // 2) + 8)
        north, south = pick(even, near[at, lanes], far[at, lanes])
        upper = iota(north.shape, 0) < DEEP
        if p % 2 == 0:
            return jnp.where(upper, north, turn(south, DEEP, 0))
        return jnp.where(upper, turn(north, DEEP, 0), south)

    return plane


def with_rows(r, sent_a, sent_b, near, far, lanes):
    rows = r.shape[0]
    even = is_even("row")
    high, low = pick(even, sent_a[:, lanes], sent_b[:, lanes])
    north, south = pick(even, near[:, lanes], far[:, lanes])
    sub = iota((8, r.shape[1]), 0)

    def across(below, above):
        open_v = jnp.minimum(below[23:24], above[20:21]) > sub.astype(F32) + 0.5
        total = jnp.where(open_v, above[:8] - below[:8], 0.0) * (above[8:16] + below[8:16])
        for by in (4, 2, 1):
            total = total + turn(total, by, 0)
        return 0.0625 * total

    up, down = across(high, north), across(south, low)
    halo = row_halo(near, far, lanes)(RHS) + jnp.where(sub == 0, -up, jnp.where(sub == 7, down, 0.0))
    first = r[:8] - jnp.where(sub == 0, down, 0.0)
    last = r[rows - 8 :] + jnp.where(sub == 7, up, 0.0)
    return jnp.concatenate([first, r[8 : rows - 8], last, halo], axis=0)


def join_cols(of_near, high, low, r, sent_a, sent_b, near, far, *refs):
    rows, width = r.shape
    out = refs[-1]
    north, south = pick(is_even("row"), near[24:, :], far[24:, :])
    sub = iota((8, 128), 0)
    halos, sides = [], []
    for lanes in (slice(width - 128, width), slice(0, 128)):
        halos.append(jnp.where(sub < 3, turn(north[:, lanes], -5, 0), jnp.where(sub < 5, 0.0, south[:, lanes])))
        sides.append(with_rows(r[:, lanes], sent_a, sent_b, near, far, lanes))
    which = 0 if of_near else 1
    even = is_even("col")
    last = even if of_near else jnp.logical_not(even)
    own = pick(even, high[...], low[...])[which]
    full = jnp.concatenate([own, pick(even, *halos)[which]], axis=0)
    rhs = turn(pick(even, *sides)[which], 29, 1)
    lane = iota(full.shape, 1)
    start = jnp.where(last, 26, 29)
    full = jnp.where((lane >= start) & (lane < start + 3), rhs, full)
    tall = rows // 4
    block = iota((tall, 128), 1) // 32
    folded = full[:tall]
    for b in range(1, 4):
        folded = jnp.where(block == b, turn(full[b * tall : (b + 1) * tall], 32 * b, 1), folded)
    out[:tall, :] = folded
    out[tall:, :] = full[rows:]


def unfold(x, by):
    tall = x.shape[0] - 8
    blocks = [turn(x[:tall], by - 32 * b, 1) for b in range(4)]
    return jnp.concatenate(blocks + [turn(x[tall:], by, 1)], axis=0)


def local_rhs(g, c, code_in, surf, diag, u, r_ref, first_ref, last_ref):
    rows, cols = surf.shape
    code = code_in[...]
    cu = jnp.where(iota(code.shape, 1) < cols - 1, jnp.minimum(code, next_col(code)), 0.0)
    cv = jnp.where(iota(code.shape, 0) < rows - 1, jnp.minimum(code, next_row(code)), 0.0)
    ub, vb = faces(g, c, cu, next_col), faces(g, c, cv, next_row)
    r_ref[...] = surf[...] + 0.0625 * ((ub - prev_col(ub)) + (vb - prev_row(vb)))
    for end, (tile, ref) in enumerate(((slice(0, 128), first_ref), (slice(cols - 128, cols), last_ref))):
        gs, cs = [g[k, :, tile] for k in range(LEV)], [c[k, :, tile] for k in range(LEV)]
        ref[...] = lane_pack(end, gs, cs, code[:, tile], diag[:, tile], u[:, tile] if end else None)


def inner(r_in, code_in, diag, sent_a, sent_b, near, far, r_ref, p1_ref, p2_ref, mom_ref, rs_ref, codes_ref, diags_ref, r_own, sem):
    rows, cols = diag.shape
    halo = row_halo(near, far, slice(0, cols))
    r = with_rows(r_in[...], sent_a, sent_b, near, far, slice(0, cols))
    r_own[...] = r[:rows]
    copy = pltpu.make_async_copy(r_own, r_ref, sem)
    copy.start()
    code = jnp.concatenate([code_in[...], halo(CODE)], axis=0)
    dg = jnp.concatenate([diag[...], halo(DIAG)], axis=0)
    left = iota((rows + 8, 128), 1) < 64
    for x, ref in ((r, rs_ref), (code, codes_ref), (dg, diags_ref)):
        ref[...] = jnp.where(left, turn(x[:, cols - 128 :], -68, 1), turn(x[:, :128], 68, 1))
    code = 0.125 * code
    cu = jnp.where(iota(code.shape, 1) < cols - 1, jnp.minimum(code, next_col(code)), 0.0)
    cv = jnp.minimum(code, next_row(code))
    p1, p2, prods = products(r, cu, cv, dg, rows)
    p1_ref[...] = p1[:rows]
    p2_ref[...] = p2[:rows]
    lane = iota((8, 128), 1)
    for m, prod in enumerate(prods):
        parts = [fold(prod, slice(128 * j, 128 * j + 128)) for j in range(cols // 128)]
        parts[0] = jnp.where(lane >= NEAR, parts[0], 0.0)
        parts[-1] = jnp.where(lane < 128 - NEAR, parts[-1], 0.0)
        mom_ref[8 * m : 8 * m + 8, :] = sum(parts[1:], parts[0])
    copy.wait()


def col_halo(near, far):
    east, west = pick(is_even("col"), near[...], far[...])

    def plane(at):
        tile = unfold(east, -at)
        return jnp.where(iota(tile.shape, 1) < 64, tile, unfold(west, 127 - at))

    return plane


def outer(rs, codes, diags, mom_in, sent_a, sent_b, near, far, r_ref, p1_ref, p2_ref, mom_ref):
    rows = rs.shape[0] - 8
    even = is_even("col")
    high, low = pick(even, sent_a[...], sent_b[...])
    east, west = pick(even, near[...], far[...])
    at = iota(high.shape, 1) % 32

    def between(first, end, x):
        return jnp.where((at >= first) & (at < end), x, 0.0)

    def across(below, above, to):
        open_u = turn(jnp.minimum(below, above), -16, 1) > at.astype(F32) + 0.5
        total = between(0, 8, jnp.where(open_u, above - below, 0.0) * turn(above + below, -8, 1))
        moved = [turn(total, to + 1 - k, 1) for k in range(LEV + 1)]
        pairs = [moved[k] + moved[k + 1] for k in range(1, LEV - 1, 2)]
        shared = (pairs[0] + pairs[1]) + (pairs[2] + moved[LEV - 1])
        one, two = shared + moved[LEV], shared + moved[0]
        first = to % 32
        return 0.0625 * (between(first, first + 1, one) - between(first + 1, first + 2, two))

    def placed(x, e, w, by):
        came = unfold(e + w, by)
        lane = iota(came.shape, 1)
        return jnp.where((lane < 60) | (lane >= 68), x, came), came

    _, added = placed(
        0.0, across(high, east, 28) + between(29, 32, east), across(west, low, 36) + turn(between(26, 29, west), 8, 1), 31
    )
    lane = iota(added.shape, 1)
    r = jnp.where((lane < 60) | (lane >= 68), rs[...], 0.0) + jnp.where((lane >= 59) & (lane < 69), added, 0.0)
    nearest = jnp.where(at == 26, turn(west, 3, 1), west)
    code, _ = placed(codes[...], between(23, 26, east), turn(between(24, 27, nearest), 4, 1), 37)
    code = 0.125 * code
    dg, _ = placed(diags[...], between(26, 28, east), turn(between(29, 31, west), 3, 1), 34)
    cu, cv = jnp.minimum(code, next_col(code)), jnp.minimum(code, next_row(code))
    p1, p2, prods = products(r, cu, cv, dg, rows)
    r_ref[...] = r
    p1_ref[...] = p1
    p2_ref[...] = p2
    lane = iota((8, 128), 1)
    mine = ((lane >= 60 - NEAR) & (lane < 60)) | ((lane >= 68) & (lane < 68 + NEAR))
    sub = iota((8, 128), 0)
    sums = jnp.zeros((8, 128), F32)
    for m, prod in enumerate(prods):
        part = mom_in[8 * m : 8 * m + 8, :] + jnp.where(mine, fold(prod, slice(0, 128)), 0.0)
        for by in (4, 2, 1):
            part = part + turn(part, by, 0)
        sums = jnp.where(sub == m, part, sums)
    sums = ((sums + turn(sums, 16, 1)) + (turn(sums, 32, 1) + turn(sums, 48, 1))) + (
        (turn(sums, 64, 1) + turn(sums, 80, 1)) + (turn(sums, 96, 1) + turn(sums, 112, 1))
    )
    sums = (sums + turn(sums, 4, 1)) + (turn(sums, 8, 1) + turn(sums, 12, 1))
    packed = jnp.zeros((8, 128), F32)
    for m in range(len(prods)):
        packed = jnp.where(lane // 4 == m, jnp.broadcast_to(sums[m : m + 1, :], (8, 128)), packed)
    for i in range(mom_ref.shape[0] // 8):
        mom_ref[8 * i : 8 * i + 8, :] = packed[:, : mom_ref.shape[1]]


def tracer_kernel(g_in, land_in, bottom_in, u_in, v_in, rn, rf, cn, cf, out_ref, g, land, bottom, u, v, out, sems, g_sems, out_sems):
    flat = [
        pltpu.make_async_copy(src, dst, sems.at[n])
        for n, (src, dst) in enumerate(((land_in, land), (bottom_in, bottom), (u_in, u), (v_in, v)))
    ]
    deep = [pltpu.make_async_copy(g_in.at[k], g.at[k], g_sems.at[k]) for k in range(LEV)]
    done = [pltpu.make_async_copy(out.at[k], out_ref.at[k], out_sems.at[k]) for k in range(LEV)]
    start_all(flat + deep)
    wait_all(flat)
    rows, cols = u.shape
    ch = col_halo(cn, cf)
    sub = iota((8, cols), 0)
    north, south = pick(is_even("row"), rn[...], rf[...])

    def wide(own, lane, above, below):
        at = [8 * (x // 8) for x in (above, below)]
        halo = jnp.where(
            sub == 0,
            turn(north[at[0] : at[0] + 8], -(above % 8), 0),
            turn(south[at[1] : at[1] + 8], 7 - below % 8, 0),
        )
        return jnp.concatenate([jnp.concatenate([own, halo], axis=0), ch(lane)], axis=1)

    code = wide(code_of(land[...], bottom[...]), 23, 20, 23)
    cu, cv = jnp.minimum(code, next_col(code)), jnp.minimum(code, next_row(code))
    uw = 0.125 * wide(u[...], 31, 28, 28)
    vw = 0.125 * wide(v[...], 31, 28, 28)
    for k in range(LEV):
        deep[k].wait()
        gk = wide(g[k], k, k, k)
        pu = jnp.where(cu > k + 0.5, next_col(gk) - gk, 0.0) * uw
        pv = jnp.where(cv > k + 0.5, next_row(gk) - gk, 0.0) * vw
        total = gk + pu + prev_col(pu) + pv + prev_row(pv)
        out[k] = total[:rows, :cols]
        done[k].start()
    wait_all(done)


def two_sum(a, b):
    s = a + b
    t = s - a
    return s, (a - (s - t)) + (b - t)


def quick(a, b):
    s = a + b
    return s, b - (s - a)


def split(a):
    t = a * 4097.0
    high = t - (t - a)
    return high, a - high


def add(x, y):
    s, e = two_sum(x[0], y[0])
    return quick(s, e + (x[1] + y[1]))


def neg(x):
    return -x[0], -x[1]


def mul(x, y):
    p = x[0] * y[0]
    (ah, al), (bh, bl) = split(x[0]), split(y[0])
    e = ((ah * bh - p) + ah * bl + al * bh) + al * bl
    return quick(p, e + (x[0] * y[1] + x[1] * y[0]))


def div(x, y):
    q = x[0] / y[0]
    rest = add(x, neg(mul((q, jnp.zeros_like(q)), y)))
    return quick(q, rest[0] / y[0])


def combine(mom, r, p1, p2, rs, p1s, p2s, x_ref, x, sems):
    zero = jnp.zeros((8, mom.shape[1]), F32)
    tiles = [(mom[8 * i : 8 * i + 8, :], zero) for i in range(mom.shape[0] // 8)]
    while len(tiles) > 1:
        tiles = [add(tiles[i], tiles[i + 1]) for i in range(0, len(tiles), 2)]
    total = tiles[0]
    for by in (4, 2, 1):
        total = add(total, tuple(pltpu.roll(a, by, 0) for a in total))
    sums = []
    for m in range(6):
        four = [
            tuple(jnp.broadcast_to(a[:, at : at + 1], (8, 128)) for a in total)
            for at in range(4 * m, 4 * m + 4)
        ]
        sums.append(add(add(four[0], four[1]), add(four[2], four[3])))
    m00, m01, m11, m12, m22, e22 = sums
    a00, a01, a02 = add(m01, m00), add(m11, m01), add(m12, m11)
    a11, a12, a22 = a02, add(m22, m12), e22
    l10 = div(a01, a00)
    l20 = div(a02, a00)
    w11 = add(a11, neg(mul(l10, a01)))
    w12 = add(a12, neg(mul(l10, a02)))
    ok1 = w11[0] > 1e-9 * a11[0]
    l21 = tuple(jnp.where(ok1, a, 0.0) for a in div(w12, w11))
    w22 = add(add(a22, neg(mul(l20, a02))), neg(mul(l21, w12)))
    ok2 = w22[0] > 1e-9 * a22[0]
    b0 = m00
    b1 = add(m01, neg(mul(l10, b0)))
    z1 = tuple(jnp.where(ok1, a, 0.0) for a in div(b1, w11))
    b2 = add(add(m11, neg(mul(l20, b0))), neg(mul(l21, b1)))
    z2 = tuple(jnp.where(ok2, a, 0.0) for a in div(b2, w22))
    y2 = z2
    y1 = add(z1, neg(mul(l21, y2)))
    y0 = add(div(b0, a00), neg(add(mul(l10, y1), mul(l20, y2))))
    rows, cols = r.shape
    bands = sems.shape[0]
    tall = rows // bands
    done = []
    for b in range(bands):
        band = slice(b * tall, (b + 1) * tall)
        for i in range(b * tall // 8, (b + 1) * tall // 8):
            at = slice(8 * i, 8 * i + 8)
            lane = iota((8, 128), 1)
            side = y0[0] * rs[at, :] + (y1[0] * p1s[at, :] + y2[0] * p2s[at, :])
            for j in range(cols // 128):
                to = (at, slice(128 * j, 128 * j + 128))
                tile = y0[0] * r[to] + (y1[0] * p1[to] + y2[0] * p2[to])
                if j == 0:
                    tile = jnp.where(lane < NEAR, turn(side, -68, 1), tile)
                if j == cols // 128 - 1:
                    tile = jnp.where(lane >= 128 - NEAR, turn(side, 68, 1), tile)
                x[to] = tile
        done.append(pltpu.make_async_copy(x.at[band, :], x_ref.at[band, :], sems.at[b]))
        done[-1].start()
    wait_all(done)


def call(kernel, ins, outs, scratch=(), name=None, cost=None):
    run = pl.pallas_call(
        kernel,
        in_specs=list(ins),
        out_specs=[spec for spec, _ in outs],
        out_shape=[spec.memory_space(shape, F32) for spec, shape in outs],
        scratch_shapes=list(scratch),
        compiler_params=PARAMS,
        cost_estimate=cost,
        name=name,
    )
    return lambda *args: run(*[pltpu.with_memory_space_constraint(x, spec.memory_space) for x, spec in zip(args, ins)])


def shards(tracer_adj_next, tracer, u_east, v_north, surf_adj_next, diag, land, bottom):
    levels, rows, cols = tracer.shape
    size = lax.axis_size("row") * lax.axis_size("col")
    g, c = tracer_adj_next, tracer
    dma = pltpu.SemaphoreType.DMA
    two, side = (rows, cols), (rows + 8, 128)
    whole = lambda kind=F32: pltpu.VMEM(two, kind)
    edges = [pltpu.VMEM((levels, 8, cols), F32)] * 4 + [pltpu.VMEM((8, cols), jnp.int32)] * 4 + [pltpu.VMEM((8, cols), F32)] * 6
    row_a, row_b = call(
        pack_rows, [HBM] * 7, [(VMEM, (32, cols))] * 2, edges + [dma((14,))], name="pack_rows"
    )(g, c, land, bottom, surf_adj_next, diag, v_north)
    row_far = lax.ppermute(row_b, "row", swap_pairs("row", 1))
    deep = pltpu.VMEM(g.shape, F32)
    code, row_a = call(
        codes_of,
        [VMEM] * 3,
        [(VMEM, two), (VMEM, (32, cols))],
        name="codes_of",
        cost=pl.CostEstimate(flops=g.size, bytes_accessed=g.size, transcendentals=0),
    )(land, bottom, row_a)
    row_near = lax.ppermute(row_a, "row", swap_pairs("row", 0))
    row_sent, row_got = (row_a, row_b), (row_near, row_far)
    rhs, low, high = call(
        local_rhs,
        [VMEM] * 6,
        [(VMEM, two)] + [(VMEM, (rows, 128))] * 2,
        name="local_rhs",
        cost=pl.CostEstimate(flops=24 * g.size, bytes_accessed=8 * g.size, transcendentals=0),
    )(g, c, code, surf_adj_next, diag, u_east)
    sent = (rows // 4 + 8, 128)
    (b,) = call(functools.partial(join_cols, False), [VMEM] * 7, [(VMEM, sent)], name="join_far")(
        high, low, rhs, *row_sent, *row_got
    )
    far = lax.ppermute(b, "col", swap_pairs("col", 1))
    r, p1, p2, mom, rs, codes, diags = call(
        inner,
        [VMEM] * 7,
        [(HBM, two)] + [(VMEM, two)] * 2 + [(VMEM, (48, 128))] + [(VMEM, side)] * 3,
        [whole(), dma],
        name="inner",
        cost=pl.CostEstimate(flops=24 * g.size, bytes_accessed=8 * g.size, transcendentals=0),
    )(rhs, code, diag, *row_sent, *row_got)
    (a,) = call(functools.partial(join_cols, True), [VMEM] * 8, [(VMEM, sent)], name="join_near")(
        high, low, rhs, *row_sent, *row_got, rs
    )
    near = lax.ppermute(a, "col", swap_pairs("col", 0))
    col_sent, col_got = (a, b), (near, far)
    *sides, mom = call(outer, [VMEM] * 8, [(VMEM, side)] * 3 + [(VMEM, (size, 32))], name="outer")(
        rs, codes, diags, mom, *col_sent, *col_got
    )
    mom = lax.all_to_all(mom, ("row", "col"), 0, 0, tiled=True)
    (tracer_adj,) = call(
        tracer_kernel,
        [HBM] * 5 + [VMEM] * 4,
        [(HBM, g.shape)],
        [deep, whole(jnp.int32), whole(jnp.int32), whole(), whole(), deep, dma((4,)), dma((levels,)), dma((levels,))],
        name="tracer",
        cost=pl.CostEstimate(flops=20 * g.size, bytes_accessed=12 * g.size, transcendentals=0),
    )(g, land, bottom, u_east, v_north, *row_got, *col_got)
    (surf_adj,) = call(
        combine,
        [VMEM] * 7,
        [(HBM, two)],
        [whole(), dma((2,))],
        name="combine",
    )(mom, r, p1, p2, *sides)
    return tracer_adj, surf_adj


def solution(mesh):
    three, two = P(None, "row", "col"), P("row", "col")
    return jax.shard_map(
        shards,
        mesh=mesh,
        in_specs=(three, three, two, two, two, two, two, two),
        out_specs=(three, two),
        check_vma=False,
    )
```
